32 devices in a mesh: gx: 4 (over x, core), gz: 8 (over z, y).
Axes of the slice: x: 2, y: 2, z: 4, core: 2. Of those that a mesh axis runs over, the one named last changes fastest.
Arguments:
- source_field: float32 [8, 512, 4096], P('gz', None, 'gx'), may hold values from -8 to 8
- coupling: float32 [8], replicated, may hold values from 0.5 to 2
- spacing: float32 [8], replicated, may hold values from 0.5 to 2
Outputs:
- pressure: float32 [8, 512, 4096], P('gz', None, 'gx')
The draws below stay inside these ranges and needn't reach their ends.
All inputs are finite; a program needn't handle non-finite values.
Results may differ from the reference program's by a relative error of at most 0.0003.
Values sent between devices are 32-bit elements; how exact they have to be, the bound alone decides.
A program may use at most 128 MiB of HBM per device.

```python
import math
import jax
import jax.numpy as jnp
from jax import lax

NX = 4096
NY = 512
NZ = 8


def steps_of(rng, extent, cuts, least, high):
    loudness, own = 1.0, jax.random.fold_in(rng, 6)
    for dim, blocks in cuts:
        steps = jnp.exp(jax.random.uniform(jax.random.fold_in(own, dim), (blocks,), jnp.float32, least / len(cuts), high / len(cuts)))
        loudness = loudness * jnp.repeat(steps, extent[dim] // blocks).reshape([-1 if axis == dim else 1 for axis in range(len(extent))])
    return loudness


def bell_draw(stream_key, extent, deviation, reach, shards=(), held_as=jnp.bfloat16):
    factor_of = steps_of(stream_key, extent, shards, -0.22, 0.18) if shards else 1.0
    entries = jax.random.normal(stream_key, extent, jnp.float32) * deviation * factor_of
    return jnp.minimum(jnp.maximum(entries, -reach), reach).astype(held_as)


def setup_inputs(seed: int = 0) -> dict:
    key_list = jax.random.split(jax.random.key(seed), 4)
    return {
        "source_field": bell_draw(key_list[0], (NZ, NY, NX), 1.0, 8.0, ((0, 8), (2, 4)), jnp.float32),
        "coupling": jnp.clip(jnp.exp(jax.random.uniform(key_list[1], (NZ,), jnp.float32, math.log(0.5), math.log(2.0))), 0.5, 2.0),
        "spacing": jnp.clip(jnp.exp(jax.random.uniform(key_list[2], (NZ,), jnp.float32, math.log(0.5), math.log(2.0))), 0.5, 2.0),
    }


TWO_PI = 2.0 * math.pi


def thomas(eigenvalue, coupling, spacing, source_real, source_imag):
    coupling_above = jnp.concatenate([coupling[1:], jnp.zeros((1,), coupling.dtype)])

    def sweep_down(carry, layer):
        ratio_prev, reduced_real, reduced_imag = carry
        coupling_low, coupling_high, height, value_real, value_imag = layer
        pivot_now = eigenvalue * height + coupling_low + coupling_high - coupling_low * ratio_prev
        ratio_now = coupling_high / pivot_now
        reduced_real = (height * value_real + coupling_low * reduced_real) / pivot_now
        reduced_imag = (height * value_imag + coupling_low * reduced_imag) / pivot_now
        return (ratio_now, reduced_real, reduced_imag), (ratio_now, reduced_real, reduced_imag)

    all_zeros = jnp.zeros_like(eigenvalue)
    unused, (ratios, reduced_real, reduced_imag) = lax.scan(
        sweep_down, (all_zeros, all_zeros, all_zeros),
        (coupling, coupling_above, spacing, source_real, source_imag))

    def sweep_up(carry, layer):
        above_real, above_imag = carry
        ratio_now, value_real, value_imag = layer
        above_real = ratio_now * above_real + value_real
        above_imag = ratio_now * above_imag + value_imag
        return (above_real, above_imag), (above_real, above_imag)

    unused_top, (solved_real, solved_imag) = lax.scan(
        sweep_up, (all_zeros, all_zeros), (ratios, reduced_real, reduced_imag), reverse=True)
    return solved_real, solved_imag


def reference(source_field, coupling, spacing):
    spectrum = jnp.fft.rfftn(source_field, axes=(1, 2))
    span_wave = jnp.arange(NY).astype(jnp.float32)
    stream_wave = jnp.arange(NX // 2 + 1).astype(jnp.float32)
    eigen_span = 2.0 - 2.0 * jnp.cos(span_wave * (TWO_PI / NY))
    eigen_stream = 2.0 - 2.0 * jnp.cos(stream_wave * (TWO_PI / NX))
    eigenvalue = eigen_span[:, None] + eigen_stream[None, :]
    solved_real, solved_imag = thomas(eigenvalue, coupling, spacing, jnp.real(spectrum), jnp.imag(spectrum))
    pressure = jnp.fft.irfftn(lax.complex(solved_real, solved_imag), s=(NY, NX), axes=(1, 2))
    return pressure.astype(jnp.float32)
```

```python
import functools
import math

import jax
import jax.numpy as jnp
import ml_dtypes
import numpy as np
from jax import lax
from jax.experimental import pallas as pl
from jax.experimental.pallas import tpu as pltpu
from jax.sharding import PartitionSpec as P

LANES = 128
MESH = pl.DeviceIdType.MESH


def cos_sin(product, period):
    angles = (product % period).astype(np.float64) * (2.0 * math.pi / period)
    return np.cos(angles), np.sin(angles)


def split_table(table):
    high = table.astype(np.float32).astype(ml_dtypes.bfloat16)
    low = (table - high.astype(np.float64)).astype(np.float32).astype(ml_dtypes.bfloat16)
    return high, low


def make_tables(span, stream, rows):
    outer = stream // LANES
    slots = outer // 2
    ks = np.arange(span)
    cosine, sine = cos_sin(ks[:, None] * ks[None, :], span)
    span_high, span_low = split_table(cosine + sine)
    lane = np.arange(LANES)
    cosine, sine = cos_sin(lane[:, None] * lane[None, :], LANES)
    regular = np.block([[cosine, -sine], [sine, cosine]])
    half_cos, half_sin = cos_sin(lane[:, None] * (slots + outer * lane[None, :]), stream)
    zeros = np.zeros((LANES, LANES))
    special = np.block([[cosine + sine, zeros], [zeros, half_cos + half_sin]])
    forward = np.stack([special, regular])
    inverse = np.stack([special.T, regular.T]) / (span * stream)
    forward_high, forward_low = split_table(forward)
    inverse_high, inverse_low = split_table(inverse)
    turn_cos, turn_sin = cos_sin(np.arange(slots)[:, None] * lane[None, :], stream)
    wave = np.arange(slots)[:, None] + outer * np.concatenate([lane, lane])[None, :]
    wave[0, LANES:] += slots
    eigen_stream = 2.0 - 2.0 * cos_sin(wave, stream)[0]
    eigen_stream = np.ascontiguousarray(np.broadcast_to(eigen_stream[:, None, :], (slots, rows, 2 * LANES)))
    eigen_span = 2.0 - 2.0 * cos_sin(ks, span)[0]
    eigen_span = np.broadcast_to(eigen_span[:, None], (span, 2 * LANES)).reshape(span // rows, rows, 2 * LANES)
    return (
        span_high, span_low, forward_high, forward_low, inverse_high, inverse_low,
        turn_cos.astype(np.float32), turn_sin.astype(np.float32),
        eigen_stream.astype(np.float32), np.ascontiguousarray(eigen_span).astype(np.float32),
    )


def real_transform(values):
    count = len(values)
    if count == 2:
        return [(values[0] + values[1], None), (values[0] - values[1], None)]
    even = real_transform(values[0::2])
    odd = real_transform(values[1::2])
    result = [None] * (count // 2 + 1)
    quarter = count // 4
    result[0] = (even[0][0] + odd[0][0], None)
    result[count // 2] = (even[0][0] - odd[0][0], None)
    result[quarter] = (even[quarter][0], -odd[quarter][0])
    for k in range(1, quarter):
        angle = 2.0 * math.pi * k / count
        cosine, sine = math.cos(angle), math.sin(angle)
        odd_real, odd_imag = odd[k]
        turned_real = odd_real * cosine + odd_imag * sine
        turned_imag = odd_imag * cosine - odd_real * sine
        even_real, even_imag = even[k]
        result[k] = (even_real + turned_real, even_imag + turned_imag)
        result[count // 2 - k] = (even_real - turned_real, turned_imag - even_imag)
    return result


def real_inverse(pairs):
    count = 2 * (len(pairs) - 1)
    if count == 2:
        return [pairs[0][0] + pairs[1][0], pairs[0][0] - pairs[1][0]]
    quarter = count // 4
    even, odd = [None] * (quarter + 1), [None] * (quarter + 1)
    even[0] = (pairs[0][0] + pairs[count // 2][0], None)
    odd[0] = (pairs[0][0] - pairs[count // 2][0], None)
    even[quarter] = (2.0 * pairs[quarter][0], None)
    odd[quarter] = (-2.0 * pairs[quarter][1], None)
    for k in range(1, quarter):
        angle = 2.0 * math.pi * k / count
        cosine, sine = math.cos(angle), math.sin(angle)
        low_real, low_imag = pairs[k]
        high_real, high_imag = pairs[count // 2 - k]
        even[k] = (low_real + high_real, low_imag - high_imag)
        diff_real, diff_imag = low_real - high_real, low_imag + high_imag
        odd[k] = (diff_real * cosine - diff_imag * sine, diff_imag * cosine + diff_real * sine)
    even_values, odd_values = real_inverse(even), real_inverse(odd)
    return [(even_values if n % 2 == 0 else odd_values)[n // 2] for n in range(count)]


def split_value(value):
    high = value.astype(jnp.bfloat16)
    return high, (value - high.astype(jnp.float32)).astype(jnp.bfloat16)


def dot3(left, right):
    dot = functools.partial(jnp.dot, preferred_element_type=jnp.float32)
    return dot(left[0], right[0]) + (dot(left[0], right[1]) + dot(left[1], right[0]))


def kernel(
    cfg, coupling, spacing, field, span_high, span_low, fwd_high, fwd_low, inv_high, inv_low,
    turn_cos, turn_sin, eig_stream, eig_span, out,
    field_high, field_low, send_box, columns, staging, spectrum, pivots_low, pivots_high, middle,
    reduced, edge_down, from_below, from_above, solved, returned,
    go_send, go_recv, up_send, up_recv, down_send, down_recv, back_send, back_recv,
):
    gx_count, group, planes, chunks, rows, levels = cfg
    peers = gx_count * group
    blocks = field.shape[2] // LANES
    outer = blocks * gx_count
    slots = outer // 2
    level_count = levels * planes
    gx = lax.axis_index("gx")
    gz = lax.axis_index("gz")
    plane = gz // group
    row = gz % group
    me = gx * group + row
    first = plane * levels

    def partner(step):
        step_gx, step_row = step // group, step % group
        to_gx, to_row = (gx + step_gx) % gx_count, (row + step_row) % group
        from_gx, from_row = (gx + gx_count - step_gx) % gx_count, (row + group - step_row) % group
        return (to_gx, to_row), (from_gx, from_row)

    barrier = pltpu.get_barrier_semaphore()
    for step in range(1, peers):
        (to_gx, to_row), _ = partner(step)
        pl.semaphore_signal(barrier, inc=1, device_id=(to_gx, plane * group + to_row), device_id_type=MESH)

    @pl.when(plane > 0)
    def _():
        pl.semaphore_signal(barrier, inc=1, device_id=(gx, gz - group), device_id_type=MESH)

    @pl.when(plane < planes - 1)
    def _():
        pl.semaphore_signal(barrier, inc=1, device_id=(gx, gz + group), device_id_type=MESH)

    def go_copy(chunk, step):
        (to_gx, to_row), _ = partner(step)
        return pltpu.make_async_remote_copy(
            src_ref=send_box.at[chunk, to_gx * group + to_row],
            dst_ref=columns.at[chunk, row, pl.ds(gx * blocks, blocks)],
            send_sem=go_send.at[chunk, step], recv_sem=go_recv.at[chunk, step],
            device_id=(to_gx, plane * group + to_row), device_id_type=MESH)

    def go_arrival(chunk, step):
        _, (from_gx, from_row) = partner(step)
        return pltpu.make_async_remote_copy(
            src_ref=send_box.at[chunk, 0],
            dst_ref=columns.at[chunk, from_row, pl.ds(from_gx * blocks, blocks)],
            send_sem=go_send.at[chunk, step], recv_sem=go_recv.at[chunk, step],
            device_id=(from_gx, plane * group + from_row), device_id_type=MESH)

    def back_copy(chunk, step):
        (to_gx, to_row), _ = partner(step)
        return pltpu.make_async_remote_copy(
            src_ref=solved.at[chunk, to_row, pl.ds(to_gx * blocks, blocks)],
            dst_ref=returned.at[chunk, me],
            send_sem=back_send.at[chunk, step], recv_sem=back_recv.at[chunk, step],
            device_id=(to_gx, plane * group + to_row), device_id_type=MESH)

    def back_arrival(chunk, step):
        _, (from_gx, from_row) = partner(step)
        return pltpu.make_async_remote_copy(
            src_ref=solved.at[chunk, 0, pl.ds(0, blocks)],
            dst_ref=returned.at[chunk, from_gx * group + from_row],
            send_sem=back_send.at[chunk, step], recv_sem=back_recv.at[chunk, step],
            device_id=(from_gx, plane * group + from_row), device_id_type=MESH)

    def up_copy(chunk):
        return pltpu.make_async_remote_copy(
            src_ref=reduced.at[chunk, levels - 1], dst_ref=from_below.at[chunk],
            send_sem=up_send.at[chunk], recv_sem=up_recv.at[chunk],
            device_id=(gx, (gz + group) % (planes * group)), device_id_type=MESH)

    def down_copy(chunk):
        return pltpu.make_async_remote_copy(
            src_ref=edge_down.at[chunk], dst_ref=from_above.at[chunk],
            send_sem=down_send.at[chunk], recv_sem=down_recv.at[chunk],
            device_id=(gx, (gz + planes * group - group) % (planes * group)), device_id_type=MESH)

    def below(level):
        return coupling[level]

    def above(level):
        return jnp.where(level + 1 < level_count, coupling[jnp.minimum(level + 1, level_count - 1)], 0.0)

    field_high[...], field_low[...] = split_value(field[0])

    def span_step(chunk, carry):
        take = pl.ds(pl.multiple_of(chunk * (peers * rows), peers * rows), peers * rows)
        left = (span_high[take, :], span_low[take, :])
        width = min(2, blocks)
        for block in range(0, blocks, width):
            cols = slice(block * LANES, (block + width) * LANES)
            modes = dot3(left, (field_high[:, cols], field_low[:, cols]))
            for part in range(width):
                piece = modes[:, part * LANES:(part + 1) * LANES]
                send_box[chunk, :, block + part] = piece.reshape(peers, rows, LANES)

        @pl.when(chunk == 0)
        def _():
            expected = peers - 1 + jnp.where(plane > 0, 1, 0) + jnp.where(plane < planes - 1, 1, 0)
            pl.semaphore_wait(barrier, expected)

        for step in range(1, peers):
            go_copy(chunk, step).start()
        columns[chunk, row, pl.ds(gx * blocks, blocks)] = send_box[chunk, me]
        return carry

    lax.fori_loop(0, chunks, span_step, 0)

    part_slots = min(4, slots)
    parts = slots // part_slots

    def coefficients(chunk):
        def part_step(part, carry):
            take = pl.ds(part * part_slots, part_slots)
            lam = eig_span[chunk * peers + me][None] + eig_stream[take]

            def from_ground(level, ratio):
                pivot = lam * spacing[level] + below(level) + above(level) - below(level) * ratio
                return above(level) / pivot

            ratio = lax.fori_loop(0, first, from_ground, jnp.zeros_like(lam))
            for own in range(levels):
                level = first + own
                pivot = lam * spacing[level] + below(level) + above(level) - below(level) * ratio
                factor = 1.0 / pivot
                pivots_low[chunk, own, take] = factor
                ratio = above(level) * factor

            def from_top(count, ratio_top):
                level = level_count - 1 - count
                pivot = lam * spacing[level] + below(level) + above(level) - above(level) * ratio_top
                return below(level) / pivot

            ratio_top = lax.fori_loop(0, level_count - first - levels, from_top, jnp.zeros_like(lam))
            middle[chunk, take] = 1.0 / (1.0 - ratio * ratio_top)
            for own in reversed(range(levels)):
                level = first + own
                pivot = lam * spacing[level] + below(level) + above(level) - above(level) * ratio_top
                factor = 1.0 / pivot
                pivots_high[chunk, own, take] = factor
                ratio_top = below(level) * factor
            return carry

        lax.fori_loop(0, parts, part_step, 0)

    tiles = rows // 8

    def stream_forward(chunk):
        def tile_step(index, carry):
            own, tile = index // tiles, index % tiles
            inner = pl.ds(pl.multiple_of(tile * 8, 8), 8)
            place = pl.ds(pl.multiple_of(own * rows + tile * 8, 8), 8)
            pairs = real_transform([columns[chunk, own, n, inner, :] for n in range(outer)])
            staging[0, place, :LANES] = pairs[0][0]
            staging[0, place, LANES:] = pairs[slots][0]
            for k in range(1, slots):
                real, imag = pairs[k]
                cosine, sine = turn_cos[k:k + 1, :], turn_sin[k:k + 1, :]
                staging[k, place, :LANES] = real * cosine + imag * sine
                staging[k, place, LANES:] = imag * cosine - real * sine
            return carry

        lax.fori_loop(0, levels * tiles, tile_step, 0)
        special = dot3(split_value(staging[0]), (fwd_high[0], fwd_low[0]))
        spectrum[chunk, 0] = special.reshape(levels, rows, 2 * LANES)
        rest = staging[1:].reshape((slots - 1) * levels * rows, 2 * LANES)
        regular = dot3(split_value(rest), (fwd_high[1], fwd_low[1]))
        spectrum[chunk, 1:] = regular.reshape(slots - 1, levels, rows, 2 * LANES)

    def sweep_up(chunk):
        @pl.when(plane > 0)
        def _():
            up_copy(chunk).wait_recv()

        @pl.when(plane == 0)
        def _():
            from_below[chunk] = jnp.zeros(from_below.shape[1:], jnp.float32)

        def part_step(part, carry):
            take = pl.ds(part * part_slots, part_slots)
            value = from_below[chunk, take]
            for own in range(levels):
                level = first + own
                value = (spacing[level] * spectrum[chunk, take, own] + below(level) * value) * pivots_low[chunk, own, take]
                reduced[chunk, own, take] = value
            return carry

        lax.fori_loop(0, parts, part_step, 0)

        @pl.when(plane < planes - 1)
        def _():
            up_copy(chunk).start()

    def sweep_down(chunk):
        @pl.when(plane < planes - 1)
        def _():
            down_copy(chunk).wait_recv()

        @pl.when(plane == planes - 1)
        def _():
            from_above[chunk] = jnp.zeros(from_above.shape[1:], jnp.float32)

        @pl.when(plane > 0)
        def _():
            def part_step(part, carry):
                take = pl.ds(part * part_slots, part_slots)
                value = from_above[chunk, take]
                for own in reversed(range(levels)):
                    level = first + own
                    value = (spacing[level] * spectrum[chunk, take, own] + above(level) * value) * pivots_high[chunk, own, take]
                edge_down[chunk, take] = value
                return carry

            lax.fori_loop(0, parts, part_step, 0)
            down_copy(chunk).start()

    def finish(chunk):
        def part_step(part, carry):
            take = pl.ds(part * part_slots, part_slots)
            value = from_above[chunk, take]
            for own in reversed(range(levels)):
                value = reduced[chunk, own, take] + above(first + own) * pivots_low[chunk, own, take] * value
                if own == levels - 1:
                    value = value * middle[chunk, take]
                staging[take, own * rows:(own + 1) * rows, :] = value
            return carry

        lax.fori_loop(0, parts, part_step, 0)
        special = dot3(split_value(staging[0]), (inv_high[0], inv_low[0]))
        rest = staging[1:].reshape((slots - 1) * levels * rows, 2 * LANES)
        regular = dot3(split_value(rest), (inv_high[1], inv_low[1]))
        staging[0] = special
        staging[1:] = regular.reshape(slots - 1, levels * rows, 2 * LANES)

        def tile_step(index, carry):
            own, tile = index // tiles, index % tiles
            inner = pl.ds(pl.multiple_of(tile * 8, 8), 8)
            place = pl.ds(pl.multiple_of(own * rows + tile * 8, 8), 8)
            pairs = [(staging[0, place, :LANES], None)]
            for k in range(1, slots):
                real, imag = staging[k, place, :LANES], staging[k, place, LANES:]
                cosine, sine = turn_cos[k:k + 1, :], turn_sin[k:k + 1, :]
                pairs.append((real * cosine - imag * sine, real * sine + imag * cosine))
            pairs.append((staging[0, place, LANES:], None))
            for n, value in enumerate(real_inverse(pairs)):
                solved[chunk, own, n, inner, :] = value
            return carry

        lax.fori_loop(0, levels * tiles, tile_step, 0)
        for step in range(1, peers):
            back_copy(chunk, step).start()
        returned[chunk, me] = solved[chunk, row, pl.ds(gx * blocks, blocks)]

    lag_down = planes - 1 - plane
    lag = jnp.maximum(plane, lag_down)

    def step(now, carry):
        @pl.when(now < chunks)
        def _():
            coefficients(now)
            for peer in range(1, peers):
                go_arrival(now, peer).wait_recv()
            stream_forward(now)

        @pl.when(jnp.logical_and(now >= plane, now < plane + chunks))
        def _():
            sweep_up(now - plane)

        @pl.when(jnp.logical_and(now >= lag_down, now < lag_down + chunks))
        def _():
            sweep_down(now - lag_down)

        @pl.when(jnp.logical_and(now >= lag, now < lag + chunks))
        def _():
            finish(now - lag)

        return carry

    lax.fori_loop(0, chunks + planes - 1, step, 0)

    def arrive(chunk, carry):
        for peer in range(1, peers):
            back_arrival(chunk, peer).wait_recv()
        return carry

    lax.fori_loop(0, chunks, arrive, 0)
    span = field.shape[1]
    width = min(2, blocks)
    for block in range(0, blocks, width):
        pieces = [returned[:, :, block + part].reshape(span, LANES) for part in range(width)]
        right = split_value(jnp.concatenate(pieces, axis=1) if width > 1 else pieces[0])
        out[0, :, block * LANES:(block + width) * LANES] = dot3((span_high[...], span_low[...]), right)

    def drain(chunk, carry):
        for peer in range(1, peers):
            go_copy(chunk, peer).wait_send()
            back_copy(chunk, peer).wait_send()

        @pl.when(plane < planes - 1)
        def _():
            up_copy(chunk).wait_send()

        @pl.when(plane > 0)
        def _():
            down_copy(chunk).wait_send()

        return carry

    lax.fori_loop(0, chunks, drain, 0)


def local(mesh_shape, source_field, coupling, spacing):
    gx_count, gz_count = mesh_shape["gx"], mesh_shape["gz"]
    own, span, part = source_field.shape
    assert own == 1
    group = gz_count // 4 if gz_count % 4 == 0 else 1
    planes = gz_count // group
    levels = group
    peers = gx_count * group
    stream = part * gx_count
    share = span // peers
    chunks = 4
    while share % (8 * chunks):
        chunks //= 2
    rows = share // chunks
    blocks = part // LANES
    outer = stream // LANES
    slots = outer // 2
    tables = make_tables(span, stream, rows)
    f32 = jnp.float32
    wide = (slots, rows, 2 * LANES)
    dma = pltpu.SemaphoreType.DMA
    vmem = pl.BlockSpec(memory_space=pltpu.VMEM)
    smem = pl.BlockSpec(memory_space=pltpu.SMEM)
    cfg = (gx_count, group, planes, chunks, rows, levels)
    return pl.pallas_call(
        functools.partial(kernel, cfg),
        out_shape=jax.ShapeDtypeStruct(source_field.shape, f32),
        in_specs=[smem, smem] + [vmem] * 11,
        out_specs=vmem,
        scratch_shapes=[
            pltpu.VMEM((span, part), jnp.bfloat16),
            pltpu.VMEM((span, part), jnp.bfloat16),
            pltpu.VMEM((chunks, peers, blocks, rows, LANES), f32),
            pltpu.VMEM((chunks, levels, outer, rows, LANES), f32),
            pltpu.VMEM((slots, levels * rows, 2 * LANES), f32),
            pltpu.VMEM((chunks, slots, levels, rows, 2 * LANES), f32),
            pltpu.VMEM((chunks, levels) + wide, f32),
            pltpu.VMEM((chunks, levels) + wide, f32),
            pltpu.VMEM((chunks,) + wide, f32),
            pltpu.VMEM((chunks, levels) + wide, f32),
            pltpu.VMEM((chunks,) + wide, f32),
            pltpu.VMEM((chunks,) + wide, f32),
            pltpu.VMEM((chunks,) + wide, f32),
            pltpu.VMEM((chunks, levels, outer, rows, LANES), f32),
            pltpu.VMEM((chunks, peers, blocks, rows, LANES), f32),
            dma((chunks, peers)), dma((chunks, peers)),
            dma((chunks,)), dma((chunks,)), dma((chunks,)), dma((chunks,)),
            dma((chunks, peers)), dma((chunks, peers)),
        ],
        compiler_params=pltpu.CompilerParams(
            collective_id=0, has_side_effects=True, vmem_limit_bytes=56 * 1024 * 1024),
        cost_estimate=pl.CostEstimate(flops=8 * 10**9, bytes_accessed=8 * 2**20, transcendentals=0),
    )(coupling, spacing, source_field, *(jnp.asarray(table) for table in tables))


def solution(mesh):
    in_specs = (P("gz", None, "gx"), P(), P())
    out_specs = P("gz", None, "gx")
    return jax.shard_map(
        functools.partial(local, dict(mesh.shape)), mesh=mesh,
        in_specs=in_specs, out_specs=out_specs, check_vma=False)
```

```python
import functools
import math

import jax
import jax.numpy as jnp
import ml_dtypes
import numpy as np
from jax import lax
from jax.experimental import pallas as pl
from jax.experimental.pallas import tpu as pltpu
from jax.sharding import PartitionSpec as P

LANES = 128
MESH = pl.DeviceIdType.MESH


def cos_sin(product, period):
    angles = (product % period).astype(np.float64) * (2.0 * math.pi / period)
    return np.cos(angles), np.sin(angles)


def split_table(table):
    high = table.astype(np.float32).astype(ml_dtypes.bfloat16)
    low = (table - high.astype(np.float64)).astype(np.float32).astype(ml_dtypes.bfloat16)
    return high, low


def make_tables(span, stream, rows):
    outer = stream // LANES
    slots = outer // 2
    ks = np.arange(span)
    cosine, sine = cos_sin(ks[:, None] * ks[None, :], span)
    span_high, span_low = split_table(cosine + sine)
    lane = np.arange(LANES)
    cosine, sine = cos_sin(lane[:, None] * lane[None, :], LANES)
    regular = np.block([[cosine, -sine], [sine, cosine]])
    half_cos, half_sin = cos_sin(lane[:, None] * (slots + outer * lane[None, :]), stream)
    zeros = np.zeros((LANES, LANES))
    special = np.block([[cosine + sine, zeros], [zeros, half_cos + half_sin]])
    forward = np.stack([special, regular])
    inverse = np.stack([special.T, regular.T]) / (span * stream)
    forward_high, forward_low = split_table(forward)
    inverse_high, inverse_low = split_table(inverse)
    turn_cos, turn_sin = cos_sin(np.arange(slots)[:, None] * lane[None, :], stream)
    wave = np.arange(slots)[:, None] + outer * np.concatenate([lane, lane])[None, :]
    wave[0, LANES:] += slots
    eigen_stream = 2.0 - 2.0 * cos_sin(wave, stream)[0]
    eigen_stream = np.ascontiguousarray(np.broadcast_to(eigen_stream[:, None, :], (slots, rows, 2 * LANES)))
    eigen_span = 2.0 - 2.0 * cos_sin(ks, span)[0]
    eigen_span = np.broadcast_to(eigen_span[:, None], (span, 2 * LANES)).reshape(span // rows, rows, 2 * LANES)
    return (
        span_high, span_low, forward_high, forward_low, inverse_high, inverse_low,
        turn_cos.astype(np.float32), turn_sin.astype(np.float32),
        eigen_stream.astype(np.float32), np.ascontiguousarray(eigen_span).astype(np.float32),
    )


def real_transform(values):
    count = len(values)
    if count == 2:
        return [(values[0] + values[1], None), (values[0] - values[1], None)]
    even = real_transform(values[0::2])
    odd = real_transform(values[1::2])
    result = [None] * (count // 2 + 1)
    quarter = count // 4
    result[0] = (even[0][0] + odd[0][0], None)
    result[count // 2] = (even[0][0] - odd[0][0], None)
    result[quarter] = (even[quarter][0], -odd[quarter][0])
    for k in range(1, quarter):
        angle = 2.0 * math.pi * k / count
        cosine, sine = math.cos(angle), math.sin(angle)
        odd_real, odd_imag = odd[k]
        turned_real = odd_real * cosine + odd_imag * sine
        turned_imag = odd_imag * cosine - odd_real * sine
        even_real, even_imag = even[k]
        result[k] = (even_real + turned_real, even_imag + turned_imag)
        result[count // 2 - k] = (even_real - turned_real, turned_imag - even_imag)
    return result


def real_inverse(pairs):
    count = 2 * (len(pairs) - 1)
    if count == 2:
        return [pairs[0][0] + pairs[1][0], pairs[0][0] - pairs[1][0]]
    quarter = count // 4
    even, odd = [None] * (quarter + 1), [None] * (quarter + 1)
    even[0] = (pairs[0][0] + pairs[count // 2][0], None)
    odd[0] = (pairs[0][0] - pairs[count // 2][0], None)
    even[quarter] = (2.0 * pairs[quarter][0], None)
    odd[quarter] = (-2.0 * pairs[quarter][1], None)
    for k in range(1, quarter):
        angle = 2.0 * math.pi * k / count
        cosine, sine = math.cos(angle), math.sin(angle)
        low_real, low_imag = pairs[k]
        high_real, high_imag = pairs[count // 2 - k]
        even[k] = (low_real + high_real, low_imag - high_imag)
        diff_real, diff_imag = low_real - high_real, low_imag + high_imag
        odd[k] = (diff_real * cosine - diff_imag * sine, diff_imag * cosine + diff_real * sine)
    even_values, odd_values = real_inverse(even), real_inverse(odd)
    return [(even_values if n % 2 == 0 else odd_values)[n // 2] for n in range(count)]


def split_value(value):
    high = value.astype(jnp.bfloat16)
    return high, (value - high.astype(jnp.float32)).astype(jnp.bfloat16)


def dot3(left, right):
    dot = functools.partial(jnp.dot, preferred_element_type=jnp.float32)
    return dot(left[0], right[0]) + (dot(left[0], right[1]) + dot(left[1], right[0]))


def kernel(
    cfg, coupling, spacing, field, span_high, span_low, fwd_high, fwd_low, inv_high, inv_low,
    turn_cos, turn_sin, eig_stream, eig_span, out,
    field_high, field_low, send_box, columns, staging, spectrum, pivots_low, pivots_high, middle,
    reduced, edge_down, from_below, from_above, solved, returned,
    go_send, go_recv, up_send, up_recv, down_send, down_recv, back_send, back_recv,
):
    gx_count, group, planes, chunks, rows, levels, batch = cfg
    peers = gx_count * group
    blocks = field.shape[2] // LANES
    outer = blocks * gx_count
    slots = outer // 2
    level_count = levels * planes
    gx = lax.axis_index("gx")
    gz = lax.axis_index("gz")
    plane = gz // group
    row = gz % group
    me = gx * group + row
    first = plane * levels

    def partner(step):
        step_gx, step_row = step // group, step % group
        to_gx, to_row = (gx + step_gx) % gx_count, (row + step_row) % group
        from_gx, from_row = (gx + gx_count - step_gx) % gx_count, (row + group - step_row) % group
        return (to_gx, to_row), (from_gx, from_row)

    barrier = pltpu.get_barrier_semaphore()
    for step in range(1, peers):
        (to_gx, to_row), _ = partner(step)
        pl.semaphore_signal(barrier, inc=1, device_id=(to_gx, plane * group + to_row), device_id_type=MESH)

    @pl.when(plane > 0)
    def _():
        pl.semaphore_signal(barrier, inc=1, device_id=(gx, gz - group), device_id_type=MESH)

    @pl.when(plane < planes - 1)
    def _():
        pl.semaphore_signal(barrier, inc=1, device_id=(gx, gz + group), device_id_type=MESH)

    def go_copy(chunk, step):
        (to_gx, to_row), _ = partner(step)
        return pltpu.make_async_remote_copy(
            src_ref=send_box.at[chunk, to_gx * group + to_row],
            dst_ref=columns.at[chunk, row, pl.ds(gx * blocks, blocks)],
            send_sem=go_send.at[chunk, step], recv_sem=go_recv.at[chunk, step],
            device_id=(to_gx, plane * group + to_row), device_id_type=MESH)

    def go_arrival(chunk, step):
        _, (from_gx, from_row) = partner(step)
        return pltpu.make_async_remote_copy(
            src_ref=send_box.at[chunk, 0],
            dst_ref=columns.at[chunk, from_row, pl.ds(from_gx * blocks, blocks)],
            send_sem=go_send.at[chunk, step], recv_sem=go_recv.at[chunk, step],
            device_id=(from_gx, plane * group + from_row), device_id_type=MESH)

    def back_copy(chunk, step):
        (to_gx, to_row), _ = partner(step)
        return pltpu.make_async_remote_copy(
            src_ref=solved.at[chunk, to_row, pl.ds(to_gx * blocks, blocks)],
            dst_ref=returned.at[chunk, me],
            send_sem=back_send.at[chunk, step], recv_sem=back_recv.at[chunk, step],
            device_id=(to_gx, plane * group + to_row), device_id_type=MESH)

    def back_arrival(chunk, step):
        _, (from_gx, from_row) = partner(step)
        return pltpu.make_async_remote_copy(
            src_ref=solved.at[chunk, 0, pl.ds(0, blocks)],
            dst_ref=returned.at[chunk, from_gx * group + from_row],
            send_sem=back_send.at[chunk, step], recv_sem=back_recv.at[chunk, step],
            device_id=(from_gx, plane * group + from_row), device_id_type=MESH)

    def up_copy(chunk):
        return pltpu.make_async_remote_copy(
            src_ref=reduced.at[chunk, levels - 1], dst_ref=from_below.at[chunk],
            send_sem=up_send.at[chunk], recv_sem=up_recv.at[chunk],
            device_id=(gx, (gz + group) % (planes * group)), device_id_type=MESH)

    def down_copy(chunk):
        return pltpu.make_async_remote_copy(
            src_ref=edge_down.at[chunk], dst_ref=from_above.at[chunk],
            send_sem=down_send.at[chunk], recv_sem=down_recv.at[chunk],
            device_id=(gx, (gz + planes * group - group) % (planes * group)), device_id_type=MESH)

    def below(level):
        return coupling[level]

    def above(level):
        return jnp.where(level + 1 < level_count, coupling[jnp.minimum(level + 1, level_count - 1)], 0.0)

    field_high[...], field_low[...] = split_value(field[0])

    def span_step(turn, carry):
        height = batch * peers * rows
        take = pl.ds(pl.multiple_of(turn * height, height), height)
        left = (span_high[take, :], span_low[take, :])
        width = min(2, blocks)
        for block in range(0, blocks, width):
            cols = slice(block * LANES, (block + width) * LANES)
            modes = dot3(left, (field_high[:, cols], field_low[:, cols]))
            for part in range(width):
                piece = modes[:, part * LANES:(part + 1) * LANES]
                piece = piece.reshape(batch, peers, rows, LANES)
                send_box[pl.ds(turn * batch, batch), :, block + part] = piece

        @pl.when(turn == 0)
        def _():
            expected = peers - 1 + jnp.where(plane > 0, 1, 0) + jnp.where(plane < planes - 1, 1, 0)
            pl.semaphore_wait(barrier, expected)

        for index in range(batch):
            chunk = turn * batch + index
            for step in range(1, peers):
                go_copy(chunk, step).start()
            columns[chunk, row, pl.ds(gx * blocks, blocks)] = send_box[chunk, me]
        return carry

    lax.fori_loop(0, chunks // batch, span_step, 0)

    part_slots = min(max(1, 64 // rows), slots)
    parts = slots // part_slots

    def coefficients(chunk):
        def part_step(part, carry):
            take = pl.ds(part * part_slots, part_slots)
            lam = eig_span[chunk * peers + me][None] + eig_stream[take]

            def from_ground(level, ratio):
                pivot = lam * spacing[level] + below(level) + above(level) - below(level) * ratio
                return above(level) / pivot

            ratio = lax.fori_loop(0, first, from_ground, jnp.zeros_like(lam))
            for own in range(levels):
                level = first + own
                pivot = lam * spacing[level] + below(level) + above(level) - below(level) * ratio
                factor = 1.0 / pivot
                pivots_low[chunk, own, take] = factor
                ratio = above(level) * factor

            def from_top(count, ratio_top):
                level = level_count - 1 - count
                pivot = lam * spacing[level] + below(level) + above(level) - above(level) * ratio_top
                return below(level) / pivot

            ratio_top = lax.fori_loop(0, level_count - first - levels, from_top, jnp.zeros_like(lam))
            middle[chunk, take] = 1.0 / (1.0 - ratio * ratio_top)
            for own in reversed(range(levels)):
                level = first + own
                pivot = lam * spacing[level] + below(level) + above(level) - above(level) * ratio_top
                factor = 1.0 / pivot
                pivots_high[chunk, own, take] = factor
                ratio_top = below(level) * factor
            return carry

        lax.fori_loop(0, parts, part_step, 0)

    tiles = rows // 8

    def stream_forward(chunk):
        def tile_step(index, carry):
            own, tile = index // tiles, index % tiles
            inner = pl.ds(pl.multiple_of(tile * 8, 8), 8)
            place = pl.ds(pl.multiple_of(own * rows + tile * 8, 8), 8)
            pairs = real_transform([columns[chunk, own, n, inner, :] for n in range(outer)])
            staging[0, place, :LANES] = pairs[0][0]
            staging[0, place, LANES:] = pairs[slots][0]
            for k in range(1, slots):
                real, imag = pairs[k]
                cosine, sine = turn_cos[k:k + 1, :], turn_sin[k:k + 1, :]
                staging[k, place, :LANES] = real * cosine + imag * sine
                staging[k, place, LANES:] = imag * cosine - real * sine
            return carry

        lax.fori_loop(0, levels * tiles, tile_step, 0)
        special = dot3(split_value(staging[0]), (fwd_high[0], fwd_low[0]))
        spectrum[chunk, 0] = special.reshape(levels, rows, 2 * LANES)
        rest = staging[1:].reshape((slots - 1) * levels * rows, 2 * LANES)
        regular = dot3(split_value(rest), (fwd_high[1], fwd_low[1]))
        spectrum[chunk, 1:] = regular.reshape(slots - 1, levels, rows, 2 * LANES)

    def sweep_up(chunk):
        @pl.when(plane > 0)
        def _():
            up_copy(chunk).wait_recv()

        @pl.when(plane == 0)
        def _():
            from_below[chunk] = jnp.zeros(from_below.shape[1:], jnp.float32)

        def part_step(part, carry):
            take = pl.ds(part * part_slots, part_slots)
            value = from_below[chunk, take]
            for own in range(levels):
                level = first + own
                value = (spacing[level] * spectrum[chunk, take, own] + below(level) * value) * pivots_low[chunk, own, take]
                reduced[chunk, own, take] = value
            return carry

        lax.fori_loop(0, parts, part_step, 0)

        @pl.when(plane < planes - 1)
        def _():
            up_copy(chunk).start()

    def sweep_down(chunk):
        @pl.when(plane < planes - 1)
        def _():
            down_copy(chunk).wait_recv()

        @pl.when(plane == planes - 1)
        def _():
            from_above[chunk] = jnp.zeros(from_above.shape[1:], jnp.float32)

        @pl.when(plane > 0)
        def _():
            def part_step(part, carry):
                take = pl.ds(part * part_slots, part_slots)
                value = from_above[chunk, take]
                for own in reversed(range(levels)):
                    level = first + own
                    value = (spacing[level] * spectrum[chunk, take, own] + above(level) * value) * pivots_high[chunk, own, take]
                edge_down[chunk, take] = value
                return carry

            lax.fori_loop(0, parts, part_step, 0)
            down_copy(chunk).start()

    def finish(chunk):
        def part_step(part, carry):
            take = pl.ds(part * part_slots, part_slots)
            value = from_above[chunk, take]
            for own in reversed(range(levels)):
                value = reduced[chunk, own, take] + above(first + own) * pivots_low[chunk, own, take] * value
                if own == levels - 1:
                    value = value * middle[chunk, take]
                staging[take, own * rows:(own + 1) * rows, :] = value
            return carry

        lax.fori_loop(0, parts, part_step, 0)
        special = dot3(split_value(staging[0]), (inv_high[0], inv_low[0]))
        rest = staging[1:].reshape((slots - 1) * levels * rows, 2 * LANES)
        regular = dot3(split_value(rest), (inv_high[1], inv_low[1]))
        staging[0] = special
        staging[1:] = regular.reshape(slots - 1, levels * rows, 2 * LANES)

        def tile_step(index, carry):
            own, tile = index // tiles, index % tiles
            inner = pl.ds(pl.multiple_of(tile * 8, 8), 8)
            place = pl.ds(pl.multiple_of(own * rows + tile * 8, 8), 8)
            pairs = [(staging[0, place, :LANES], None)]
            for k in range(1, slots):
                real, imag = staging[k, place, :LANES], staging[k, place, LANES:]
                cosine, sine = turn_cos[k:k + 1, :], turn_sin[k:k + 1, :]
                pairs.append((real * cosine - imag * sine, real * sine + imag * cosine))
            pairs.append((staging[0, place, LANES:], None))
            for n, value in enumerate(real_inverse(pairs)):
                solved[chunk, own, n, inner, :] = value
            return carry

        lax.fori_loop(0, levels * tiles, tile_step, 0)
        for step in range(1, peers):
            back_copy(chunk, step).start()
        returned[chunk, me] = solved[chunk, row, pl.ds(gx * blocks, blocks)]

    lag_down = planes - 1 - plane
    lag = jnp.maximum(plane, lag_down)

    def step(now, carry):
        @pl.when(now < chunks)
        def _():
            coefficients(now)
            for peer in range(1, peers):
                go_arrival(now, peer).wait_recv()
            stream_forward(now)

        @pl.when(jnp.logical_and(now >= plane, now < plane + chunks))
        def _():
            sweep_up(now - plane)

        @pl.when(jnp.logical_and(now >= lag_down, now < lag_down + chunks))
        def _():
            sweep_down(now - lag_down)

        @pl.when(jnp.logical_and(now >= lag, now < lag + chunks))
        def _():
            finish(now - lag)

        return carry

    lax.fori_loop(0, chunks + planes - 1, step, 0)

    def arrive(chunk, carry):
        for peer in range(1, peers):
            back_arrival(chunk, peer).wait_recv()
        return carry

    span = field.shape[1]
    width = min(2, blocks)
    halves = 2 if chunks % 2 == 0 else 1
    depth = span // halves
    for half in range(halves):
        lax.fori_loop(half * (chunks // halves), (half + 1) * (chunks // halves), arrive, 0)
        near = slice(half * depth, (half + 1) * depth)
        here = slice(half * (chunks // halves), (half + 1) * (chunks // halves))
        left = (span_high[:, near], span_low[:, near])
        for block in range(0, blocks, width):
            pieces = [returned[here, :, block + part].reshape(depth, LANES) for part in range(width)]
            right = split_value(jnp.concatenate(pieces, axis=1) if width > 1 else pieces[0])
            value = dot3(left, right)
            cols = slice(block * LANES, (block + width) * LANES)
            out[0, :, cols] = value if half == 0 else out[0, :, cols] + value

    def drain(chunk, carry):
        for peer in range(1, peers):
            go_copy(chunk, peer).wait_send()
            back_copy(chunk, peer).wait_send()

        @pl.when(plane < planes - 1)
        def _():
            up_copy(chunk).wait_send()

        @pl.when(plane > 0)
        def _():
            down_copy(chunk).wait_send()

        return carry

    lax.fori_loop(0, chunks, drain, 0)


def local(mesh_shape, source_field, coupling, spacing):
    gx_count, gz_count = mesh_shape["gx"], mesh_shape["gz"]
    own, span, part = source_field.shape
    assert own == 1
    group = gz_count // 4 if gz_count % 4 == 0 else 1
    planes = gz_count // group
    levels = group
    peers = gx_count * group
    stream = part * gx_count
    share = span // peers
    chunks = 8
    while share % (8 * chunks):
        chunks //= 2
    rows = share // chunks
    batch = 2 if chunks % 2 == 0 and peers * rows < 128 else 1
    blocks = part // LANES
    outer = stream // LANES
    slots = outer // 2
    tables = make_tables(span, stream, rows)
    f32 = jnp.float32
    wide = (slots, rows, 2 * LANES)
    dma = pltpu.SemaphoreType.DMA
    vmem = pl.BlockSpec(memory_space=pltpu.VMEM)
    smem = pl.BlockSpec(memory_space=pltpu.SMEM)
    cfg = (gx_count, group, planes, chunks, rows, levels, batch)
    return pl.pallas_call(
        functools.partial(kernel, cfg),
        out_shape=jax.ShapeDtypeStruct(source_field.shape, f32),
        in_specs=[smem, smem] + [vmem] * 11,
        out_specs=vmem,
        scratch_shapes=[
            pltpu.VMEM((span, part), jnp.bfloat16),
            pltpu.VMEM((span, part), jnp.bfloat16),
            pltpu.VMEM((chunks, peers, blocks, rows, LANES), f32),
            pltpu.VMEM((chunks, levels, outer, rows, LANES), f32),
            pltpu.VMEM((slots, levels * rows, 2 * LANES), f32),
            pltpu.VMEM((chunks, slots, levels, rows, 2 * LANES), f32),
            pltpu.VMEM((chunks, levels) + wide, f32),
            pltpu.VMEM((chunks, levels) + wide, f32),
            pltpu.VMEM((chunks,) + wide, f32),
            pltpu.VMEM((chunks, levels) + wide, f32),
            pltpu.VMEM((chunks,) + wide, f32),
            pltpu.VMEM((chunks,) + wide, f32),
            pltpu.VMEM((chunks,) + wide, f32),
            pltpu.VMEM((chunks, levels, outer, rows, LANES), f32),
            pltpu.VMEM((chunks, peers, blocks, rows, LANES), f32),
            dma((chunks, peers)), dma((chunks, peers)),
            dma((chunks,)), dma((chunks,)), dma((chunks,)), dma((chunks,)),
            dma((chunks, peers)), dma((chunks, peers)),
        ],
        compiler_params=pltpu.CompilerParams(
            collective_id=0, has_side_effects=True, vmem_limit_bytes=56 * 1024 * 1024),
        cost_estimate=pl.CostEstimate(flops=8 * 10**9, bytes_accessed=8 * 2**20, transcendentals=0),
    )(coupling, spacing, source_field, *(jnp.asarray(table) for table in tables))


def solution(mesh):
    in_specs = (P("gz", None, "gx"), P(), P())
    out_specs = P("gz", None, "gx")
    return jax.shard_map(
        functools.partial(local, dict(mesh.shape)), mesh=mesh,
        in_specs=in_specs, out_specs=out_specs, check_vma=False)
```

```python
import functools
import math

import jax
import jax.numpy as jnp
import ml_dtypes
import numpy as np
from jax import lax
from jax.experimental import pallas as pl
from jax.experimental.pallas import tpu as pltpu
from jax.sharding import PartitionSpec as P

LANES = 128
MESH = pl.DeviceIdType.MESH


def cos_sin(product, period):
    angles = (product % period).astype(np.float64) * (2.0 * math.pi / period)
    return np.cos(angles), np.sin(angles)


def split_table(table):
    high = table.astype(np.float32).astype(ml_dtypes.bfloat16)
    low = (table - high.astype(np.float64)).astype(np.float32).astype(ml_dtypes.bfloat16)
    return high, low


def make_tables(span, stream, rows):
    outer = stream // LANES
    slots = outer // 2
    ks = np.arange(span)
    cosine, sine = cos_sin(ks[:, None] * ks[None, :], span)
    span_high, span_low = split_table(cosine + sine)
    lane = np.arange(LANES)
    cosine, sine = cos_sin(lane[:, None] * lane[None, :], LANES)
    regular = np.block([[cosine, -sine], [sine, cosine]])
    half_cos, half_sin = cos_sin(lane[:, None] * (slots + outer * lane[None, :]), stream)
    zeros = np.zeros((LANES, LANES))
    special = np.block([[cosine + sine, zeros], [zeros, half_cos + half_sin]])
    forward = np.stack([special, regular])
    inverse = np.stack([special.T, regular.T]) / (span * stream)
    forward_high, forward_low = split_table(forward)
    inverse_high, inverse_low = split_table(inverse)
    turn_cos, turn_sin = cos_sin(np.arange(slots)[:, None] * lane[None, :], stream)
    wave = np.arange(slots)[:, None] + outer * np.concatenate([lane, lane])[None, :]
    wave[0, LANES:] += slots
    eigen_stream = 2.0 - 2.0 * cos_sin(wave, stream)[0]
    eigen_stream = np.ascontiguousarray(np.broadcast_to(eigen_stream[:, None, :], (slots, rows, 2 * LANES)))
    eigen_span = 2.0 - 2.0 * cos_sin(ks, span)[0]
    eigen_span = np.broadcast_to(eigen_span[:, None], (span, 2 * LANES)).reshape(span // rows, rows, 2 * LANES)
    return (
        span_high, span_low, forward_high, forward_low, inverse_high, inverse_low,
        turn_cos.astype(np.float32), turn_sin.astype(np.float32),
        eigen_stream.astype(np.float32), np.ascontiguousarray(eigen_span).astype(np.float32),
    )


def real_transform(values):
    count = len(values)
    if count == 2:
        return [(values[0] + values[1], None), (values[0] - values[1], None)]
    even = real_transform(values[0::2])
    odd = real_transform(values[1::2])
    result = [None] * (count // 2 + 1)
    quarter = count // 4
    result[0] = (even[0][0] + odd[0][0], None)
    result[count // 2] = (even[0][0] - odd[0][0], None)
    result[quarter] = (even[quarter][0], -odd[quarter][0])
    for k in range(1, quarter):
        angle = 2.0 * math.pi * k / count
        cosine, sine = math.cos(angle), math.sin(angle)
        odd_real, odd_imag = odd[k]
        turned_real = odd_real * cosine + odd_imag * sine
        turned_imag = odd_imag * cosine - odd_real * sine
        even_real, even_imag = even[k]
        result[k] = (even_real + turned_real, even_imag + turned_imag)
        result[count // 2 - k] = (even_real - turned_real, turned_imag - even_imag)
    return result


def real_inverse(pairs):
    count = 2 * (len(pairs) - 1)
    if count == 2:
        return [pairs[0][0] + pairs[1][0], pairs[0][0] - pairs[1][0]]
    quarter = count // 4
    even, odd = [None] * (quarter + 1), [None] * (quarter + 1)
    even[0] = (pairs[0][0] + pairs[count // 2][0], None)
    odd[0] = (pairs[0][0] - pairs[count // 2][0], None)
    even[quarter] = (2.0 * pairs[quarter][0], None)
    odd[quarter] = (-2.0 * pairs[quarter][1], None)
    for k in range(1, quarter):
        angle = 2.0 * math.pi * k / count
        cosine, sine = math.cos(angle), math.sin(angle)
        low_real, low_imag = pairs[k]
        high_real, high_imag = pairs[count // 2 - k]
        even[k] = (low_real + high_real, low_imag - high_imag)
        diff_real, diff_imag = low_real - high_real, low_imag + high_imag
        odd[k] = (diff_real * cosine - diff_imag * sine, diff_imag * cosine + diff_real * sine)
    even_values, odd_values = real_inverse(even), real_inverse(odd)
    return [(even_values if n % 2 == 0 else odd_values)[n // 2] for n in range(count)]


def split_value(value):
    high = value.astype(jnp.bfloat16)
    return high, (value - high.astype(jnp.float32)).astype(jnp.bfloat16)


def dot3(left, right):
    wide = jnp.concatenate([left[0], left[1], left[0]], axis=1)
    tall = jnp.concatenate([right[0], right[0], right[1]], axis=0)
    return jnp.dot(wide, tall, preferred_element_type=jnp.float32)


def inverse_of(value):
    guess = pl.reciprocal(value, approx=True)
    guess = guess * (2.0 - value * guess)
    return guess * (2.0 - value * guess)


def kernel(
    cfg, coupling, spacing, field, span_high, span_low, fwd_high, fwd_low, inv_high, inv_low,
    turn_cos, turn_sin, eig_stream, eig_span, out,
    field_high, field_low, send_box, columns, staging, spectrum, pivots_low, pivots_high, middle,
    reduced, edge_down, from_below, from_above, solved, returned,
    go_send, go_recv, up_send, up_recv, down_send, down_recv, back_send, back_recv,
):
    gx_count, group, planes, chunks, rows, levels, batch = cfg
    peers = gx_count * group
    blocks = field.shape[2] // LANES
    outer = blocks * gx_count
    slots = outer // 2
    level_count = levels * planes
    gx = lax.axis_index("gx")
    gz = lax.axis_index("gz")
    plane = gz // group
    row = gz % group
    me = gx * group + row
    first = plane * levels

    def partner(step):
        return (gx + step // group) % gx_count, (row + step % group) % group

    barrier = pltpu.get_barrier_semaphore()
    for step in range(1, peers):
        to_gx, to_row = partner(step)
        pl.semaphore_signal(barrier, inc=1, device_id=(to_gx, plane * group + to_row), device_id_type=MESH)

    @pl.when(plane > 0)
    def _():
        pl.semaphore_signal(barrier, inc=1, device_id=(gx, gz - group), device_id_type=MESH)

    @pl.when(plane < planes - 1)
    def _():
        pl.semaphore_signal(barrier, inc=1, device_id=(gx, gz + group), device_id_type=MESH)

    def go_copy(chunk, step):
        to_gx, to_row = partner(step)
        return pltpu.make_async_remote_copy(
            src_ref=send_box.at[chunk, to_gx * group + to_row],
            dst_ref=columns.at[chunk, row, pl.ds(gx * blocks, blocks)],
            send_sem=go_send.at[chunk], recv_sem=go_recv.at[chunk],
            device_id=(to_gx, plane * group + to_row), device_id_type=MESH)

    def all_blocks(box, chunk, sem):
        blocks_here = box.at[chunk, pl.ds(0, peers - 1)]
        pltpu.make_async_copy(blocks_here, blocks_here, sem.at[chunk]).wait()

    def back_copy(chunk, step):
        to_gx, to_row = partner(step)
        return pltpu.make_async_remote_copy(
            src_ref=solved.at[chunk, to_row, pl.ds(to_gx * blocks, blocks)],
            dst_ref=returned.at[chunk, me],
            send_sem=back_send.at[chunk], recv_sem=back_recv.at[chunk],
            device_id=(to_gx, plane * group + to_row), device_id_type=MESH)

    def up_copy(chunk):
        return pltpu.make_async_remote_copy(
            src_ref=reduced.at[chunk, levels - 1], dst_ref=from_below.at[chunk],
            send_sem=up_send.at[chunk], recv_sem=up_recv.at[chunk],
            device_id=(gx, (gz + group) % (planes * group)), device_id_type=MESH)

    def down_copy(chunk):
        return pltpu.make_async_remote_copy(
            src_ref=edge_down.at[chunk], dst_ref=from_above.at[chunk],
            send_sem=down_send.at[chunk], recv_sem=down_recv.at[chunk],
            device_id=(gx, (gz + planes * group - group) % (planes * group)), device_id_type=MESH)

    def below(level):
        return coupling[level]

    def above(level):
        return jnp.where(level + 1 < level_count, coupling[jnp.minimum(level + 1, level_count - 1)], 0.0)

    field_high[...], field_low[...] = split_value(field[0])

    def span_step(turn, carry):
        height = batch * peers * rows
        take = pl.ds(pl.multiple_of(turn * height, height), height)
        left = (span_high[take, :], span_low[take, :])
        width = min(2, blocks)
        for block in range(0, blocks, width):
            cols = slice(block * LANES, (block + width) * LANES)
            modes = dot3(left, (field_high[:, cols], field_low[:, cols]))
            for part in range(width):
                piece = modes[:, part * LANES:(part + 1) * LANES]
                piece = piece.reshape(batch, peers, rows, LANES)
                send_box[pl.ds(turn * batch, batch), :, block + part] = piece

        @pl.when(turn == 0)
        def _():
            expected = peers - 1 + jnp.where(plane > 0, 1, 0) + jnp.where(plane < planes - 1, 1, 0)
            pl.semaphore_wait(barrier, expected)

        for index in range(batch):
            chunk = turn * batch + index
            for step in range(1, peers):
                go_copy(chunk, step).start()
            columns[chunk, row, pl.ds(gx * blocks, blocks)] = send_box[chunk, me]
        return carry

    lax.fori_loop(0, chunks // batch, span_step, 0)

    part_slots = min(max(1, 64 // rows), slots)
    parts = slots // part_slots

    def coefficients(chunk):
        def part_step(part, carry):
            take = pl.ds(part * part_slots, part_slots)
            lam = eig_span[chunk * peers + me][None] + eig_stream[take]

            def diagonal(level):
                return lam * spacing[level] + (below(level) + above(level))

            def from_ground(level, pair):
                now, before = pair
                return diagonal(level) * now - (below(level) * below(level)) * before, now

            def from_top(count, pair):
                level = level_count - 1 - count
                now, before = pair
                return diagonal(level) * now - (above(level) * above(level)) * before, now

            nought = lam * 0.0
            start = (nought + 1.0, nought)
            low = lax.fori_loop(0, first, from_ground, start)
            for own in range(levels):
                after = from_ground(first + own, low)
                pivots_low[chunk, own, take] = low[0] * inverse_of(after[0])
                low = after
            top = lax.fori_loop(0, level_count - first - levels, from_top, start)
            edge = above(first + levels - 1)
            both = low[0] * top[0]
            middle[chunk, take] = both * inverse_of(both - (edge * edge) * (low[1] * top[1]))
            for own in reversed(range(levels)):
                after = from_top(level_count - 1 - first - own, top)
                pivots_high[chunk, own, take] = top[0] * inverse_of(after[0])
                top = after
            return carry

        lax.fori_loop(0, parts, part_step, 0)

    tiles = rows // 8

    def stream_forward(chunk):
        def tile_step(index, carry):
            own, tile = index // tiles, index % tiles
            inner = pl.ds(pl.multiple_of(tile * 8, 8), 8)
            place = pl.ds(pl.multiple_of(own * rows + tile * 8, 8), 8)
            pairs = real_transform([columns[chunk, own, n, inner, :] for n in range(outer)])
            staging[0, place, :LANES] = pairs[0][0]
            staging[0, place, LANES:] = pairs[slots][0]
            for k in range(1, slots):
                real, imag = pairs[k]
                cosine, sine = turn_cos[k:k + 1, :], turn_sin[k:k + 1, :]
                staging[k, place, :LANES] = real * cosine + imag * sine
                staging[k, place, LANES:] = imag * cosine - real * sine
            return carry

        lax.fori_loop(0, levels * tiles, tile_step, 0)
        special = dot3(split_value(staging[0]), (fwd_high[0], fwd_low[0]))
        spectrum[chunk, 0] = special.reshape(levels, rows, 2 * LANES)
        rest = staging[1:].reshape((slots - 1) * levels * rows, 2 * LANES)
        regular = dot3(split_value(rest), (fwd_high[1], fwd_low[1]))
        spectrum[chunk, 1:] = regular.reshape(slots - 1, levels, rows, 2 * LANES)

    def sweep_up(chunk):
        @pl.when(plane > 0)
        def _():
            up_copy(chunk).wait_recv()

        @pl.when(plane == 0)
        def _():
            from_below[chunk] = jnp.zeros(from_below.shape[1:], jnp.float32)

        def part_step(part, carry):
            take = pl.ds(part * part_slots, part_slots)
            value = from_below[chunk, take]
            for own in range(levels):
                level = first + own
                value = (spacing[level] * spectrum[chunk, take, own] + below(level) * value) * pivots_low[chunk, own, take]
                reduced[chunk, own, take] = value
            return carry

        lax.fori_loop(0, parts, part_step, 0)

        @pl.when(plane < planes - 1)
        def _():
            up_copy(chunk).start()

    def sweep_down(chunk):
        @pl.when(plane < planes - 1)
        def _():
            down_copy(chunk).wait_recv()

        @pl.when(plane == planes - 1)
        def _():
            from_above[chunk] = jnp.zeros(from_above.shape[1:], jnp.float32)

        @pl.when(plane > 0)
        def _():
            def part_step(part, carry):
                take = pl.ds(part * part_slots, part_slots)
                value = from_above[chunk, take]
                for own in reversed(range(levels)):
                    level = first + own
                    value = (spacing[level] * spectrum[chunk, take, own] + above(level) * value) * pivots_high[chunk, own, take]
                edge_down[chunk, take] = value
                return carry

            lax.fori_loop(0, parts, part_step, 0)
            down_copy(chunk).start()

    def finish(chunk):
        def part_step(part, carry):
            take = pl.ds(part * part_slots, part_slots)
            value = from_above[chunk, take]
            for own in reversed(range(levels)):
                value = reduced[chunk, own, take] + above(first + own) * pivots_low[chunk, own, take] * value
                if own == levels - 1:
                    value = value * middle[chunk, take]
                staging[take, own * rows:(own + 1) * rows, :] = value
            return carry

        lax.fori_loop(0, parts, part_step, 0)
        special = dot3(split_value(staging[0]), (inv_high[0], inv_low[0]))
        rest = staging[1:].reshape((slots - 1) * levels * rows, 2 * LANES)
        regular = dot3(split_value(rest), (inv_high[1], inv_low[1]))
        staging[0] = special
        staging[1:] = regular.reshape(slots - 1, levels * rows, 2 * LANES)

        def tile_step(index, carry):
            own, tile = index // tiles, index % tiles
            inner = pl.ds(pl.multiple_of(tile * 8, 8), 8)
            place = pl.ds(pl.multiple_of(own * rows + tile * 8, 8), 8)
            pairs = [(staging[0, place, :LANES], None)]
            for k in range(1, slots):
                real, imag = staging[k, place, :LANES], staging[k, place, LANES:]
                cosine, sine = turn_cos[k:k + 1, :], turn_sin[k:k + 1, :]
                pairs.append((real * cosine - imag * sine, real * sine + imag * cosine))
            pairs.append((staging[0, place, LANES:], None))
            for n, value in enumerate(real_inverse(pairs)):
                solved[chunk, own, n, inner, :] = value
            return carry

        lax.fori_loop(0, levels * tiles, tile_step, 0)
        for step in range(1, peers):
            back_copy(chunk, step).start()
        returned[chunk, me] = solved[chunk, row, pl.ds(gx * blocks, blocks)]

    lag_down = planes - 1 - plane
    lag = jnp.maximum(plane, lag_down)

    def step(now, carry):
        @pl.when(now < chunks)
        def _():
            coefficients(now)
            all_blocks(send_box, now, go_recv)
            stream_forward(now)

        @pl.when(jnp.logical_and(now >= plane, now < plane + chunks))
        def _():
            sweep_up(now - plane)

        @pl.when(jnp.logical_and(now >= lag_down, now < lag_down + chunks))
        def _():
            sweep_down(now - lag_down)

        @pl.when(jnp.logical_and(now >= lag, now < lag + chunks))
        def _():
            finish(now - lag)

        return carry

    lax.fori_loop(0, chunks + planes - 1, step, 0)

    def arrive(chunk, carry):
        all_blocks(returned, chunk, back_recv)
        return carry

    span = field.shape[1]
    width = min(2, blocks)
    halves = 2 if chunks % 2 == 0 else 1
    depth = span // halves
    for half in range(halves):
        lax.fori_loop(half * (chunks // halves), (half + 1) * (chunks // halves), arrive, 0)
        near = slice(half * depth, (half + 1) * depth)
        here = slice(half * (chunks // halves), (half + 1) * (chunks // halves))
        left = (span_high[:, near], span_low[:, near])
        for block in range(0, blocks, width):
            pieces = [returned[here, :, block + part].reshape(depth, LANES) for part in range(width)]
            right = split_value(jnp.concatenate(pieces, axis=1) if width > 1 else pieces[0])
            value = dot3(left, right)
            cols = slice(block * LANES, (block + width) * LANES)
            out[0, :, cols] = value if half == 0 else out[0, :, cols] + value

    def drain(chunk, carry):
        all_blocks(send_box, chunk, go_send)
        all_blocks(returned, chunk, back_send)

        @pl.when(plane < planes - 1)
        def _():
            up_copy(chunk).wait_send()

        @pl.when(plane > 0)
        def _():
            down_copy(chunk).wait_send()

        return carry

    lax.fori_loop(0, chunks, drain, 0)


def local(mesh_shape, source_field, coupling, spacing):
    gx_count, gz_count = mesh_shape["gx"], mesh_shape["gz"]
    own, span, part = source_field.shape
    assert own == 1
    group = gz_count // 4 if gz_count % 4 == 0 else 1
    planes = gz_count // group
    levels = group
    peers = gx_count * group
    stream = part * gx_count
    share = span // peers
    chunks = 8
    while share % (8 * chunks):
        chunks //= 2
    rows = share // chunks
    batch = 2 if chunks % 2 == 0 and peers * rows < 128 else 1
    blocks = part // LANES
    outer = stream // LANES
    slots = outer // 2
    tables = make_tables(span, stream, rows)
    f32 = jnp.float32
    wide = (slots, rows, 2 * LANES)
    dma = pltpu.SemaphoreType.DMA
    vmem = pl.BlockSpec(memory_space=pltpu.VMEM)
    smem = pl.BlockSpec(memory_space=pltpu.SMEM)
    cfg = (gx_count, group, planes, chunks, rows, levels, batch)
    return pl.pallas_call(
        functools.partial(kernel, cfg),
        out_shape=jax.ShapeDtypeStruct(source_field.shape, f32),
        in_specs=[smem, smem] + [vmem] * 11,
        out_specs=vmem,
        scratch_shapes=[
            pltpu.VMEM((span, part), jnp.bfloat16),
            pltpu.VMEM((span, part), jnp.bfloat16),
            pltpu.VMEM((chunks, peers, blocks, rows, LANES), f32),
            pltpu.VMEM((chunks, levels, outer, rows, LANES), f32),
            pltpu.VMEM((slots, levels * rows, 2 * LANES), f32),
            pltpu.VMEM((chunks, slots, levels, rows, 2 * LANES), f32),
            pltpu.VMEM((chunks, levels) + wide, f32),
            pltpu.VMEM((chunks, levels) + wide, f32),
            pltpu.VMEM((chunks,) + wide, f32),
            pltpu.VMEM((chunks, levels) + wide, f32),
            pltpu.VMEM((chunks,) + wide, f32),
            pltpu.VMEM((chunks,) + wide, f32),
            pltpu.VMEM((chunks,) + wide, f32),
            pltpu.VMEM((chunks, levels, outer, rows, LANES), f32),
            pltpu.VMEM((chunks, peers, blocks, rows, LANES), f32),
            dma((chunks,)), dma((chunks,)),
            dma((chunks,)), dma((chunks,)), dma((chunks,)), dma((chunks,)),
            dma((chunks,)), dma((chunks,)),
        ],
        compiler_params=pltpu.CompilerParams(
            collective_id=0, has_side_effects=True, vmem_limit_bytes=56 * 1024 * 1024),
        cost_estimate=pl.CostEstimate(flops=8 * 10**9, bytes_accessed=8 * 2**20, transcendentals=0),
    )(coupling, spacing, source_field, *(jnp.asarray(table) for table in tables))


def solution(mesh):
    in_specs = (P("gz", None, "gx"), P(), P())
    out_specs = P("gz", None, "gx")
    return jax.shard_map(
        functools.partial(local, dict(mesh.shape)), mesh=mesh,
        in_specs=in_specs, out_specs=out_specs, check_vma=False)
```

```python
import functools
import math

import jax
import jax.numpy as jnp
import ml_dtypes
import numpy as np
from jax import lax
from jax.experimental import pallas as pl
from jax.experimental.pallas import tpu as pltpu
from jax.sharding import PartitionSpec as P

LANES = 128
MESH = pl.DeviceIdType.MESH


def cos_sin(product, period):
    angles = (product % period).astype(np.float64) * (2.0 * math.pi / period)
    return np.cos(angles), np.sin(angles)


def split_table(table):
    high = table.astype(np.float32).astype(ml_dtypes.bfloat16)
    low = (table - high.astype(np.float64)).astype(np.float32).astype(ml_dtypes.bfloat16)
    return high, low


def make_tables(span, stream, rows):
    outer = stream // LANES
    slots = outer // 2
    ks = np.arange(span)
    cosine, sine = cos_sin(ks[:, None] * ks[None, :], span)
    span_high, span_low = split_table(cosine + sine)
    lane = np.arange(LANES)
    cosine, sine = cos_sin(lane[:, None] * lane[None, :], LANES)
    regular = np.block([[cosine, -sine], [sine, cosine]])
    half_cos, half_sin = cos_sin(lane[:, None] * (slots + outer * lane[None, :]), stream)
    zeros = np.zeros((LANES, LANES))
    special = np.block([[cosine + sine, zeros], [zeros, half_cos + half_sin]])
    forward = np.stack([special, regular])
    inverse = np.stack([special.T, regular.T]) / (span * stream)
    forward_high, forward_low = split_table(forward)
    inverse_high, inverse_low = split_table(inverse)
    turn_cos, turn_sin = cos_sin(np.arange(slots)[:, None] * lane[None, :], stream)
    wave = np.arange(slots)[:, None] + outer * np.concatenate([lane, lane])[None, :]
    wave[0, LANES:] += slots
    eigen_stream = 2.0 - 2.0 * cos_sin(wave, stream)[0]
    eigen_stream = np.ascontiguousarray(np.broadcast_to(eigen_stream[:, None, :], (slots, rows, 2 * LANES)))
    eigen_span = 2.0 - 2.0 * cos_sin(ks, span)[0]
    eigen_span = np.broadcast_to(eigen_span[:, None], (span, 2 * LANES)).reshape(span // rows, rows, 2 * LANES)
    return (
        span_high, span_low, forward_high, forward_low, inverse_high, inverse_low,
        turn_cos.astype(np.float32), turn_sin.astype(np.float32),
        eigen_stream.astype(np.float32), np.ascontiguousarray(eigen_span).astype(np.float32),
    )


def real_transform(values):
    count = len(values)
    if count == 2:
        return [(values[0] + values[1], None), (values[0] - values[1], None)]
    even = real_transform(values[0::2])
    odd = real_transform(values[1::2])
    result = [None] * (count // 2 + 1)
    quarter = count // 4
    result[0] = (even[0][0] + odd[0][0], None)
    result[count // 2] = (even[0][0] - odd[0][0], None)
    result[quarter] = (even[quarter][0], -odd[quarter][0])
    for k in range(1, quarter):
        angle = 2.0 * math.pi * k / count
        cosine, sine = math.cos(angle), math.sin(angle)
        odd_real, odd_imag = odd[k]
        turned_real = odd_real * cosine + odd_imag * sine
        turned_imag = odd_imag * cosine - odd_real * sine
        even_real, even_imag = even[k]
        result[k] = (even_real + turned_real, even_imag + turned_imag)
        result[count // 2 - k] = (even_real - turned_real, turned_imag - even_imag)
    return result


def real_inverse(pairs):
    count = 2 * (len(pairs) - 1)
    if count == 2:
        return [pairs[0][0] + pairs[1][0], pairs[0][0] - pairs[1][0]]
    quarter = count // 4
    even, odd = [None] * (quarter + 1), [None] * (quarter + 1)
    even[0] = (pairs[0][0] + pairs[count // 2][0], None)
    odd[0] = (pairs[0][0] - pairs[count // 2][0], None)
    even[quarter] = (2.0 * pairs[quarter][0], None)
    odd[quarter] = (-2.0 * pairs[quarter][1], None)
    for k in range(1, quarter):
        angle = 2.0 * math.pi * k / count
        cosine, sine = math.cos(angle), math.sin(angle)
        low_real, low_imag = pairs[k]
        high_real, high_imag = pairs[count // 2 - k]
        even[k] = (low_real + high_real, low_imag - high_imag)
        diff_real, diff_imag = low_real - high_real, low_imag + high_imag
        odd[k] = (diff_real * cosine - diff_imag * sine, diff_imag * cosine + diff_real * sine)
    even_values, odd_values = real_inverse(even), real_inverse(odd)
    return [(even_values if n % 2 == 0 else odd_values)[n // 2] for n in range(count)]


def split_value(value):
    high = value.astype(jnp.bfloat16)
    return high, (value - high.astype(jnp.float32)).astype(jnp.bfloat16)


def dot3(left, right):
    wide = jnp.concatenate([left[0], left[1], left[0]], axis=1)
    tall = jnp.concatenate([right[0], right[0], right[1]], axis=0)
    return jnp.dot(wide, tall, preferred_element_type=jnp.float32)


def inverse_of(value):
    guess = pl.reciprocal(value, approx=True)
    guess = guess * (2.0 - value * guess)
    return guess * (2.0 - value * guess)


def kernel(
    cfg, coupling, spacing, field, span_high, span_low, fwd_high, fwd_low, inv_high, inv_low,
    turn_cos, turn_sin, eig_stream, eig_span, out,
    field_high, field_low, send_box, columns, staging, spectrum, pivots_low, pivots_high, middle,
    reduced, edge_down, from_below, from_above, solved, returned,
    go_send, go_recv, up_send, up_recv, down_send, down_recv, back_send, back_recv,
):
    gx_count, group, planes, chunks, rows, levels, batch = cfg
    peers = gx_count * group
    blocks = field.shape[2] // LANES
    outer = blocks * gx_count
    slots = outer // 2
    level_count = levels * planes
    gx = lax.axis_index("gx")
    gz = lax.axis_index("gz")
    plane = gz // group
    row = gz % group
    me = gx * group + row
    first = plane * levels

    def partner(step):
        return (gx + step // group) % gx_count, (row + step % group) % group

    barrier = pltpu.get_barrier_semaphore()
    for step in range(1, peers):
        to_gx, to_row = partner(step)
        pl.semaphore_signal(barrier, inc=1, device_id=(to_gx, plane * group + to_row), device_id_type=MESH)

    @pl.when(plane > 0)
    def _():
        pl.semaphore_signal(barrier, inc=1, device_id=(gx, gz - group), device_id_type=MESH)

    @pl.when(plane < planes - 1)
    def _():
        pl.semaphore_signal(barrier, inc=1, device_id=(gx, gz + group), device_id_type=MESH)

    def go_copy(chunk, step):
        to_gx, to_row = partner(step)
        return pltpu.make_async_remote_copy(
            src_ref=send_box.at[chunk, to_gx * group + to_row],
            dst_ref=columns.at[chunk, row, pl.ds(gx * blocks, blocks)],
            send_sem=go_send.at[chunk], recv_sem=go_recv.at[chunk],
            device_id=(to_gx, plane * group + to_row), device_id_type=MESH)

    def all_blocks(box, chunk, sem):
        blocks_here = box.at[chunk, pl.ds(0, peers - 1)]
        pltpu.make_async_copy(blocks_here, blocks_here, sem.at[chunk]).wait()

    def back_copy(chunk, step):
        to_gx, to_row = partner(step)
        return pltpu.make_async_remote_copy(
            src_ref=solved.at[chunk, to_row, pl.ds(to_gx * blocks, blocks)],
            dst_ref=returned.at[chunk, me],
            send_sem=back_send.at[chunk], recv_sem=back_recv.at[chunk],
            device_id=(to_gx, plane * group + to_row), device_id_type=MESH)

    def up_copy(chunk):
        return pltpu.make_async_remote_copy(
            src_ref=reduced.at[chunk, levels - 1], dst_ref=from_below.at[chunk],
            send_sem=up_send.at[chunk], recv_sem=up_recv.at[chunk],
            device_id=(gx, (gz + group) % (planes * group)), device_id_type=MESH)

    def down_copy(chunk):
        return pltpu.make_async_remote_copy(
            src_ref=edge_down.at[chunk], dst_ref=from_above.at[chunk],
            send_sem=down_send.at[chunk], recv_sem=down_recv.at[chunk],
            device_id=(gx, (gz + planes * group - group) % (planes * group)), device_id_type=MESH)

    def below(level):
        return coupling[level]

    def above(level):
        return jnp.where(level + 1 < level_count, coupling[jnp.minimum(level + 1, level_count - 1)], 0.0)

    field_high[...], field_low[...] = split_value(field[0])

    def span_step(turn, carry):
        height = batch * peers * rows
        take = pl.ds(pl.multiple_of(turn * height, height), height)
        left = (span_high[take, :], span_low[take, :])
        width = min(2, blocks)
        for block in range(0, blocks, width):
            cols = slice(block * LANES, (block + width) * LANES)
            modes = dot3(left, (field_high[:, cols], field_low[:, cols]))
            for part in range(width):
                piece = modes[:, part * LANES:(part + 1) * LANES]
                piece = piece.reshape(batch, peers, rows, LANES)
                send_box[pl.ds(turn * batch, batch), :, block + part] = piece

        @pl.when(turn == 0)
        def _():
            expected = peers - 1 + jnp.where(plane > 0, 1, 0) + jnp.where(plane < planes - 1, 1, 0)
            pl.semaphore_wait(barrier, expected)

        for index in range(batch):
            chunk = turn * batch + index
            for step in range(1, peers):
                go_copy(chunk, step).start()
            columns[chunk, row, pl.ds(gx * blocks, blocks)] = send_box[chunk, me]
        return carry

    lax.fori_loop(0, chunks // batch, span_step, 0)

    part_slots = min(max(1, 64 // rows), slots)
    parts = slots // part_slots

    def coefficients(chunk):
        def part_step(part, carry):
            take = pl.ds(part * part_slots, part_slots)
            lam = eig_span[chunk * peers + me][None] + eig_stream[take]

            def diagonal(level):
                return lam * spacing[level] + (below(level) + above(level))

            def from_ground(level, pair):
                now, before = pair
                return diagonal(level) * now - (below(level) * below(level)) * before, now

            def from_top(count, pair):
                level = level_count - 1 - count
                now, before = pair
                return diagonal(level) * now - (above(level) * above(level)) * before, now

            nought = lam * 0.0
            start = (nought + 1.0, nought)
            low = lax.fori_loop(0, first, from_ground, start)
            for own in range(levels):
                after = from_ground(first + own, low)
                pivots_low[chunk, own, take] = low[0] * inverse_of(after[0])
                low = after
            top = lax.fori_loop(0, level_count - first - levels, from_top, start)
            edge = above(first + levels - 1)
            both = low[0] * top[0]
            middle[chunk, take] = both * inverse_of(both - (edge * edge) * (low[1] * top[1]))
            for own in reversed(range(levels)):
                after = from_top(level_count - 1 - first - own, top)
                pivots_high[chunk, own, take] = top[0] * inverse_of(after[0])
                top = after
            return carry

        lax.fori_loop(0, parts, part_step, 0)

    tiles = rows // 8

    def stream_forward(chunk):
        def tile_step(index, carry):
            own, tile = index // tiles, index % tiles
            inner = pl.ds(pl.multiple_of(tile * 8, 8), 8)
            place = pl.ds(pl.multiple_of(own * rows + tile * 8, 8), 8)
            pairs = real_transform([columns[chunk, own, n, inner, :] for n in range(outer)])
            staging[0, place, :LANES] = pairs[0][0]
            staging[0, place, LANES:] = pairs[slots][0]
            for k in range(1, slots):
                real, imag = pairs[k]
                cosine, sine = turn_cos[k:k + 1, :], turn_sin[k:k + 1, :]
                staging[k, place, :LANES] = real * cosine + imag * sine
                staging[k, place, LANES:] = imag * cosine - real * sine
            return carry

        lax.fori_loop(0, levels * tiles, tile_step, 0)
        special = dot3(split_value(staging[0]), (fwd_high[0], fwd_low[0]))
        spectrum[chunk, 0] = special.reshape(levels, rows, 2 * LANES)
        rest = staging[1:].reshape((slots - 1) * levels * rows, 2 * LANES)
        regular = dot3(split_value(rest), (fwd_high[1], fwd_low[1]))
        spectrum[chunk, 1:] = regular.reshape(slots - 1, levels, rows, 2 * LANES)

    def sweep_up(chunk):
        @pl.when(plane > 0)
        def _():
            up_copy(chunk).wait_recv()

        @pl.when(plane == 0)
        def _():
            from_below[chunk] = jnp.zeros(from_below.shape[1:], jnp.float32)

        def part_step(part, carry):
            take = pl.ds(part * part_slots, part_slots)
            value = from_below[chunk, take]
            for own in range(levels):
                level = first + own
                value = (spacing[level] * spectrum[chunk, take, own] + below(level) * value) * pivots_low[chunk, own, take]
                reduced[chunk, own, take] = value
            return carry

        lax.fori_loop(0, parts, part_step, 0)

        @pl.when(plane < planes - 1)
        def _():
            up_copy(chunk).start()

    def sweep_down(chunk):
        @pl.when(plane < planes - 1)
        def _():
            down_copy(chunk).wait_recv()

        @pl.when(plane == planes - 1)
        def _():
            from_above[chunk] = jnp.zeros(from_above.shape[1:], jnp.float32)

        @pl.when(plane > 0)
        def _():
            def part_step(part, carry):
                take = pl.ds(part * part_slots, part_slots)
                value = from_above[chunk, take]
                for own in reversed(range(levels)):
                    level = first + own
                    value = (spacing[level] * spectrum[chunk, take, own] + above(level) * value) * pivots_high[chunk, own, take]
                edge_down[chunk, take] = value
                return carry

            lax.fori_loop(0, parts, part_step, 0)
            down_copy(chunk).start()

    def finish(chunk):
        def part_step(part, carry):
            take = pl.ds(part * part_slots, part_slots)
            value = from_above[chunk, take]
            for own in reversed(range(levels)):
                value = reduced[chunk, own, take] + above(first + own) * pivots_low[chunk, own, take] * value
                if own == levels - 1:
                    value = value * middle[chunk, take]
                staging[take, own * rows:(own + 1) * rows, :] = value
            return carry

        lax.fori_loop(0, parts, part_step, 0)
        special = dot3(split_value(staging[0]), (inv_high[0], inv_low[0]))
        rest = staging[1:].reshape((slots - 1) * levels * rows, 2 * LANES)
        regular = dot3(split_value(rest), (inv_high[1], inv_low[1]))
        staging[0] = special
        staging[1:] = regular.reshape(slots - 1, levels * rows, 2 * LANES)

        def tile_step(index, carry):
            own, tile = index // tiles, index % tiles
            inner = pl.ds(pl.multiple_of(tile * 8, 8), 8)
            place = pl.ds(pl.multiple_of(own * rows + tile * 8, 8), 8)
            pairs = [(staging[0, place, :LANES], None)]
            for k in range(1, slots):
                real, imag = staging[k, place, :LANES], staging[k, place, LANES:]
                cosine, sine = turn_cos[k:k + 1, :], turn_sin[k:k + 1, :]
                pairs.append((real * cosine - imag * sine, real * sine + imag * cosine))
            pairs.append((staging[0, place, LANES:], None))
            for n, value in enumerate(real_inverse(pairs)):
                solved[chunk, own, n, inner, :] = value
            return carry

        lax.fori_loop(0, levels * tiles, tile_step, 0)
        returned[chunk, me] = solved[chunk, row, pl.ds(gx * blocks, blocks)]

    def send_back(chunk, carry):
        for step in range(1, peers):
            back_copy(chunk, step).start()
        return carry

    lag_down = planes - 1 - plane
    lag = jnp.maximum(plane, lag_down)
    hold = jnp.maximum(lag, chunks - 2)

    def step(now, carry):
        @pl.when(now < chunks)
        def _():
            coefficients(now)
            all_blocks(send_box, now, go_recv)
            stream_forward(now)

        @pl.when(jnp.logical_and(now >= plane, now < plane + chunks))
        def _():
            sweep_up(now - plane)

        @pl.when(jnp.logical_and(now >= lag_down, now < lag_down + chunks))
        def _():
            sweep_down(now - lag_down)

        @pl.when(jnp.logical_and(now >= lag, now < lag + chunks))
        def _():
            finish(now - lag)

            @pl.when(now >= hold)
            def _():
                lax.fori_loop(jnp.where(now == hold, 0, now - lag), now - lag + 1, send_back, 0)

        return carry

    lax.fori_loop(0, chunks + planes - 1, step, 0)

    def arrive(chunk, carry):
        all_blocks(returned, chunk, back_recv)
        return carry

    span = field.shape[1]
    width = min(2, blocks)
    halves = 2 if chunks % 2 == 0 else 1
    depth = span // halves
    for half in range(halves):
        lax.fori_loop(half * (chunks // halves), (half + 1) * (chunks // halves), arrive, 0)
        near = slice(half * depth, (half + 1) * depth)
        here = slice(half * (chunks // halves), (half + 1) * (chunks // halves))
        left = (span_high[:, near], span_low[:, near])
        for block in range(0, blocks, width):
            pieces = [returned[here, :, block + part].reshape(depth, LANES) for part in range(width)]
            right = split_value(jnp.concatenate(pieces, axis=1) if width > 1 else pieces[0])
            value = dot3(left, right)
            cols = slice(block * LANES, (block + width) * LANES)
            out[0, :, cols] = value if half == 0 else out[0, :, cols] + value

    def drain(chunk, carry):
        all_blocks(send_box, chunk, go_send)
        all_blocks(returned, chunk, back_send)

        @pl.when(plane < planes - 1)
        def _():
            up_copy(chunk).wait_send()

        @pl.when(plane > 0)
        def _():
            down_copy(chunk).wait_send()

        return carry

    lax.fori_loop(0, chunks, drain, 0)


def local(mesh_shape, source_field, coupling, spacing):
    gx_count, gz_count = mesh_shape["gx"], mesh_shape["gz"]
    own, span, part = source_field.shape
    assert own == 1
    group = gz_count // 4 if gz_count % 4 == 0 else 1
    planes = gz_count // group
    levels = group
    peers = gx_count * group
    stream = part * gx_count
    share = span // peers
    chunks = 8
    while share % (8 * chunks):
        chunks //= 2
    rows = share // chunks
    batch = 2 if chunks % 2 == 0 and peers * rows < 128 else 1
    blocks = part // LANES
    outer = stream // LANES
    slots = outer // 2
    tables = make_tables(span, stream, rows)
    f32 = jnp.float32
    wide = (slots, rows, 2 * LANES)
    dma = pltpu.SemaphoreType.DMA
    vmem = pl.BlockSpec(memory_space=pltpu.VMEM)
    smem = pl.BlockSpec(memory_space=pltpu.SMEM)
    cfg = (gx_count, group, planes, chunks, rows, levels, batch)
    return pl.pallas_call(
        functools.partial(kernel, cfg),
        out_shape=jax.ShapeDtypeStruct(source_field.shape, f32),
        in_specs=[smem, smem] + [vmem] * 11,
        out_specs=vmem,
        scratch_shapes=[
            pltpu.VMEM((span, part), jnp.bfloat16),
            pltpu.VMEM((span, part), jnp.bfloat16),
            pltpu.VMEM((chunks, peers, blocks, rows, LANES), f32),
            pltpu.VMEM((chunks, levels, outer, rows, LANES), f32),
            pltpu.VMEM((slots, levels * rows, 2 * LANES), f32),
            pltpu.VMEM((chunks, slots, levels, rows, 2 * LANES), f32),
            pltpu.VMEM((chunks, levels) + wide, f32),
            pltpu.VMEM((chunks, levels) + wide, f32),
            pltpu.VMEM((chunks,) + wide, f32),
            pltpu.VMEM((chunks, levels) + wide, f32),
            pltpu.VMEM((chunks,) + wide, f32),
            pltpu.VMEM((chunks,) + wide, f32),
            pltpu.VMEM((chunks,) + wide, f32),
            pltpu.VMEM((chunks, levels, outer, rows, LANES), f32),
            pltpu.VMEM((chunks, peers, blocks, rows, LANES), f32),
            dma((chunks,)), dma((chunks,)),
            dma((chunks,)), dma((chunks,)), dma((chunks,)), dma((chunks,)),
            dma((chunks,)), dma((chunks,)),
        ],
        compiler_params=pltpu.CompilerParams(
            collective_id=0, has_side_effects=True, vmem_limit_bytes=56 * 1024 * 1024),
        cost_estimate=pl.CostEstimate(flops=8 * 10**9, bytes_accessed=8 * 2**20, transcendentals=0),
    )(coupling, spacing, source_field, *(jnp.asarray(table) for table in tables))


def solution(mesh):
    in_specs = (P("gz", None, "gx"), P(), P())
    out_specs = P("gz", None, "gx")
    return jax.shard_map(
        functools.partial(local, dict(mesh.shape)), mesh=mesh,
        in_specs=in_specs, out_specs=out_specs, check_vma=False)
```

```python
import functools
import math

import jax
import jax.numpy as jnp
import ml_dtypes
import numpy as np
from jax import lax
from jax.experimental import pallas as pl
from jax.experimental.pallas import tpu as pltpu
from jax.sharding import PartitionSpec as P

LANES = 128
MESH = pl.DeviceIdType.MESH


def cos_sin(product, period):
    angles = (product % period).astype(np.float64) * (2.0 * math.pi / period)
    return np.cos(angles), np.sin(angles)


def split_table(table):
    high = table.astype(np.float32).astype(ml_dtypes.bfloat16)
    low = (table - high.astype(np.float64)).astype(np.float32).astype(ml_dtypes.bfloat16)
    return high, low


def make_tables(span, stream, rows):
    outer = stream // LANES
    slots = outer // 2
    ks = np.arange(span)
    cosine, sine = cos_sin(ks[:, None] * ks[None, :], span)
    span_high, span_low = split_table(cosine + sine)
    lane = np.arange(LANES)
    cosine, sine = cos_sin(lane[:, None] * lane[None, :], LANES)
    regular = np.block([[cosine, -sine], [sine, cosine]])
    half_cos, half_sin = cos_sin(lane[:, None] * (slots + outer * lane[None, :]), stream)
    zeros = np.zeros((LANES, LANES))
    special = np.block([[cosine + sine, zeros], [zeros, half_cos + half_sin]])
    forward = np.stack([special, regular])
    inverse = np.stack([special.T, regular.T]) / (span * stream)
    forward_high, forward_low = split_table(forward)
    inverse_high, inverse_low = split_table(inverse)
    turn_cos, turn_sin = cos_sin(np.arange(slots)[:, None] * lane[None, :], stream)
    wave = np.arange(slots + 1)[:, None] + outer * lane[None, :]
    eigen_stream = 2.0 - 2.0 * cos_sin(wave, stream)[0]
    eigen_stream = np.ascontiguousarray(np.broadcast_to(eigen_stream[:, None, :], (slots + 1, rows, LANES)))
    eigen_span = 2.0 - 2.0 * cos_sin(ks, span)[0]
    eigen_span = np.broadcast_to(eigen_span[:, None], (span, LANES)).reshape(span // rows, rows, LANES)
    return (
        span_high, span_low, forward_high, forward_low, inverse_high, inverse_low,
        turn_cos.astype(np.float32), turn_sin.astype(np.float32),
        eigen_stream.astype(np.float32), np.ascontiguousarray(eigen_span).astype(np.float32),
    )


def real_transform(values):
    count = len(values)
    if count == 2:
        return [(values[0] + values[1], None), (values[0] - values[1], None)]
    even = real_transform(values[0::2])
    odd = real_transform(values[1::2])
    result = [None] * (count // 2 + 1)
    quarter = count // 4
    result[0] = (even[0][0] + odd[0][0], None)
    result[count // 2] = (even[0][0] - odd[0][0], None)
    result[quarter] = (even[quarter][0], -odd[quarter][0])
    for k in range(1, quarter):
        angle = 2.0 * math.pi * k / count
        cosine, sine = math.cos(angle), math.sin(angle)
        odd_real, odd_imag = odd[k]
        turned_real = odd_real * cosine + odd_imag * sine
        turned_imag = odd_imag * cosine - odd_real * sine
        even_real, even_imag = even[k]
        result[k] = (even_real + turned_real, even_imag + turned_imag)
        result[count // 2 - k] = (even_real - turned_real, turned_imag - even_imag)
    return result


def real_inverse(pairs):
    count = 2 * (len(pairs) - 1)
    if count == 2:
        return [pairs[0][0] + pairs[1][0], pairs[0][0] - pairs[1][0]]
    quarter = count // 4
    even, odd = [None] * (quarter + 1), [None] * (quarter + 1)
    even[0] = (pairs[0][0] + pairs[count // 2][0], None)
    odd[0] = (pairs[0][0] - pairs[count // 2][0], None)
    even[quarter] = (2.0 * pairs[quarter][0], None)
    odd[quarter] = (-2.0 * pairs[quarter][1], None)
    for k in range(1, quarter):
        angle = 2.0 * math.pi * k / count
        cosine, sine = math.cos(angle), math.sin(angle)
        low_real, low_imag = pairs[k]
        high_real, high_imag = pairs[count // 2 - k]
        even[k] = (low_real + high_real, low_imag - high_imag)
        diff_real, diff_imag = low_real - high_real, low_imag + high_imag
        odd[k] = (diff_real * cosine - diff_imag * sine, diff_imag * cosine + diff_real * sine)
    even_values, odd_values = real_inverse(even), real_inverse(odd)
    return [(even_values if n % 2 == 0 else odd_values)[n // 2] for n in range(count)]


def split_value(value):
    high = value.astype(jnp.bfloat16)
    return high, (value - high.astype(jnp.float32)).astype(jnp.bfloat16)


def dot3(left, right):
    wide = jnp.concatenate([left[0], left[1], left[0]], axis=1)
    tall = jnp.concatenate([right[0], right[0], right[1]], axis=0)
    return jnp.dot(wide, tall, preferred_element_type=jnp.float32)


def inverse_of(value):
    guess = pl.reciprocal(value, approx=True)
    guess = guess * (2.0 - value * guess)
    return guess * (2.0 - value * guess)


def kernel(
    cfg, coupling, spacing, field, span_high, span_low, fwd_high, fwd_low, inv_high, inv_low,
    turn_cos, turn_sin, eig_stream, eig_span, out,
    field_high, field_low, send_box, columns, staging, spectrum, pivots_low, pivots_high, middle,
    reduced, edge_down, from_below, from_above, solved, returned,
    go_send, go_recv, up_send, up_recv, down_send, down_recv, back_send, back_recv,
):
    gx_count, group, planes, chunks, rows, levels, batch, back_groups = cfg
    peers = gx_count * group
    blocks = field.shape[2] // LANES
    outer = blocks * gx_count
    slots = outer // 2
    level_count = levels * planes
    gx = lax.axis_index("gx")
    gz = lax.axis_index("gz")
    plane = gz // group
    row = gz % group
    me = gx * group + row
    first = plane * levels

    def partner(step):
        return (gx + step // group) % gx_count, (row + step % group) % group

    barrier = pltpu.get_barrier_semaphore()
    for step in range(1, peers):
        to_gx, to_row = partner(step)
        pl.semaphore_signal(barrier, inc=1, device_id=(to_gx, plane * group + to_row), device_id_type=MESH)

    @pl.when(plane > 0)
    def _():
        pl.semaphore_signal(barrier, inc=1, device_id=(gx, gz - group), device_id_type=MESH)

    @pl.when(plane < planes - 1)
    def _():
        pl.semaphore_signal(barrier, inc=1, device_id=(gx, gz + group), device_id_type=MESH)

    def go_copy(turn, step):
        to_gx, to_row = partner(step)
        here = pl.ds(turn * batch, batch)
        return pltpu.make_async_remote_copy(
            src_ref=send_box.at[here, to_gx * group + to_row],
            dst_ref=columns.at[here, row, pl.ds(gx * blocks, blocks)],
            send_sem=go_send.at[turn], recv_sem=go_recv.at[turn],
            device_id=(to_gx, plane * group + to_row), device_id_type=MESH)

    def back_copy(index, step):
        begin, count = back_groups[index]
        to_gx, to_row = partner(step)
        return pltpu.make_async_remote_copy(
            src_ref=solved.at[begin:begin + count, to_row, pl.ds(to_gx * blocks, blocks)],
            dst_ref=returned.at[begin:begin + count, me],
            send_sem=back_send.at[index], recv_sem=back_recv.at[index],
            device_id=(to_gx, plane * group + to_row), device_id_type=MESH)

    def all_blocks(box, begin, count, sem):
        blocks_here = box.at[pl.ds(begin, count), pl.ds(0, peers - 1)]
        pltpu.make_async_copy(blocks_here, blocks_here, sem).wait()

    def up_copy(chunk):
        return pltpu.make_async_remote_copy(
            src_ref=reduced.at[chunk, levels - 1], dst_ref=from_below.at[chunk],
            send_sem=up_send.at[chunk], recv_sem=up_recv.at[chunk],
            device_id=(gx, (gz + group) % (planes * group)), device_id_type=MESH)

    def down_copy(chunk):
        return pltpu.make_async_remote_copy(
            src_ref=edge_down.at[chunk], dst_ref=from_above.at[chunk],
            send_sem=down_send.at[chunk], recv_sem=down_recv.at[chunk],
            device_id=(gx, (gz + planes * group - group) % (planes * group)), device_id_type=MESH)

    def below(level):
        return coupling[level]

    def above(level):
        return jnp.where(level + 1 < level_count, coupling[jnp.minimum(level + 1, level_count - 1)], 0.0)

    field_high[...], field_low[...] = split_value(field[0])

    def span_step(turn, carry):
        height = batch * peers * rows
        take = pl.ds(pl.multiple_of(turn * height, height), height)
        left = (span_high[take, :], span_low[take, :])
        width = min(2, blocks)
        for block in range(0, blocks, width):
            cols = slice(block * LANES, (block + width) * LANES)
            modes = dot3(left, (field_high[:, cols], field_low[:, cols]))
            for part in range(width):
                piece = modes[:, part * LANES:(part + 1) * LANES]
                piece = piece.reshape(batch, peers, rows, LANES)
                send_box[pl.ds(turn * batch, batch), :, block + part] = piece

        @pl.when(turn == 0)
        def _():
            expected = peers - 1 + jnp.where(plane > 0, 1, 0) + jnp.where(plane < planes - 1, 1, 0)
            pl.semaphore_wait(barrier, expected)

        for step in range(1, peers):
            go_copy(turn, step).start()
        for index in range(batch):
            chunk = turn * batch + index
            columns[chunk, row, pl.ds(gx * blocks, blocks)] = send_box[chunk, me]
        return carry

    lax.fori_loop(0, chunks // batch, span_step, 0)

    part_slots = min(max(1, 64 // rows), slots)
    parts = slots // part_slots

    def coefficients(chunk):
        def store(target, begin, value):
            count = value.shape[0]
            low, high = (1 if begin == 0 else 0), (count - 1 if begin + count == slots + 1 else count)
            if low:
                target[0, :, :LANES] = value[0]
            if high < count:
                target[0, :, LANES:] = value[high]
            target[begin + low:begin + high, :, :LANES] = value[low:high]
            target[begin + low:begin + high, :, LANES:] = value[low:high]

        middle_unit = slots // 2 + 1
        for begin, end in ((0, middle_unit), (middle_unit, slots + 1)):
            lam = eig_span[chunk * peers + me][None] + eig_stream[begin:end]

            def diagonal(level):
                return lam * spacing[level] + (below(level) + above(level))

            def from_ground(level, pair):
                now, before = pair
                return diagonal(level) * now - (below(level) * below(level)) * before, now

            def from_top(count, pair):
                level = level_count - 1 - count
                now, before = pair
                return diagonal(level) * now - (above(level) * above(level)) * before, now

            nought = lam * 0.0
            start = (nought + 1.0, nought)
            low = lax.fori_loop(0, first, from_ground, start)
            for own in range(levels):
                after = from_ground(first + own, low)
                store(pivots_low.at[chunk, own], begin, low[0] * inverse_of(after[0]))
                low = after
            top = lax.fori_loop(0, level_count - first - levels, from_top, start)
            edge = above(first + levels - 1)
            both = low[0] * top[0]
            store(middle.at[chunk], begin, both * inverse_of(both - (edge * edge) * (low[1] * top[1])))
            for own in reversed(range(levels)):
                after = from_top(level_count - 1 - first - own, top)
                store(pivots_high.at[chunk, own], begin, top[0] * inverse_of(after[0]))
                top = after

    tiles = rows // 8

    def stream_forward(chunk):
        def tile_step(index, carry):
            own, tile = index // tiles, index % tiles
            inner = pl.ds(pl.multiple_of(tile * 8, 8), 8)
            place = pl.ds(pl.multiple_of(own * rows + tile * 8, 8), 8)
            pairs = real_transform([columns[chunk, own, n, inner, :] for n in range(outer)])
            staging[0, place, :LANES] = pairs[0][0]
            staging[0, place, LANES:] = pairs[slots][0]
            for k in range(1, slots):
                real, imag = pairs[k]
                cosine, sine = turn_cos[k:k + 1, :], turn_sin[k:k + 1, :]
                staging[k, place, :LANES] = real * cosine + imag * sine
                staging[k, place, LANES:] = imag * cosine - real * sine
            return carry

        lax.fori_loop(0, levels * tiles, tile_step, 0)
        special = dot3(split_value(staging[0]), (fwd_high[0], fwd_low[0]))
        spectrum[chunk, 0] = special.reshape(levels, rows, 2 * LANES)
        rest = staging[1:].reshape((slots - 1) * levels * rows, 2 * LANES)
        regular = dot3(split_value(rest), (fwd_high[1], fwd_low[1]))
        spectrum[chunk, 1:] = regular.reshape(slots - 1, levels, rows, 2 * LANES)

    def sweep_up(chunk):
        @pl.when(plane > 0)
        def _():
            up_copy(chunk).wait_recv()

        @pl.when(plane == 0)
        def _():
            from_below[chunk] = jnp.zeros(from_below.shape[1:], jnp.float32)

        def part_step(part, carry):
            take = pl.ds(part * part_slots, part_slots)
            value = from_below[chunk, take]
            for own in range(levels):
                level = first + own
                value = (spacing[level] * spectrum[chunk, take, own] + below(level) * value) * pivots_low[chunk, own, take]
                reduced[chunk, own, take] = value
            return carry

        lax.fori_loop(0, parts, part_step, 0)

        @pl.when(plane < planes - 1)
        def _():
            up_copy(chunk).start()

    def sweep_down(chunk):
        @pl.when(plane < planes - 1)
        def _():
            down_copy(chunk).wait_recv()

        @pl.when(plane == planes - 1)
        def _():
            from_above[chunk] = jnp.zeros(from_above.shape[1:], jnp.float32)

        @pl.when(plane > 0)
        def _():
            def part_step(part, carry):
                take = pl.ds(part * part_slots, part_slots)
                value = from_above[chunk, take]
                for own in reversed(range(levels)):
                    level = first + own
                    value = (spacing[level] * spectrum[chunk, take, own] + above(level) * value) * pivots_high[chunk, own, take]
                edge_down[chunk, take] = value
                return carry

            lax.fori_loop(0, parts, part_step, 0)
            down_copy(chunk).start()

    def finish(chunk):
        def part_step(part, carry):
            take = pl.ds(part * part_slots, part_slots)
            value = from_above[chunk, take]
            for own in reversed(range(levels)):
                value = reduced[chunk, own, take] + above(first + own) * pivots_low[chunk, own, take] * value
                if own == levels - 1:
                    value = value * middle[chunk, take]
                staging[take, own * rows:(own + 1) * rows, :] = value
            return carry

        lax.fori_loop(0, parts, part_step, 0)
        special = dot3(split_value(staging[0]), (inv_high[0], inv_low[0]))
        rest = staging[1:].reshape((slots - 1) * levels * rows, 2 * LANES)
        regular = dot3(split_value(rest), (inv_high[1], inv_low[1]))
        staging[0] = special
        staging[1:] = regular.reshape(slots - 1, levels * rows, 2 * LANES)

        def tile_step(index, carry):
            own, tile = index // tiles, index % tiles
            inner = pl.ds(pl.multiple_of(tile * 8, 8), 8)
            place = pl.ds(pl.multiple_of(own * rows + tile * 8, 8), 8)
            pairs = [(staging[0, place, :LANES], None)]
            for k in range(1, slots):
                real, imag = staging[k, place, :LANES], staging[k, place, LANES:]
                cosine, sine = turn_cos[k:k + 1, :], turn_sin[k:k + 1, :]
                pairs.append((real * cosine - imag * sine, real * sine + imag * cosine))
            pairs.append((staging[0, place, LANES:], None))
            for n, value in enumerate(real_inverse(pairs)):
                solved[chunk, own, n, inner, :] = value
            return carry

        lax.fori_loop(0, levels * tiles, tile_step, 0)
        returned[chunk, me] = solved[chunk, row, pl.ds(gx * blocks, blocks)]
        for index, (begin, count) in enumerate(back_groups):
            @pl.when(chunk == begin + count - 1)
            def _():
                for step in range(1, peers):
                    back_copy(index, step).start()

    lag_down = planes - 1 - plane
    lag = jnp.maximum(plane, lag_down)

    def step(now, carry):
        @pl.when(now < chunks)
        def _():
            coefficients(now)

            @pl.when(now % batch == 0)
            def _():
                all_blocks(send_box, now, batch, go_recv.at[now // batch])

            stream_forward(now)

        @pl.when(jnp.logical_and(now >= plane, now < plane + chunks))
        def _():
            sweep_up(now - plane)

        @pl.when(jnp.logical_and(now >= lag_down, now < lag_down + chunks))
        def _():
            sweep_down(now - lag_down)

        @pl.when(jnp.logical_and(now >= lag, now < lag + chunks))
        def _():
            finish(now - lag)

        return carry

    lax.fori_loop(0, chunks + planes - 1, step, 0)

    span = field.shape[1]
    width = min(2, blocks)
    halves = 2 if chunks % 2 == 0 else 1
    depth = span // halves
    for half in range(halves):
        for index, (begin, count) in enumerate(back_groups):
            if half * (chunks // halves) <= begin < (half + 1) * (chunks // halves):
                all_blocks(returned, begin, count, back_recv.at[index])
        near = slice(half * depth, (half + 1) * depth)
        here = slice(half * (chunks // halves), (half + 1) * (chunks // halves))
        left = (span_high[:, near], span_low[:, near])
        for block in range(0, blocks, width):
            pieces = [returned[here, :, block + part].reshape(depth, LANES) for part in range(width)]
            right = split_value(jnp.concatenate(pieces, axis=1) if width > 1 else pieces[0])
            value = dot3(left, right)
            cols = slice(block * LANES, (block + width) * LANES)
            out[0, :, cols] = value if half == 0 else out[0, :, cols] + value

    def drain(chunk, carry):
        @pl.when(plane < planes - 1)
        def _():
            up_copy(chunk).wait_send()

        @pl.when(plane > 0)
        def _():
            down_copy(chunk).wait_send()

        return carry

    lax.fori_loop(0, chunks, drain, 0)
    for turn in range(chunks // batch):
        all_blocks(send_box, turn * batch, batch, go_send.at[turn])
    for index, (begin, count) in enumerate(back_groups):
        all_blocks(returned, begin, count, back_send.at[index])


def local(mesh_shape, source_field, coupling, spacing):
    gx_count, gz_count = mesh_shape["gx"], mesh_shape["gz"]
    own, span, part = source_field.shape
    assert own == 1
    group = gz_count // 4 if gz_count % 4 == 0 else 1
    planes = gz_count // group
    levels = group
    peers = gx_count * group
    stream = part * gx_count
    share = span // peers
    chunks = 8
    while share % (8 * chunks):
        chunks //= 2
    rows = share // chunks
    batch = 2 if chunks % 2 == 0 and peers * rows < 128 else 1
    paired = max(0, chunks - 2) // 2 * 2
    back_groups = [(begin, 2) for begin in range(0, paired, 2)] + [(begin, 1) for begin in range(paired, chunks)]
    blocks = part // LANES
    outer = stream // LANES
    slots = outer // 2
    tables = make_tables(span, stream, rows)
    f32 = jnp.float32
    wide = (slots, rows, 2 * LANES)
    dma = pltpu.SemaphoreType.DMA
    vmem = pl.BlockSpec(memory_space=pltpu.VMEM)
    smem = pl.BlockSpec(memory_space=pltpu.SMEM)
    cfg = (gx_count, group, planes, chunks, rows, levels, batch, back_groups)
    return pl.pallas_call(
        functools.partial(kernel, cfg),
        out_shape=jax.ShapeDtypeStruct(source_field.shape, f32),
        in_specs=[smem, smem] + [vmem] * 11,
        out_specs=vmem,
        scratch_shapes=[
            pltpu.VMEM((span, part), jnp.bfloat16),
            pltpu.VMEM((span, part), jnp.bfloat16),
            pltpu.VMEM((chunks, peers, blocks, rows, LANES), f32),
            pltpu.VMEM((chunks, levels, outer, rows, LANES), f32),
            pltpu.VMEM((slots, levels * rows, 2 * LANES), f32),
            pltpu.VMEM((chunks, slots, levels, rows, 2 * LANES), f32),
            pltpu.VMEM((chunks, levels) + wide, f32),
            pltpu.VMEM((chunks, levels) + wide, f32),
            pltpu.VMEM((chunks,) + wide, f32),
            pltpu.VMEM((chunks, levels) + wide, f32),
            pltpu.VMEM((chunks,) + wide, f32),
            pltpu.VMEM((chunks,) + wide, f32),
            pltpu.VMEM((chunks,) + wide, f32),
            pltpu.VMEM((chunks, levels, outer, rows, LANES), f32),
            pltpu.VMEM((chunks, peers, blocks, rows, LANES), f32),
            dma((chunks // batch,)), dma((chunks // batch,)),
            dma((chunks,)), dma((chunks,)), dma((chunks,)), dma((chunks,)),
            dma((len(back_groups),)), dma((len(back_groups),)),
        ],
        compiler_params=pltpu.CompilerParams(
            collective_id=0, has_side_effects=True, vmem_limit_bytes=56 * 1024 * 1024),
        cost_estimate=pl.CostEstimate(flops=8 * 10**9, bytes_accessed=8 * 2**20, transcendentals=0),
    )(coupling, spacing, source_field, *(jnp.asarray(table) for table in tables))


def solution(mesh):
    in_specs = (P("gz", None, "gx"), P(), P())
    out_specs = P("gz", None, "gx")
    return jax.shard_map(
        functools.partial(local, dict(mesh.shape)), mesh=mesh,
        in_specs=in_specs, out_specs=out_specs, check_vma=False)
```

```python
import functools
import math

import jax
import jax.numpy as jnp
import ml_dtypes
import numpy as np
from jax import lax
from jax.experimental import pallas as pl
from jax.experimental.pallas import tpu as pltpu
from jax.sharding import PartitionSpec as P

LANES = 128
MESH = pl.DeviceIdType.MESH


def cos_sin(product, period):
    angles = (product % period).astype(np.float64) * (2.0 * math.pi / period)
    return np.cos(angles), np.sin(angles)


def split_table(table):
    high = table.astype(np.float32).astype(ml_dtypes.bfloat16)
    low = (table - high.astype(np.float64)).astype(np.float32).astype(ml_dtypes.bfloat16)
    return high, low


def make_tables(span, stream, rows):
    outer = stream // LANES
    slots = outer // 2
    ks = np.arange(span)
    cosine, sine = cos_sin(ks[:, None] * ks[None, :], span)
    span_high, span_low = split_table(cosine + sine)
    lane = np.arange(LANES)
    cosine, sine = cos_sin(lane[:, None] * lane[None, :], LANES)
    regular = np.block([[cosine, -sine], [sine, cosine]])
    half_cos, half_sin = cos_sin(lane[:, None] * (slots + outer * lane[None, :]), stream)
    zeros = np.zeros((LANES, LANES))
    special = np.block([[cosine + sine, zeros], [zeros, half_cos + half_sin]])
    forward = np.stack([special, regular])
    inverse = np.stack([special.T, regular.T]) / (span * stream)
    forward_high, forward_low = split_table(forward)
    inverse_high, inverse_low = split_table(inverse)
    turn_cos, turn_sin = cos_sin(np.arange(slots)[:, None] * lane[None, :], stream)
    wave = np.arange(slots + 1)[:, None] + outer * lane[None, :]
    eigen_stream = 2.0 - 2.0 * cos_sin(wave, stream)[0]
    eigen_stream = np.ascontiguousarray(np.broadcast_to(eigen_stream[:, None, :], (slots + 1, rows, LANES)))
    eigen_span = 2.0 - 2.0 * cos_sin(ks, span)[0]
    eigen_span = np.broadcast_to(eigen_span[:, None], (span, LANES)).reshape(span // rows, rows, LANES)
    return (
        span_high, span_low, forward_high, forward_low, inverse_high, inverse_low,
        turn_cos.astype(np.float32), turn_sin.astype(np.float32),
        eigen_stream.astype(np.float32), np.ascontiguousarray(eigen_span).astype(np.float32),
    )


def real_transform(values):
    count = len(values)
    if count == 2:
        return [(values[0] + values[1], None), (values[0] - values[1], None)]
    even = real_transform(values[0::2])
    odd = real_transform(values[1::2])
    result = [None] * (count // 2 + 1)
    quarter = count // 4
    result[0] = (even[0][0] + odd[0][0], None)
    result[count // 2] = (even[0][0] - odd[0][0], None)
    result[quarter] = (even[quarter][0], -odd[quarter][0])
    for k in range(1, quarter):
        angle = 2.0 * math.pi * k / count
        cosine, sine = math.cos(angle), math.sin(angle)
        odd_real, odd_imag = odd[k]
        turned_real = odd_real * cosine + odd_imag * sine
        turned_imag = odd_imag * cosine - odd_real * sine
        even_real, even_imag = even[k]
        result[k] = (even_real + turned_real, even_imag + turned_imag)
        result[count // 2 - k] = (even_real - turned_real, turned_imag - even_imag)
    return result


def real_inverse(pairs):
    count = 2 * (len(pairs) - 1)
    if count == 2:
        return [pairs[0][0] + pairs[1][0], pairs[0][0] - pairs[1][0]]
    quarter = count // 4
    even, odd = [None] * (quarter + 1), [None] * (quarter + 1)
    even[0] = (pairs[0][0] + pairs[count // 2][0], None)
    odd[0] = (pairs[0][0] - pairs[count // 2][0], None)
    even[quarter] = (2.0 * pairs[quarter][0], None)
    odd[quarter] = (-2.0 * pairs[quarter][1], None)
    for k in range(1, quarter):
        angle = 2.0 * math.pi * k / count
        cosine, sine = math.cos(angle), math.sin(angle)
        low_real, low_imag = pairs[k]
        high_real, high_imag = pairs[count // 2 - k]
        even[k] = (low_real + high_real, low_imag - high_imag)
        diff_real, diff_imag = low_real - high_real, low_imag + high_imag
        odd[k] = (diff_real * cosine - diff_imag * sine, diff_imag * cosine + diff_real * sine)
    even_values, odd_values = real_inverse(even), real_inverse(odd)
    return [(even_values if n % 2 == 0 else odd_values)[n // 2] for n in range(count)]


def split_value(value):
    high = value.astype(jnp.bfloat16)
    return high, (value - high.astype(jnp.float32)).astype(jnp.bfloat16)


def dot3(left, right):
    wide = jnp.concatenate([left[0], left[1], left[0]], axis=1)
    tall = jnp.concatenate([right[0], right[0], right[1]], axis=0)
    return jnp.dot(wide, tall, preferred_element_type=jnp.float32)


def inverse_of(value):
    guess = pl.reciprocal(value, approx=True)
    guess = guess * (2.0 - value * guess)
    return guess * (2.0 - value * guess)


def kernel(
    cfg, coupling, spacing, field, span_high, span_low, fwd_high, fwd_low, inv_high, inv_low,
    turn_cos, turn_sin, eig_stream, eig_span, returned,
    field_high, field_low, send_box, columns, staging, spectrum, pivots_low, pivots_high, middle,
    reduced, edge_down, from_below, from_above, solved,
    go_send, go_recv, up_send, up_recv, down_send, down_recv, back_send, back_recv, own_sem,
):
    gx_count, group, planes, chunks, rows, levels, batch, back_groups = cfg
    peers = gx_count * group
    blocks = field.shape[2] // LANES
    outer = blocks * gx_count
    slots = outer // 2
    level_count = levels * planes
    gx = lax.axis_index("gx")
    gz = lax.axis_index("gz")
    plane = gz // group
    row = gz % group
    me = gx * group + row
    first = plane * levels

    def partner(step):
        return (gx + step // group) % gx_count, (row + step % group) % group

    barrier = pltpu.get_barrier_semaphore()
    for step in range(1, peers):
        to_gx, to_row = partner(step)
        pl.semaphore_signal(barrier, inc=1, device_id=(to_gx, plane * group + to_row), device_id_type=MESH)

    @pl.when(plane > 0)
    def _():
        pl.semaphore_signal(barrier, inc=1, device_id=(gx, gz - group), device_id_type=MESH)

    @pl.when(plane < planes - 1)
    def _():
        pl.semaphore_signal(barrier, inc=1, device_id=(gx, gz + group), device_id_type=MESH)

    def go_copy(turn, step):
        to_gx, to_row = partner(step)
        here = pl.ds(turn * batch, batch)
        return pltpu.make_async_remote_copy(
            src_ref=send_box.at[here, to_gx * group + to_row],
            dst_ref=columns.at[here, row, pl.ds(gx * blocks, blocks)],
            send_sem=go_send.at[turn], recv_sem=go_recv.at[turn],
            device_id=(to_gx, plane * group + to_row), device_id_type=MESH)

    def back_copy(index, step):
        begin, count = back_groups[index]
        to_gx, to_row = partner(step)
        return pltpu.make_async_remote_copy(
            src_ref=solved.at[begin:begin + count, to_row, pl.ds(to_gx * blocks, blocks)],
            dst_ref=returned.at[begin:begin + count, me],
            send_sem=back_send.at[index], recv_sem=back_recv.at[index],
            device_id=(to_gx, plane * group + to_row), device_id_type=MESH)

    def own_copy(chunk):
        return pltpu.make_async_copy(
            solved.at[chunk, row, pl.ds(gx * blocks, blocks)], returned.at[chunk, me], own_sem.at[chunk])

    def all_blocks(box, begin, count, sem):
        blocks_here = box.at[pl.ds(begin, count), pl.ds(0, peers - 1)]
        pltpu.make_async_copy(blocks_here, blocks_here, sem).wait()

    def up_copy(chunk):
        return pltpu.make_async_remote_copy(
            src_ref=reduced.at[chunk, levels - 1], dst_ref=from_below.at[chunk],
            send_sem=up_send.at[chunk], recv_sem=up_recv.at[chunk],
            device_id=(gx, (gz + group) % (planes * group)), device_id_type=MESH)

    def down_copy(chunk):
        return pltpu.make_async_remote_copy(
            src_ref=edge_down.at[chunk], dst_ref=from_above.at[chunk],
            send_sem=down_send.at[chunk], recv_sem=down_recv.at[chunk],
            device_id=(gx, (gz + planes * group - group) % (planes * group)), device_id_type=MESH)

    def below(level):
        return coupling[level]

    def above(level):
        return jnp.where(level + 1 < level_count, coupling[jnp.minimum(level + 1, level_count - 1)], 0.0)

    field_high[...], field_low[...] = split_value(field[0])

    def span_step(turn, carry):
        height = batch * peers * rows
        take = pl.ds(pl.multiple_of(turn * height, height), height)
        left = (span_high[take, :], span_low[take, :])
        width = min(2, blocks)
        for block in range(0, blocks, width):
            cols = slice(block * LANES, (block + width) * LANES)
            modes = dot3(left, (field_high[:, cols], field_low[:, cols]))
            for part in range(width):
                piece = modes[:, part * LANES:(part + 1) * LANES]
                piece = piece.reshape(batch, peers, rows, LANES)
                send_box[pl.ds(turn * batch, batch), :, block + part] = piece

        @pl.when(turn == 0)
        def _():
            expected = peers - 1 + jnp.where(plane > 0, 1, 0) + jnp.where(plane < planes - 1, 1, 0)
            pl.semaphore_wait(barrier, expected)

        for step in range(1, peers):
            go_copy(turn, step).start()
        for index in range(batch):
            chunk = turn * batch + index
            columns[chunk, row, pl.ds(gx * blocks, blocks)] = send_box[chunk, me]
        return carry

    lax.fori_loop(0, chunks // batch, span_step, 0)

    part_slots = min(max(1, 64 // rows), slots)
    parts = slots // part_slots

    def coefficients(chunk):
        def store(target, begin, value):
            count = value.shape[0]
            low, high = (1 if begin == 0 else 0), (count - 1 if begin + count == slots + 1 else count)
            if low:
                target[0, :, :LANES] = value[0]
            if high < count:
                target[0, :, LANES:] = value[high]
            target[begin + low:begin + high, :, :LANES] = value[low:high]
            target[begin + low:begin + high, :, LANES:] = value[low:high]

        middle_unit = slots // 2 + 1
        for begin, end in ((0, middle_unit), (middle_unit, slots + 1)):
            lam = eig_span[chunk * peers + me][None] + eig_stream[begin:end]

            def diagonal(level):
                return lam * spacing[level] + (below(level) + above(level))

            def from_ground(level, pair):
                now, before = pair
                return diagonal(level) * now - (below(level) * below(level)) * before, now

            def from_top(count, pair):
                level = level_count - 1 - count
                now, before = pair
                return diagonal(level) * now - (above(level) * above(level)) * before, now

            nought = lam * 0.0
            start = (nought + 1.0, nought)
            low = lax.fori_loop(0, first, from_ground, start)
            for own in range(levels):
                after = from_ground(first + own, low)
                store(pivots_low.at[chunk, own], begin, low[0] * inverse_of(after[0]))
                low = after
            top = lax.fori_loop(0, level_count - first - levels, from_top, start)
            edge = above(first + levels - 1)
            both = low[0] * top[0]
            store(middle.at[chunk], begin, both * inverse_of(both - (edge * edge) * (low[1] * top[1])))
            for own in reversed(range(levels)):
                after = from_top(level_count - 1 - first - own, top)
                store(pivots_high.at[chunk, own], begin, top[0] * inverse_of(after[0]))
                top = after

    tiles = rows // 8

    def stream_forward(chunk):
        def tile_step(index, carry):
            own, tile = index // tiles, index % tiles
            inner = pl.ds(pl.multiple_of(tile * 8, 8), 8)
            place = pl.ds(pl.multiple_of(own * rows + tile * 8, 8), 8)
            pairs = real_transform([columns[chunk, own, n, inner, :] for n in range(outer)])
            staging[0, place, :LANES] = pairs[0][0]
            staging[0, place, LANES:] = pairs[slots][0]
            for k in range(1, slots):
                real, imag = pairs[k]
                cosine, sine = turn_cos[k:k + 1, :], turn_sin[k:k + 1, :]
                staging[k, place, :LANES] = real * cosine + imag * sine
                staging[k, place, LANES:] = imag * cosine - real * sine
            return carry

        lax.fori_loop(0, levels * tiles, tile_step, 0)
        special = dot3(split_value(staging[0]), (fwd_high[0], fwd_low[0]))
        spectrum[chunk, 0] = special.reshape(levels, rows, 2 * LANES)
        rest = staging[1:].reshape((slots - 1) * levels * rows, 2 * LANES)
        regular = dot3(split_value(rest), (fwd_high[1], fwd_low[1]))
        spectrum[chunk, 1:] = regular.reshape(slots - 1, levels, rows, 2 * LANES)

    def sweep_up(chunk):
        @pl.when(plane > 0)
        def _():
            up_copy(chunk).wait_recv()

        @pl.when(plane == 0)
        def _():
            from_below[chunk] = jnp.zeros(from_below.shape[1:], jnp.float32)

        def part_step(part, carry):
            take = pl.ds(part * part_slots, part_slots)
            value = from_below[chunk, take]
            for own in range(levels):
                level = first + own
                value = (spacing[level] * spectrum[chunk, take, own] + below(level) * value) * pivots_low[chunk, own, take]
                reduced[chunk, own, take] = value
            return carry

        lax.fori_loop(0, parts, part_step, 0)

        @pl.when(plane < planes - 1)
        def _():
            up_copy(chunk).start()

    def sweep_down(chunk):
        @pl.when(plane < planes - 1)
        def _():
            down_copy(chunk).wait_recv()

        @pl.when(plane == planes - 1)
        def _():
            from_above[chunk] = jnp.zeros(from_above.shape[1:], jnp.float32)

        @pl.when(plane > 0)
        def _():
            def part_step(part, carry):
                take = pl.ds(part * part_slots, part_slots)
                value = from_above[chunk, take]
                for own in reversed(range(levels)):
                    level = first + own
                    value = (spacing[level] * spectrum[chunk, take, own] + above(level) * value) * pivots_high[chunk, own, take]
                edge_down[chunk, take] = value
                return carry

            lax.fori_loop(0, parts, part_step, 0)
            down_copy(chunk).start()

    def finish(chunk):
        def part_step(part, carry):
            take = pl.ds(part * part_slots, part_slots)
            value = from_above[chunk, take]
            for own in reversed(range(levels)):
                value = reduced[chunk, own, take] + above(first + own) * pivots_low[chunk, own, take] * value
                if own == levels - 1:
                    value = value * middle[chunk, take]
                staging[take, own * rows:(own + 1) * rows, :] = value
            return carry

        lax.fori_loop(0, parts, part_step, 0)
        special = dot3(split_value(staging[0]), (inv_high[0], inv_low[0]))
        rest = staging[1:].reshape((slots - 1) * levels * rows, 2 * LANES)
        regular = dot3(split_value(rest), (inv_high[1], inv_low[1]))
        staging[0] = special
        staging[1:] = regular.reshape(slots - 1, levels * rows, 2 * LANES)

        def tile_step(index, carry):
            own, tile = index // tiles, index % tiles
            inner = pl.ds(pl.multiple_of(tile * 8, 8), 8)
            place = pl.ds(pl.multiple_of(own * rows + tile * 8, 8), 8)
            pairs = [(staging[0, place, :LANES], None)]
            for k in range(1, slots):
                real, imag = staging[k, place, :LANES], staging[k, place, LANES:]
                cosine, sine = turn_cos[k:k + 1, :], turn_sin[k:k + 1, :]
                pairs.append((real * cosine - imag * sine, real * sine + imag * cosine))
            pairs.append((staging[0, place, LANES:], None))
            for n, value in enumerate(real_inverse(pairs)):
                solved[chunk, own, n, inner, :] = value
            return carry

        lax.fori_loop(0, levels * tiles, tile_step, 0)
        own_copy(chunk).start()
        for index, (begin, count) in enumerate(back_groups):
            @pl.when(chunk == begin + count - 1)
            def _():
                for step in range(1, peers):
                    back_copy(index, step).start()

    lag_down = planes - 1 - plane
    lag = jnp.maximum(plane, lag_down)

    def step(now, carry):
        @pl.when(now < chunks)
        def _():
            coefficients(now)

            @pl.when(now % batch == 0)
            def _():
                all_blocks(send_box, now, batch, go_recv.at[now // batch])

            stream_forward(now)

        @pl.when(jnp.logical_and(now >= plane, now < plane + chunks))
        def _():
            sweep_up(now - plane)

        @pl.when(jnp.logical_and(now >= lag_down, now < lag_down + chunks))
        def _():
            sweep_down(now - lag_down)

        @pl.when(jnp.logical_and(now >= lag, now < lag + chunks))
        def _():
            finish(now - lag)

        return carry

    lax.fori_loop(0, chunks + planes - 1, step, 0)

    for index, (begin, count) in enumerate(back_groups):
        all_blocks(send_box, begin, count, back_recv.at[index])

    def drain(chunk, carry):
        own_copy(chunk).wait()

        @pl.when(plane < planes - 1)
        def _():
            up_copy(chunk).wait_send()

        @pl.when(plane > 0)
        def _():
            down_copy(chunk).wait_send()

        return carry

    lax.fori_loop(0, chunks, drain, 0)
    for turn in range(chunks // batch):
        all_blocks(send_box, turn * batch, batch, go_send.at[turn])
    for index, (begin, count) in enumerate(back_groups):
        all_blocks(send_box, begin, count, back_send.at[index])


def last_product(returned, span_high, span_low, out):
    span, width = out.shape[1], out.shape[2] // LANES
    pieces = [returned[:, :, part].reshape(span, LANES) for part in range(width)]
    right = split_value(jnp.concatenate(pieces, axis=1) if width > 1 else pieces[0])
    out[0] = dot3((span_high[...], span_low[...]), right)


def local(mesh_shape, source_field, coupling, spacing):
    gx_count, gz_count = mesh_shape["gx"], mesh_shape["gz"]
    own, span, part = source_field.shape
    assert own == 1
    group = gz_count // 4 if gz_count % 4 == 0 else 1
    planes = gz_count // group
    levels = group
    peers = gx_count * group
    stream = part * gx_count
    share = span // peers
    chunks = 8
    while share % (8 * chunks):
        chunks //= 2
    rows = share // chunks
    batch = 2 if chunks % 2 == 0 and peers * rows < 128 else 1
    paired = max(0, chunks - 2) // 2 * 2
    back_groups = [(begin, 2) for begin in range(0, paired, 2)] + [(begin, 1) for begin in range(paired, chunks)]
    blocks = part // LANES
    outer = stream // LANES
    slots = outer // 2
    tables = make_tables(span, stream, rows)
    f32 = jnp.float32
    wide = (slots, rows, 2 * LANES)
    dma = pltpu.SemaphoreType.DMA
    vmem = pl.BlockSpec(memory_space=pltpu.VMEM)
    smem = pl.BlockSpec(memory_space=pltpu.SMEM)
    cfg = (gx_count, group, planes, chunks, rows, levels, batch, back_groups)
    box = (chunks, peers, blocks, rows, LANES)
    tables = [jnp.asarray(table) for table in tables]
    returned = pl.pallas_call(
        functools.partial(kernel, cfg),
        out_shape=jax.ShapeDtypeStruct(box, f32),
        in_specs=[smem, smem] + [vmem] * 11,
        out_specs=pl.BlockSpec(memory_space=pl.ANY),
        scratch_shapes=[
            pltpu.VMEM((span, part), jnp.bfloat16),
            pltpu.VMEM((span, part), jnp.bfloat16),
            pltpu.VMEM((chunks, peers, blocks, rows, LANES), f32),
            pltpu.VMEM((chunks, levels, outer, rows, LANES), f32),
            pltpu.VMEM((slots, levels * rows, 2 * LANES), f32),
            pltpu.VMEM((chunks, slots, levels, rows, 2 * LANES), f32),
            pltpu.VMEM((chunks, levels) + wide, f32),
            pltpu.VMEM((chunks, levels) + wide, f32),
            pltpu.VMEM((chunks,) + wide, f32),
            pltpu.VMEM((chunks, levels) + wide, f32),
            pltpu.VMEM((chunks,) + wide, f32),
            pltpu.VMEM((chunks,) + wide, f32),
            pltpu.VMEM((chunks,) + wide, f32),
            pltpu.VMEM((chunks, levels, outer, rows, LANES), f32),
            dma((chunks // batch,)), dma((chunks // batch,)),
            dma((chunks,)), dma((chunks,)), dma((chunks,)), dma((chunks,)),
            dma((len(back_groups),)), dma((len(back_groups),)), dma((chunks,)),
        ],
        compiler_params=pltpu.CompilerParams(
            collective_id=0, has_side_effects=True, vmem_limit_bytes=56 * 1024 * 1024),
        cost_estimate=pl.CostEstimate(flops=8 * 10**9, bytes_accessed=8 * 2**20, transcendentals=0),
    )(coupling, spacing, source_field, *tables)
    width = min(2, blocks)
    return pl.pallas_call(
        last_product,
        grid=(blocks // width,),
        out_shape=jax.ShapeDtypeStruct(source_field.shape, f32),
        in_specs=[
            pl.BlockSpec((chunks, peers, width, rows, LANES), lambda index: (0, 0, index, 0, 0)),
            pl.BlockSpec((span, span), lambda index: (0, 0)),
            pl.BlockSpec((span, span), lambda index: (0, 0)),
        ],
        out_specs=pl.BlockSpec((1, span, width * LANES), lambda index: (0, 0, index)),
        compiler_params=pltpu.CompilerParams(vmem_limit_bytes=32 * 1024 * 1024),
        cost_estimate=pl.CostEstimate(flops=2 * 10**9, bytes_accessed=5 * 2**20, transcendentals=0),
    )(returned, tables[0], tables[1])


def solution(mesh):
    in_specs = (P("gz", None, "gx"), P(), P())
    out_specs = P("gz", None, "gx")
    return jax.shard_map(
        functools.partial(local, dict(mesh.shape)), mesh=mesh,
        in_specs=in_specs, out_specs=out_specs, check_vma=False)
```

```python
import functools
import math

import jax
import jax.numpy as jnp
import ml_dtypes
import numpy as np
from jax import lax
from jax.experimental import pallas as pl
from jax.experimental.pallas import tpu as pltpu
from jax.sharding import PartitionSpec as P

LANES = 128
MESH = pl.DeviceIdType.MESH


def cos_sin(product, period):
    angles = (product % period).astype(np.float64) * (2.0 * math.pi / period)
    return np.cos(angles), np.sin(angles)


def split_table(table):
    high = table.astype(np.float32).astype(ml_dtypes.bfloat16)
    low = (table - high.astype(np.float64)).astype(np.float32).astype(ml_dtypes.bfloat16)
    return high, low


def make_tables(span, stream, rows):
    outer = stream // LANES
    slots = outer // 2
    ks = np.arange(span)
    cosine, sine = cos_sin(ks[:, None] * ks[None, :], span)
    span_high, span_low = split_table(cosine + sine)
    lane = np.arange(LANES)
    cosine, sine = cos_sin(lane[:, None] * lane[None, :], LANES)
    regular = np.block([[cosine, -sine], [sine, cosine]])
    half_cos, half_sin = cos_sin(lane[:, None] * (slots + outer * lane[None, :]), stream)
    zeros = np.zeros((LANES, LANES))
    special = np.block([[cosine + sine, zeros], [zeros, half_cos + half_sin]])
    forward = np.stack([special, regular])
    inverse = np.stack([special.T, regular.T]) / (span * stream)
    forward_high, forward_low = split_table(forward)
    inverse_high, inverse_low = split_table(inverse)
    turn_cos, turn_sin = cos_sin(np.arange(slots)[:, None] * lane[None, :], stream)
    wave = np.arange(slots + 1)[:, None] + outer * lane[None, :]
    eigen_stream = 2.0 - 2.0 * cos_sin(wave, stream)[0]
    eigen_stream = np.ascontiguousarray(np.broadcast_to(eigen_stream[:, None, :], (slots + 1, rows, LANES)))
    eigen_span = 2.0 - 2.0 * cos_sin(ks, span)[0]
    eigen_span = np.broadcast_to(eigen_span[:, None], (span, LANES)).reshape(span // rows, rows, LANES)
    return (
        span_high, span_low, forward_high, forward_low, inverse_high, inverse_low,
        turn_cos.astype(np.float32), turn_sin.astype(np.float32),
        eigen_stream.astype(np.float32), np.ascontiguousarray(eigen_span).astype(np.float32),
    )


def real_transform(values):
    count = len(values)
    if count == 2:
        return [(values[0] + values[1], None), (values[0] - values[1], None)]
    even = real_transform(values[0::2])
    odd = real_transform(values[1::2])
    result = [None] * (count // 2 + 1)
    quarter = count // 4
    result[0] = (even[0][0] + odd[0][0], None)
    result[count // 2] = (even[0][0] - odd[0][0], None)
    result[quarter] = (even[quarter][0], -odd[quarter][0])
    for k in range(1, quarter):
        angle = 2.0 * math.pi * k / count
        cosine, sine = math.cos(angle), math.sin(angle)
        odd_real, odd_imag = odd[k]
        turned_real = odd_real * cosine + odd_imag * sine
        turned_imag = odd_imag * cosine - odd_real * sine
        even_real, even_imag = even[k]
        result[k] = (even_real + turned_real, even_imag + turned_imag)
        result[count // 2 - k] = (even_real - turned_real, turned_imag - even_imag)
    return result


def real_inverse(pairs):
    count = 2 * (len(pairs) - 1)
    if count == 2:
        return [pairs[0][0] + pairs[1][0], pairs[0][0] - pairs[1][0]]
    quarter = count // 4
    even, odd = [None] * (quarter + 1), [None] * (quarter + 1)
    even[0] = (pairs[0][0] + pairs[count // 2][0], None)
    odd[0] = (pairs[0][0] - pairs[count // 2][0], None)
    even[quarter] = (2.0 * pairs[quarter][0], None)
    odd[quarter] = (-2.0 * pairs[quarter][1], None)
    for k in range(1, quarter):
        angle = 2.0 * math.pi * k / count
        cosine, sine = math.cos(angle), math.sin(angle)
        low_real, low_imag = pairs[k]
        high_real, high_imag = pairs[count // 2 - k]
        even[k] = (low_real + high_real, low_imag - high_imag)
        diff_real, diff_imag = low_real - high_real, low_imag + high_imag
        odd[k] = (diff_real * cosine - diff_imag * sine, diff_imag * cosine + diff_real * sine)
    even_values, odd_values = real_inverse(even), real_inverse(odd)
    return [(even_values if n % 2 == 0 else odd_values)[n // 2] for n in range(count)]


def split_value(value):
    high = value.astype(jnp.bfloat16)
    return high, (value - high.astype(jnp.float32)).astype(jnp.bfloat16)


def dot3(left, right):
    wide = jnp.concatenate([left[0], left[1], left[0]], axis=1)
    tall = jnp.concatenate([right[0], right[0], right[1]], axis=0)
    return jnp.dot(wide, tall, preferred_element_type=jnp.float32)


def inverse_of(value):
    guess = pl.reciprocal(value, approx=True)
    guess = guess * (2.0 - value * guess)
    return guess * (2.0 - value * guess)


def kernel(
    cfg, coupling, spacing, field, span_high, span_low, fwd_high, fwd_low, inv_high, inv_low,
    turn_cos, turn_sin, eig_stream, eig_span, returned,
    field_high, field_low, send_box, columns, staging, spectrum, pivots_low, pivots_high, middle,
    reduced, edge_down, from_below, from_above, solved,
    go_send, go_recv, up_send, up_recv, down_send, down_recv, back_send, back_recv, own_sem,
):
    gx_count, group, planes, chunks, rows, levels, batch, back_groups = cfg
    peers = gx_count * group
    blocks = field.shape[2] // LANES
    outer = blocks * gx_count
    slots = outer // 2
    level_count = levels * planes
    gx = lax.axis_index("gx")
    gz = lax.axis_index("gz")
    plane = gz // group
    row = gz % group
    me = gx * group + row
    first = plane * levels

    def partner(step):
        return (gx + step // group) % gx_count, (row + step % group) % group

    barrier = pltpu.get_barrier_semaphore()
    for step in range(1, peers):
        to_gx, to_row = partner(step)
        pl.semaphore_signal(barrier, inc=1, device_id=(to_gx, plane * group + to_row), device_id_type=MESH)

    @pl.when(plane > 0)
    def _():
        pl.semaphore_signal(barrier, inc=1, device_id=(gx, gz - group), device_id_type=MESH)

    @pl.when(plane < planes - 1)
    def _():
        pl.semaphore_signal(barrier, inc=1, device_id=(gx, gz + group), device_id_type=MESH)

    def go_copy(turn, step):
        to_gx, to_row = partner(step)
        here = pl.ds(turn * batch, batch)
        return pltpu.make_async_remote_copy(
            src_ref=send_box.at[here, to_gx * group + to_row],
            dst_ref=columns.at[here, row, pl.ds(gx * blocks, blocks)],
            send_sem=go_send.at[turn], recv_sem=go_recv.at[turn],
            device_id=(to_gx, plane * group + to_row), device_id_type=MESH)

    def back_copy(index, step):
        begin, count = back_groups[index]
        to_gx, to_row = partner(step)
        return pltpu.make_async_remote_copy(
            src_ref=solved.at[begin:begin + count, to_row, pl.ds(to_gx * blocks, blocks)],
            dst_ref=returned.at[begin:begin + count, me],
            send_sem=back_send.at[index], recv_sem=back_recv.at[index],
            device_id=(to_gx, plane * group + to_row), device_id_type=MESH)

    def own_copy(chunk):
        return pltpu.make_async_copy(
            solved.at[chunk, row, pl.ds(gx * blocks, blocks)], returned.at[chunk, me], own_sem.at[chunk])

    def all_blocks(box, begin, count, sem):
        blocks_here = box.at[pl.ds(begin, count), pl.ds(0, peers - 1)]
        pltpu.make_async_copy(blocks_here, blocks_here, sem).wait()

    part_slots = min(max(1, 32 // rows), slots)
    parts = slots // part_slots

    def up_copy(chunk, part):
        take = pl.ds(part * part_slots, part_slots)
        return pltpu.make_async_remote_copy(
            src_ref=reduced.at[chunk, levels - 1, take], dst_ref=from_below.at[chunk, take],
            send_sem=up_send.at[chunk, part], recv_sem=up_recv.at[chunk, part],
            device_id=(gx, (gz + group) % (planes * group)), device_id_type=MESH)

    def down_copy(chunk, part):
        take = pl.ds(part * part_slots, part_slots)
        return pltpu.make_async_remote_copy(
            src_ref=edge_down.at[chunk, take], dst_ref=from_above.at[chunk, take],
            send_sem=down_send.at[chunk, part], recv_sem=down_recv.at[chunk, part],
            device_id=(gx, (gz + planes * group - group) % (planes * group)), device_id_type=MESH)

    def below(level):
        return coupling[level]

    def above(level):
        return jnp.where(level + 1 < level_count, coupling[jnp.minimum(level + 1, level_count - 1)], 0.0)

    field_high[...], field_low[...] = split_value(field[0])

    def span_step(turn, carry):
        height = batch * peers * rows
        take = pl.ds(pl.multiple_of(turn * height, height), height)
        left = (span_high[take, :], span_low[take, :])
        width = min(2, blocks)
        for block in range(0, blocks, width):
            cols = slice(block * LANES, (block + width) * LANES)
            modes = dot3(left, (field_high[:, cols], field_low[:, cols]))
            for part in range(width):
                piece = modes[:, part * LANES:(part + 1) * LANES]
                piece = piece.reshape(batch, peers, rows, LANES)
                send_box[pl.ds(turn * batch, batch), :, block + part] = piece

        @pl.when(turn == 0)
        def _():
            expected = peers - 1 + jnp.where(plane > 0, 1, 0) + jnp.where(plane < planes - 1, 1, 0)
            pl.semaphore_wait(barrier, expected)

        for step in range(1, peers):
            go_copy(turn, step).start()
        for index in range(batch):
            chunk = turn * batch + index
            columns[chunk, row, pl.ds(gx * blocks, blocks)] = send_box[chunk, me]
        return carry

    lax.fori_loop(0, chunks // batch, span_step, 0)

    def coefficients(chunk):
        def store(target, begin, value):
            count = value.shape[0]
            low, high = (1 if begin == 0 else 0), (count - 1 if begin + count == slots + 1 else count)
            if low:
                target[0, :, :LANES] = value[0]
            if high < count:
                target[0, :, LANES:] = value[high]
            target[begin + low:begin + high, :, :LANES] = value[low:high]
            target[begin + low:begin + high, :, LANES:] = value[low:high]

        middle_unit = slots // 2 + 1
        for begin, end in ((0, middle_unit), (middle_unit, slots + 1)):
            lam = eig_span[chunk * peers + me][None] + eig_stream[begin:end]

            def diagonal(level):
                return lam * spacing[level] + (below(level) + above(level))

            def from_ground(level, pair):
                now, before = pair
                return diagonal(level) * now - (below(level) * below(level)) * before, now

            def from_top(count, pair):
                level = level_count - 1 - count
                now, before = pair
                return diagonal(level) * now - (above(level) * above(level)) * before, now

            nought = lam * 0.0
            start = (nought + 1.0, nought)
            low = lax.fori_loop(0, first, from_ground, start)
            for own in range(levels):
                after = from_ground(first + own, low)
                store(pivots_low.at[chunk, own], begin, low[0] * inverse_of(after[0]))
                low = after
            top = lax.fori_loop(0, level_count - first - levels, from_top, start)
            edge = above(first + levels - 1)
            both = low[0] * top[0]
            store(middle.at[chunk], begin, both * inverse_of(both - (edge * edge) * (low[1] * top[1])))
            for own in reversed(range(levels)):
                after = from_top(level_count - 1 - first - own, top)
                store(pivots_high.at[chunk, own], begin, top[0] * inverse_of(after[0]))
                top = after

    tiles = rows // 8

    def stream_forward(chunk):
        def tile_step(index, carry):
            own, tile = index // tiles, index % tiles
            inner = pl.ds(pl.multiple_of(tile * 8, 8), 8)
            place = pl.ds(pl.multiple_of(own * rows + tile * 8, 8), 8)
            pairs = real_transform([columns[chunk, own, n, inner, :] for n in range(outer)])
            staging[0, place, :LANES] = pairs[0][0]
            staging[0, place, LANES:] = pairs[slots][0]
            for k in range(1, slots):
                real, imag = pairs[k]
                cosine, sine = turn_cos[k:k + 1, :], turn_sin[k:k + 1, :]
                staging[k, place, :LANES] = real * cosine + imag * sine
                staging[k, place, LANES:] = imag * cosine - real * sine
            return carry

        lax.fori_loop(0, levels * tiles, tile_step, 0)
        special = dot3(split_value(staging[0]), (fwd_high[0], fwd_low[0]))
        spectrum[chunk, 0] = special.reshape(levels, rows, 2 * LANES)
        rest = staging[1:].reshape((slots - 1) * levels * rows, 2 * LANES)
        regular = dot3(split_value(rest), (fwd_high[1], fwd_low[1]))
        spectrum[chunk, 1:] = regular.reshape(slots - 1, levels, rows, 2 * LANES)

    def sweep_up(chunk):
        @pl.when(plane == 0)
        def _():
            from_below[chunk] = jnp.zeros(from_below.shape[1:], jnp.float32)

        for part in range(parts):
            @pl.when(plane > 0)
            def _():
                up_copy(chunk, part).wait_recv()

            take = pl.ds(part * part_slots, part_slots)
            value = from_below[chunk, take]
            for own in range(levels):
                level = first + own
                value = (spacing[level] * spectrum[chunk, take, own] + below(level) * value) * pivots_low[chunk, own, take]
                reduced[chunk, own, take] = value

            @pl.when(plane < planes - 1)
            def _():
                up_copy(chunk, part).start()

    def sweep_down(chunk):
        @pl.when(plane == planes - 1)
        def _():
            from_above[chunk] = jnp.zeros(from_above.shape[1:], jnp.float32)

        for part in range(parts):
            @pl.when(plane < planes - 1)
            def _():
                down_copy(chunk, part).wait_recv()

            @pl.when(plane > 0)
            def _():
                take = pl.ds(part * part_slots, part_slots)
                value = from_above[chunk, take]
                for own in reversed(range(levels)):
                    level = first + own
                    value = (spacing[level] * spectrum[chunk, take, own] + above(level) * value) * pivots_high[chunk, own, take]
                edge_down[chunk, take] = value
                down_copy(chunk, part).start()

    def finish(chunk):
        def part_step(part, carry):
            take = pl.ds(part * part_slots, part_slots)
            value = from_above[chunk, take]
            for own in reversed(range(levels)):
                value = reduced[chunk, own, take] + above(first + own) * pivots_low[chunk, own, take] * value
                if own == levels - 1:
                    value = value * middle[chunk, take]
                staging[take, own * rows:(own + 1) * rows, :] = value
            return carry

        lax.fori_loop(0, parts, part_step, 0)
        special = dot3(split_value(staging[0]), (inv_high[0], inv_low[0]))
        rest = staging[1:].reshape((slots - 1) * levels * rows, 2 * LANES)
        regular = dot3(split_value(rest), (inv_high[1], inv_low[1]))
        staging[0] = special
        staging[1:] = regular.reshape(slots - 1, levels * rows, 2 * LANES)

        def tile_step(index, carry):
            own, tile = index // tiles, index % tiles
            inner = pl.ds(pl.multiple_of(tile * 8, 8), 8)
            place = pl.ds(pl.multiple_of(own * rows + tile * 8, 8), 8)
            pairs = [(staging[0, place, :LANES], None)]
            for k in range(1, slots):
                real, imag = staging[k, place, :LANES], staging[k, place, LANES:]
                cosine, sine = turn_cos[k:k + 1, :], turn_sin[k:k + 1, :]
                pairs.append((real * cosine - imag * sine, real * sine + imag * cosine))
            pairs.append((staging[0, place, LANES:], None))
            for n, value in enumerate(real_inverse(pairs)):
                solved[chunk, own, n, inner, :] = value
            return carry

        lax.fori_loop(0, levels * tiles, tile_step, 0)
        own_copy(chunk).start()
        for index, (begin, count) in enumerate(back_groups):
            @pl.when(chunk == begin + count - 1)
            def _():
                for step in range(1, peers):
                    back_copy(index, step).start()

    lag_down = planes - 1 - plane
    lag = jnp.maximum(plane, lag_down)

    def step(now, carry):
        @pl.when(now < chunks)
        def _():
            coefficients(now)

            @pl.when(now % batch == 0)
            def _():
                all_blocks(send_box, now, batch, go_recv.at[now // batch])

            stream_forward(now)

        @pl.when(jnp.logical_and(now >= plane, now < plane + chunks))
        def _():
            sweep_up(now - plane)

        @pl.when(jnp.logical_and(now >= lag_down, now < lag_down + chunks))
        def _():
            sweep_down(now - lag_down)

        @pl.when(jnp.logical_and(now >= lag, now < lag + chunks))
        def _():
            finish(now - lag)

        return carry

    lax.fori_loop(0, chunks + planes - 1, step, 0)

    for index, (begin, count) in enumerate(back_groups):
        all_blocks(send_box, begin, count, back_recv.at[index])

    def drain(chunk, carry):
        own_copy(chunk).wait()

        for part in range(parts):
            @pl.when(plane < planes - 1)
            def _():
                up_copy(chunk, part).wait_send()

            @pl.when(plane > 0)
            def _():
                down_copy(chunk, part).wait_send()

        return carry

    lax.fori_loop(0, chunks, drain, 0)
    for turn in range(chunks // batch):
        all_blocks(send_box, turn * batch, batch, go_send.at[turn])
    for index, (begin, count) in enumerate(back_groups):
        all_blocks(send_box, begin, count, back_send.at[index])


def last_product(returned, span_high, span_low, out):
    span, width = out.shape[1], out.shape[2] // LANES
    pieces = [returned[:, :, part].reshape(span, LANES) for part in range(width)]
    right = split_value(jnp.concatenate(pieces, axis=1) if width > 1 else pieces[0])
    out[0] = dot3((span_high[...], span_low[...]), right)


def local(mesh_shape, source_field, coupling, spacing):
    gx_count, gz_count = mesh_shape["gx"], mesh_shape["gz"]
    own, span, part = source_field.shape
    assert own == 1
    group = gz_count // 4 if gz_count % 4 == 0 else 1
    planes = gz_count // group
    levels = group
    peers = gx_count * group
    stream = part * gx_count
    share = span // peers
    chunks = 8
    while share % (8 * chunks):
        chunks //= 2
    rows = share // chunks
    batch = 2 if chunks % 2 == 0 and peers * rows < 128 else 1
    paired = max(0, chunks - 2) // 2 * 2
    back_groups = [(begin, 2) for begin in range(0, paired, 2)] + [(begin, 1) for begin in range(paired, chunks)]
    blocks = part // LANES
    outer = stream // LANES
    slots = outer // 2
    tables = make_tables(span, stream, rows)
    f32 = jnp.float32
    wide = (slots, rows, 2 * LANES)
    parts = slots // min(max(1, 32 // rows), slots)
    dma = pltpu.SemaphoreType.DMA
    vmem = pl.BlockSpec(memory_space=pltpu.VMEM)
    smem = pl.BlockSpec(memory_space=pltpu.SMEM)
    cfg = (gx_count, group, planes, chunks, rows, levels, batch, back_groups)
    box = (chunks, peers, blocks, rows, LANES)
    tables = [jnp.asarray(table) for table in tables]
    returned = pl.pallas_call(
        functools.partial(kernel, cfg),
        out_shape=jax.ShapeDtypeStruct(box, f32),
        in_specs=[smem, smem] + [vmem] * 11,
        out_specs=pl.BlockSpec(memory_space=pl.ANY),
        scratch_shapes=[
            pltpu.VMEM((span, part), jnp.bfloat16),
            pltpu.VMEM((span, part), jnp.bfloat16),
            pltpu.VMEM((chunks, peers, blocks, rows, LANES), f32),
            pltpu.VMEM((chunks, levels, outer, rows, LANES), f32),
            pltpu.VMEM((slots, levels * rows, 2 * LANES), f32),
            pltpu.VMEM((chunks, slots, levels, rows, 2 * LANES), f32),
            pltpu.VMEM((chunks, levels) + wide, f32),
            pltpu.VMEM((chunks, levels) + wide, f32),
            pltpu.VMEM((chunks,) + wide, f32),
            pltpu.VMEM((chunks, levels) + wide, f32),
            pltpu.VMEM((chunks,) + wide, f32),
            pltpu.VMEM((chunks,) + wide, f32),
            pltpu.VMEM((chunks,) + wide, f32),
            pltpu.VMEM((chunks, levels, outer, rows, LANES), f32),
            dma((chunks // batch,)), dma((chunks // batch,)),
            *[dma((chunks, parts)) for _ in range(4)],
            dma((len(back_groups),)), dma((len(back_groups),)), dma((chunks,)),
        ],
        compiler_params=pltpu.CompilerParams(
            collective_id=0, has_side_effects=True, vmem_limit_bytes=56 * 1024 * 1024),
        cost_estimate=pl.CostEstimate(flops=8 * 10**9, bytes_accessed=8 * 2**20, transcendentals=0),
    )(coupling, spacing, source_field, *tables)
    width = min(2, blocks)
    return pl.pallas_call(
        last_product,
        grid=(blocks // width,),
        out_shape=jax.ShapeDtypeStruct(source_field.shape, f32),
        in_specs=[
            pl.BlockSpec((chunks, peers, width, rows, LANES), lambda index: (0, 0, index, 0, 0)),
            pl.BlockSpec((span, span), lambda index: (0, 0)),
            pl.BlockSpec((span, span), lambda index: (0, 0)),
        ],
        out_specs=pl.BlockSpec((1, span, width * LANES), lambda index: (0, 0, index)),
        compiler_params=pltpu.CompilerParams(vmem_limit_bytes=56 * 1024 * 1024),
        cost_estimate=pl.CostEstimate(flops=2 * 10**9, bytes_accessed=5 * 2**20, transcendentals=0),
    )(returned, tables[0], tables[1])


def solution(mesh):
    in_specs = (P("gz", None, "gx"), P(), P())
    out_specs = P("gz", None, "gx")
    return jax.shard_map(
        functools.partial(local, dict(mesh.shape)), mesh=mesh,
        in_specs=in_specs, out_specs=out_specs, check_vma=False)
```

```python
import functools
import math

import jax
import jax.numpy as jnp
import ml_dtypes
import numpy as np
from jax import lax
from jax.experimental import pallas as pl
from jax.experimental.pallas import tpu as pltpu
from jax.sharding import PartitionSpec as P

LANES = 128
MESH = pl.DeviceIdType.MESH


def cos_sin(product, period):
    angles = (product % period).astype(np.float64) * (2.0 * math.pi / period)
    return np.cos(angles), np.sin(angles)


def split_table(table):
    high = table.astype(np.float32).astype(ml_dtypes.bfloat16)
    low = (table - high.astype(np.float64)).astype(np.float32).astype(ml_dtypes.bfloat16)
    return high, low


def make_tables(span, stream, rows):
    outer = stream // LANES
    slots = outer // 2
    ks = np.arange(span)
    cosine, sine = cos_sin(ks[:, None] * ks[None, :], span)
    span_high, span_low = split_table(cosine + sine)
    lane = np.arange(LANES)
    cosine, sine = cos_sin(lane[:, None] * lane[None, :], LANES)
    regular = np.block([[cosine, -sine], [sine, cosine]])
    half_cos, half_sin = cos_sin(lane[:, None] * (slots + outer * lane[None, :]), stream)
    zeros = np.zeros((LANES, LANES))
    special = np.block([[cosine + sine, zeros], [zeros, half_cos + half_sin]])
    forward = np.stack([special, regular])
    inverse = np.stack([special.T, regular.T]) / (span * stream)
    forward_high, forward_low = split_table(forward)
    inverse_high, inverse_low = split_table(inverse)
    turn_cos, turn_sin = cos_sin(np.arange(slots)[:, None] * lane[None, :], stream)
    wave = np.arange(slots + 1)[:, None] + outer * lane[None, :]
    eigen_stream = 2.0 - 2.0 * cos_sin(wave, stream)[0]
    eigen_stream = np.ascontiguousarray(np.broadcast_to(eigen_stream[:, None, :], (slots + 1, rows, LANES)))
    eigen_span = 2.0 - 2.0 * cos_sin(ks, span)[0]
    eigen_span = np.broadcast_to(eigen_span[:, None], (span, LANES)).reshape(span // rows, rows, LANES)
    return (
        span_high, span_low, forward_high, forward_low, inverse_high, inverse_low,
        turn_cos.astype(np.float32), turn_sin.astype(np.float32),
        eigen_stream.astype(np.float32), np.ascontiguousarray(eigen_span).astype(np.float32),
    )


def real_transform(values):
    count = len(values)
    if count == 2:
        return [(values[0] + values[1], None), (values[0] - values[1], None)]
    even = real_transform(values[0::2])
    odd = real_transform(values[1::2])
    result = [None] * (count // 2 + 1)
    quarter = count // 4
    result[0] = (even[0][0] + odd[0][0], None)
    result[count // 2] = (even[0][0] - odd[0][0], None)
    result[quarter] = (even[quarter][0], -odd[quarter][0])
    for k in range(1, quarter):
        angle = 2.0 * math.pi * k / count
        cosine, sine = math.cos(angle), math.sin(angle)
        odd_real, odd_imag = odd[k]
        turned_real = odd_real * cosine + odd_imag * sine
        turned_imag = odd_imag * cosine - odd_real * sine
        even_real, even_imag = even[k]
        result[k] = (even_real + turned_real, even_imag + turned_imag)
        result[count // 2 - k] = (even_real - turned_real, turned_imag - even_imag)
    return result


def real_inverse(pairs):
    count = 2 * (len(pairs) - 1)
    if count == 2:
        return [pairs[0][0] + pairs[1][0], pairs[0][0] - pairs[1][0]]
    quarter = count // 4
    even, odd = [None] * (quarter + 1), [None] * (quarter + 1)
    even[0] = (pairs[0][0] + pairs[count // 2][0], None)
    odd[0] = (pairs[0][0] - pairs[count // 2][0], None)
    even[quarter] = (2.0 * pairs[quarter][0], None)
    odd[quarter] = (-2.0 * pairs[quarter][1], None)
    for k in range(1, quarter):
        angle = 2.0 * math.pi * k / count
        cosine, sine = math.cos(angle), math.sin(angle)
        low_real, low_imag = pairs[k]
        high_real, high_imag = pairs[count // 2 - k]
        even[k] = (low_real + high_real, low_imag - high_imag)
        diff_real, diff_imag = low_real - high_real, low_imag + high_imag
        odd[k] = (diff_real * cosine - diff_imag * sine, diff_imag * cosine + diff_real * sine)
    even_values, odd_values = real_inverse(even), real_inverse(odd)
    return [(even_values if n % 2 == 0 else odd_values)[n // 2] for n in range(count)]


def split_value(value):
    high = value.astype(jnp.bfloat16)
    return high, (value - high.astype(jnp.float32)).astype(jnp.bfloat16)


def dot3(left, right):
    wide = jnp.concatenate([left[0], left[1], left[0]], axis=1)
    tall = jnp.concatenate([right[0], right[0], right[1]], axis=0)
    return jnp.dot(wide, tall, preferred_element_type=jnp.float32)


def inverse_of(value):
    guess = pl.reciprocal(value, approx=True)
    guess = guess * (2.0 - value * guess)
    return guess * (2.0 - value * guess)


def kernel(
    cfg, coupling, spacing, field, span_high, span_low, fwd_high, fwd_low, inv_high, inv_low,
    turn_cos, turn_sin, eig_stream, eig_span, returned,
    field_high, field_low, send_box, columns, staging, spectrum, pivots_low, pivots_high, middle,
    reduced, edge_down, from_below, from_above, solved,
    go_send, go_recv, up_send, up_recv, down_send, down_recv, back_send, back_recv, own_sem,
):
    gx_count, group, planes, chunks, rows, levels, batch, back_groups = cfg
    peers = gx_count * group
    blocks = field.shape[2] // LANES
    outer = blocks * gx_count
    slots = outer // 2
    level_count = levels * planes
    gx = lax.axis_index("gx")
    gz = lax.axis_index("gz")
    plane = gz // group
    row = gz % group
    me = gx * group + row
    first = plane * levels

    def partner(step):
        return (gx + step // group) % gx_count, (row + step % group) % group

    barrier = pltpu.get_barrier_semaphore()
    for step in range(1, peers):
        to_gx, to_row = partner(step)
        pl.semaphore_signal(barrier, inc=1, device_id=(to_gx, plane * group + to_row), device_id_type=MESH)

    @pl.when(plane > 0)
    def _():
        pl.semaphore_signal(barrier, inc=1, device_id=(gx, gz - group), device_id_type=MESH)

    @pl.when(plane < planes - 1)
    def _():
        pl.semaphore_signal(barrier, inc=1, device_id=(gx, gz + group), device_id_type=MESH)

    def go_copy(chunk, step):
        to_gx, to_row = partner(step)
        return pltpu.make_async_remote_copy(
            src_ref=send_box.at[chunk, to_gx * group + to_row],
            dst_ref=columns.at[chunk, row, pl.ds(gx * blocks, blocks)],
            send_sem=go_send.at[chunk], recv_sem=go_recv.at[chunk],
            device_id=(to_gx, plane * group + to_row), device_id_type=MESH)

    def back_copy(index, step):
        begin, count = back_groups[index]
        to_gx, to_row = partner(step)
        return pltpu.make_async_remote_copy(
            src_ref=solved.at[begin:begin + count, to_row, pl.ds(to_gx * blocks, blocks)],
            dst_ref=returned.at[begin:begin + count, me],
            send_sem=back_send.at[index], recv_sem=back_recv.at[index],
            device_id=(to_gx, plane * group + to_row), device_id_type=MESH)

    def own_copy(chunk):
        return pltpu.make_async_copy(
            solved.at[chunk, row, pl.ds(gx * blocks, blocks)], returned.at[chunk, me], own_sem.at[chunk])

    def all_blocks(box, begin, count, sem):
        blocks_here = box.at[pl.ds(begin, count), pl.ds(0, peers - 1)]
        pltpu.make_async_copy(blocks_here, blocks_here, sem).wait()

    part_slots = min(max(1, 32 // rows), slots)
    parts = slots // part_slots

    def up_copy(chunk, part):
        take = pl.ds(part * part_slots, part_slots)
        return pltpu.make_async_remote_copy(
            src_ref=reduced.at[chunk, levels - 1, take], dst_ref=from_below.at[chunk, take],
            send_sem=up_send.at[chunk, part], recv_sem=up_recv.at[chunk, part],
            device_id=(gx, (gz + group) % (planes * group)), device_id_type=MESH)

    def down_copy(chunk, part):
        take = pl.ds(part * part_slots, part_slots)
        return pltpu.make_async_remote_copy(
            src_ref=edge_down.at[chunk, take], dst_ref=from_above.at[chunk, take],
            send_sem=down_send.at[chunk, part], recv_sem=down_recv.at[chunk, part],
            device_id=(gx, (gz + planes * group - group) % (planes * group)), device_id_type=MESH)

    def below(level):
        return coupling[level]

    def above(level):
        return jnp.where(level + 1 < level_count, coupling[jnp.minimum(level + 1, level_count - 1)], 0.0)

    field_high[...], field_low[...] = split_value(field[0])

    def span_step(turn, carry):
        height = batch * peers * rows
        take = pl.ds(pl.multiple_of(turn * height, height), height)
        left = (span_high[take, :], span_low[take, :])
        width = min(2, blocks)
        for block in range(0, blocks, width):
            cols = slice(block * LANES, (block + width) * LANES)
            modes = dot3(left, (field_high[:, cols], field_low[:, cols]))
            for part in range(width):
                piece = modes[:, part * LANES:(part + 1) * LANES]
                piece = piece.reshape(batch, peers, rows, LANES)
                send_box[pl.ds(turn * batch, batch), :, block + part] = piece

        @pl.when(turn == 0)
        def _():
            expected = peers - 1 + jnp.where(plane > 0, 1, 0) + jnp.where(plane < planes - 1, 1, 0)
            pl.semaphore_wait(barrier, expected)

        for index in range(batch):
            chunk = turn * batch + index
            for step in range(1, peers):
                go_copy(chunk, step).start()
            columns[chunk, row, pl.ds(gx * blocks, blocks)] = send_box[chunk, me]
        return carry

    lax.fori_loop(0, chunks // batch, span_step, 0)

    def coefficients(chunk):
        def store(target, begin, value):
            count = value.shape[0]
            low, high = (1 if begin == 0 else 0), (count - 1 if begin + count == slots + 1 else count)
            if low:
                target[0, :, :LANES] = value[0]
            if high < count:
                target[0, :, LANES:] = value[high]
            target[begin + low:begin + high, :, :LANES] = value[low:high]
            target[begin + low:begin + high, :, LANES:] = value[low:high]

        middle_unit = slots // 2 + 1
        for begin, end in ((0, middle_unit), (middle_unit, slots + 1)):
            lam = eig_span[chunk * peers + me][None] + eig_stream[begin:end]

            def diagonal(level):
                return lam * spacing[level] + (below(level) + above(level))

            def from_ground(level, pair):
                now, before = pair
                return diagonal(level) * now - (below(level) * below(level)) * before, now

            def from_top(count, pair):
                level = level_count - 1 - count
                now, before = pair
                return diagonal(level) * now - (above(level) * above(level)) * before, now

            nought = lam * 0.0
            start = (nought + 1.0, nought)
            low = lax.fori_loop(0, first, from_ground, start)
            for own in range(levels):
                after = from_ground(first + own, low)
                store(pivots_low.at[chunk, own], begin, low[0] * inverse_of(after[0]))
                low = after
            top = lax.fori_loop(0, level_count - first - levels, from_top, start)
            edge = above(first + levels - 1)
            both = low[0] * top[0]
            store(middle.at[chunk], begin, both * inverse_of(both - (edge * edge) * (low[1] * top[1])))
            for own in reversed(range(levels)):
                after = from_top(level_count - 1 - first - own, top)
                store(pivots_high.at[chunk, own], begin, top[0] * inverse_of(after[0]))
                top = after

    tiles = rows // 8

    def stream_forward(chunk):
        def tile_step(index, carry):
            own, tile = index // tiles, index % tiles
            inner = pl.ds(pl.multiple_of(tile * 8, 8), 8)
            place = pl.ds(pl.multiple_of(own * rows + tile * 8, 8), 8)
            pairs = real_transform([columns[chunk, own, n, inner, :] for n in range(outer)])
            staging[0, place, :LANES] = pairs[0][0]
            staging[0, place, LANES:] = pairs[slots][0]
            for k in range(1, slots):
                real, imag = pairs[k]
                cosine, sine = turn_cos[k:k + 1, :], turn_sin[k:k + 1, :]
                staging[k, place, :LANES] = real * cosine + imag * sine
                staging[k, place, LANES:] = imag * cosine - real * sine
            return carry

        lax.fori_loop(0, levels * tiles, tile_step, 0)
        special = dot3(split_value(staging[0]), (fwd_high[0], fwd_low[0]))
        spectrum[chunk, 0] = special.reshape(levels, rows, 2 * LANES)
        rest = staging[1:].reshape((slots - 1) * levels * rows, 2 * LANES)
        regular = dot3(split_value(rest), (fwd_high[1], fwd_low[1]))
        spectrum[chunk, 1:] = regular.reshape(slots - 1, levels, rows, 2 * LANES)

    def sweep_up(chunk):
        @pl.when(plane == 0)
        def _():
            from_below[chunk] = jnp.zeros(from_below.shape[1:], jnp.float32)

        for part in range(parts):
            @pl.when(plane > 0)
            def _():
                up_copy(chunk, part).wait_recv()

            take = pl.ds(part * part_slots, part_slots)
            value = from_below[chunk, take]
            for own in range(levels):
                level = first + own
                value = (spacing[level] * spectrum[chunk, take, own] + below(level) * value) * pivots_low[chunk, own, take]
                reduced[chunk, own, take] = value

            @pl.when(plane < planes - 1)
            def _():
                up_copy(chunk, part).start()

    def sweep_down(chunk):
        @pl.when(plane == planes - 1)
        def _():
            from_above[chunk] = jnp.zeros(from_above.shape[1:], jnp.float32)

        for part in range(parts):
            @pl.when(plane < planes - 1)
            def _():
                down_copy(chunk, part).wait_recv()

            @pl.when(plane > 0)
            def _():
                take = pl.ds(part * part_slots, part_slots)
                value = from_above[chunk, take]
                for own in reversed(range(levels)):
                    level = first + own
                    value = (spacing[level] * spectrum[chunk, take, own] + above(level) * value) * pivots_high[chunk, own, take]
                edge_down[chunk, take] = value
                down_copy(chunk, part).start()

    def finish(chunk):
        def part_step(part, carry):
            take = pl.ds(part * part_slots, part_slots)
            value = from_above[chunk, take]
            for own in reversed(range(levels)):
                value = reduced[chunk, own, take] + above(first + own) * pivots_low[chunk, own, take] * value
                if own == levels - 1:
                    value = value * middle[chunk, take]
                staging[take, own * rows:(own + 1) * rows, :] = value
            return carry

        lax.fori_loop(0, parts, part_step, 0)
        special = dot3(split_value(staging[0]), (inv_high[0], inv_low[0]))
        rest = staging[1:].reshape((slots - 1) * levels * rows, 2 * LANES)
        regular = dot3(split_value(rest), (inv_high[1], inv_low[1]))
        staging[0] = special
        staging[1:] = regular.reshape(slots - 1, levels * rows, 2 * LANES)

        def tile_step(index, carry):
            own, tile = index // tiles, index % tiles
            inner = pl.ds(pl.multiple_of(tile * 8, 8), 8)
            place = pl.ds(pl.multiple_of(own * rows + tile * 8, 8), 8)
            pairs = [(staging[0, place, :LANES], None)]
            for k in range(1, slots):
                real, imag = staging[k, place, :LANES], staging[k, place, LANES:]
                cosine, sine = turn_cos[k:k + 1, :], turn_sin[k:k + 1, :]
                pairs.append((real * cosine - imag * sine, real * sine + imag * cosine))
            pairs.append((staging[0, place, LANES:], None))
            for n, value in enumerate(real_inverse(pairs)):
                solved[chunk, own, n, inner, :] = value
            return carry

        lax.fori_loop(0, levels * tiles, tile_step, 0)
        own_copy(chunk).start()
        for index, (begin, count) in enumerate(back_groups):
            @pl.when(chunk == begin + count - 1)
            def _():
                for step in range(1, peers):
                    back_copy(index, step).start()

    lag_down = planes - 1 - plane
    lag = jnp.maximum(plane, lag_down)

    def step(now, carry):
        @pl.when(now < chunks)
        def _():
            coefficients(now)
            all_blocks(send_box, now, 1, go_recv.at[now])
            stream_forward(now)

        @pl.when(jnp.logical_and(now >= plane, now < plane + chunks))
        def _():
            sweep_up(now - plane)

        @pl.when(jnp.logical_and(now >= lag_down, now < lag_down + chunks))
        def _():
            sweep_down(now - lag_down)

        @pl.when(jnp.logical_and(now >= lag, now < lag + chunks))
        def _():
            finish(now - lag)

        return carry

    lax.fori_loop(0, chunks + planes - 1, step, 0)

    for index, (begin, count) in enumerate(back_groups):
        all_blocks(send_box, begin, count, back_recv.at[index])

    def drain(chunk, carry):
        own_copy(chunk).wait()

        for part in range(parts):
            @pl.when(plane < planes - 1)
            def _():
                up_copy(chunk, part).wait_send()

            @pl.when(plane > 0)
            def _():
                down_copy(chunk, part).wait_send()

        return carry

    lax.fori_loop(0, chunks, drain, 0)
    for chunk in range(chunks):
        all_blocks(send_box, chunk, 1, go_send.at[chunk])
    for index, (begin, count) in enumerate(back_groups):
        all_blocks(send_box, begin, count, back_send.at[index])


def last_product(returned, span_high, span_low, out):
    span, width = out.shape[1], out.shape[2] // LANES
    pieces = [returned[:, :, part].reshape(span, LANES) for part in range(width)]
    right = split_value(jnp.concatenate(pieces, axis=1) if width > 1 else pieces[0])
    out[0] = dot3((span_high[...], span_low[...]), right)


def local(mesh_shape, source_field, coupling, spacing):
    gx_count, gz_count = mesh_shape["gx"], mesh_shape["gz"]
    own, span, part = source_field.shape
    assert own == 1
    group = gz_count // 4 if gz_count % 4 == 0 else 1
    planes = gz_count // group
    levels = group
    peers = gx_count * group
    stream = part * gx_count
    share = span // peers
    chunks = 8
    while share % (8 * chunks):
        chunks //= 2
    rows = share // chunks
    batch = 2 if chunks % 2 == 0 and peers * rows < 128 else 1
    back_groups = [(begin, 1) for begin in range(chunks)]
    blocks = part // LANES
    outer = stream // LANES
    slots = outer // 2
    tables = make_tables(span, stream, rows)
    f32 = jnp.float32
    wide = (slots, rows, 2 * LANES)
    parts = slots // min(max(1, 32 // rows), slots)
    dma = pltpu.SemaphoreType.DMA
    vmem = pl.BlockSpec(memory_space=pltpu.VMEM)
    smem = pl.BlockSpec(memory_space=pltpu.SMEM)
    cfg = (gx_count, group, planes, chunks, rows, levels, batch, back_groups)
    box = (chunks, peers, blocks, rows, LANES)
    tables = [jnp.asarray(table) for table in tables]
    returned = pl.pallas_call(
        functools.partial(kernel, cfg),
        out_shape=jax.ShapeDtypeStruct(box, f32),
        in_specs=[smem, smem] + [vmem] * 11,
        out_specs=pl.BlockSpec(memory_space=pl.ANY),
        scratch_shapes=[
            pltpu.VMEM((span, part), jnp.bfloat16),
            pltpu.VMEM((span, part), jnp.bfloat16),
            pltpu.VMEM((chunks, peers, blocks, rows, LANES), f32),
            pltpu.VMEM((chunks, levels, outer, rows, LANES), f32),
            pltpu.VMEM((slots, levels * rows, 2 * LANES), f32),
            pltpu.VMEM((chunks, slots, levels, rows, 2 * LANES), f32),
            pltpu.VMEM((chunks, levels) + wide, f32),
            pltpu.VMEM((chunks, levels) + wide, f32),
            pltpu.VMEM((chunks,) + wide, f32),
            pltpu.VMEM((chunks, levels) + wide, f32),
            pltpu.VMEM((chunks,) + wide, f32),
            pltpu.VMEM((chunks,) + wide, f32),
            pltpu.VMEM((chunks,) + wide, f32),
            pltpu.VMEM((chunks, levels, outer, rows, LANES), f32),
            dma((chunks,)), dma((chunks,)),
            *[dma((chunks, parts)) for _ in range(4)],
            dma((len(back_groups),)), dma((len(back_groups),)), dma((chunks,)),
        ],
        compiler_params=pltpu.CompilerParams(
            collective_id=0, has_side_effects=True, vmem_limit_bytes=56 * 1024 * 1024),
        cost_estimate=pl.CostEstimate(flops=8 * 10**9, bytes_accessed=8 * 2**20, transcendentals=0),
    )(coupling, spacing, source_field, *tables)
    width = min(2, blocks)
    return pl.pallas_call(
        last_product,
        grid=(blocks // width,),
        out_shape=jax.ShapeDtypeStruct(source_field.shape, f32),
        in_specs=[
            pl.BlockSpec((chunks, peers, width, rows, LANES), lambda index: (0, 0, index, 0, 0)),
            pl.BlockSpec((span, span), lambda index: (0, 0)),
            pl.BlockSpec((span, span), lambda index: (0, 0)),
        ],
        out_specs=pl.BlockSpec((1, span, width * LANES), lambda index: (0, 0, index)),
        compiler_params=pltpu.CompilerParams(vmem_limit_bytes=56 * 1024 * 1024),
        cost_estimate=pl.CostEstimate(flops=2 * 10**9, bytes_accessed=5 * 2**20, transcendentals=0),
    )(returned, tables[0], tables[1])


def solution(mesh):
    in_specs = (P("gz", None, "gx"), P(), P())
    out_specs = P("gz", None, "gx")
    return jax.shard_map(
        functools.partial(local, dict(mesh.shape)), mesh=mesh,
        in_specs=in_specs, out_specs=out_specs, check_vma=False)
```

```python
import functools
import math

import jax
import jax.numpy as jnp
import ml_dtypes
import numpy as np
from jax import lax
from jax.experimental import pallas as pl
from jax.experimental.pallas import tpu as pltpu
from jax.sharding import PartitionSpec as P

LANES = 128
MESH = pl.DeviceIdType.MESH


def cos_sin(product, period):
    angles = (product % period).astype(np.float64) * (2.0 * math.pi / period)
    return np.cos(angles), np.sin(angles)


def split_table(table):
    high = table.astype(np.float32).astype(ml_dtypes.bfloat16)
    low = (table - high.astype(np.float64)).astype(np.float32).astype(ml_dtypes.bfloat16)
    return high, low


def make_tables(span, stream, rows):
    outer = stream // LANES
    slots = outer // 2
    ks = np.arange(span)
    cosine, sine = cos_sin(ks[:, None] * ks[None, :], span)
    span_high, span_low = split_table(cosine + sine)
    lane = np.arange(LANES)
    cosine, sine = cos_sin(lane[:, None] * lane[None, :], LANES)
    regular = np.block([[cosine, -sine], [sine, cosine]])
    half_cos, half_sin = cos_sin(lane[:, None] * (slots + outer * lane[None, :]), stream)
    zeros = np.zeros((LANES, LANES))
    special = np.block([[cosine + sine, zeros], [zeros, half_cos + half_sin]])
    forward = np.stack([special, regular])
    inverse = np.stack([special.T, regular.T]) / (span * stream)
    forward_high, forward_low = split_table(forward)
    inverse_high, inverse_low = split_table(inverse)
    turn_cos, turn_sin = cos_sin(np.arange(slots)[:, None] * lane[None, :], stream)
    wave = np.arange(slots + 1)[:, None] + outer * lane[None, :]
    eigen_stream = 2.0 - 2.0 * cos_sin(wave, stream)[0]
    eigen_stream = np.ascontiguousarray(np.broadcast_to(eigen_stream[:, None, :], (slots + 1, rows, LANES)))
    eigen_span = 2.0 - 2.0 * cos_sin(ks, span)[0]
    eigen_span = np.broadcast_to(eigen_span[:, None], (span, LANES)).reshape(span // rows, rows, LANES)
    return (
        span_high, span_low, forward_high, forward_low, inverse_high, inverse_low,
        turn_cos.astype(np.float32), turn_sin.astype(np.float32),
        eigen_stream.astype(np.float32), np.ascontiguousarray(eigen_span).astype(np.float32),
    )


def real_transform(values):
    count = len(values)
    if count == 2:
        return [(values[0] + values[1], None), (values[0] - values[1], None)]
    even = real_transform(values[0::2])
    odd = real_transform(values[1::2])
    result = [None] * (count // 2 + 1)
    quarter = count // 4
    result[0] = (even[0][0] + odd[0][0], None)
    result[count // 2] = (even[0][0] - odd[0][0], None)
    result[quarter] = (even[quarter][0], -odd[quarter][0])
    for k in range(1, quarter):
        angle = 2.0 * math.pi * k / count
        cosine, sine = math.cos(angle), math.sin(angle)
        odd_real, odd_imag = odd[k]
        turned_real = odd_real * cosine + odd_imag * sine
        turned_imag = odd_imag * cosine - odd_real * sine
        even_real, even_imag = even[k]
        result[k] = (even_real + turned_real, even_imag + turned_imag)
        result[count // 2 - k] = (even_real - turned_real, turned_imag - even_imag)
    return result


def real_inverse(pairs):
    count = 2 * (len(pairs) - 1)
    if count == 2:
        return [pairs[0][0] + pairs[1][0], pairs[0][0] - pairs[1][0]]
    quarter = count // 4
    even, odd = [None] * (quarter + 1), [None] * (quarter + 1)
    even[0] = (pairs[0][0] + pairs[count // 2][0], None)
    odd[0] = (pairs[0][0] - pairs[count // 2][0], None)
    even[quarter] = (2.0 * pairs[quarter][0], None)
    odd[quarter] = (-2.0 * pairs[quarter][1], None)
    for k in range(1, quarter):
        angle = 2.0 * math.pi * k / count
        cosine, sine = math.cos(angle), math.sin(angle)
        low_real, low_imag = pairs[k]
        high_real, high_imag = pairs[count // 2 - k]
        even[k] = (low_real + high_real, low_imag - high_imag)
        diff_real, diff_imag = low_real - high_real, low_imag + high_imag
        odd[k] = (diff_real * cosine - diff_imag * sine, diff_imag * cosine + diff_real * sine)
    even_values, odd_values = real_inverse(even), real_inverse(odd)
    return [(even_values if n % 2 == 0 else odd_values)[n // 2] for n in range(count)]


def split_value(value):
    high = value.astype(jnp.bfloat16)
    return high, (value - high.astype(jnp.float32)).astype(jnp.bfloat16)


def dot3(left, right):
    wide = jnp.concatenate([left[0], left[1], left[0]], axis=1)
    tall = jnp.concatenate([right[0], right[0], right[1]], axis=0)
    return jnp.dot(wide, tall, preferred_element_type=jnp.float32)


def inverse_of(value):
    guess = pl.reciprocal(value, approx=True)
    guess = guess * (2.0 - value * guess)
    return guess * (2.0 - value * guess)


def kernel(
    cfg, coupling, spacing, field, span_high, span_low, fwd_high, fwd_low, inv_high, inv_low,
    turn_cos, turn_sin, eig_stream, eig_span, returned,
    field_high, field_low, send_box, columns, staging, spectrum, pivots_low, pivots_high, middle,
    reduced, edge_down, from_below, from_above, solved,
    go_send, go_recv, up_send, up_recv, down_send, down_recv, back_send, back_recv, own_sem,
):
    gx_count, group, planes, chunks, rows, levels, batch, back_groups = cfg
    peers = gx_count * group
    blocks = field.shape[2] // LANES
    outer = blocks * gx_count
    slots = outer // 2
    level_count = levels * planes
    gx = lax.axis_index("gx")
    gz = lax.axis_index("gz")
    plane = gz // group
    row = gz % group
    me = gx * group + row
    first = plane * levels

    def partner(step):
        return (gx + step // group) % gx_count, (row + step % group) % group

    barrier = pltpu.get_barrier_semaphore()
    for step in range(1, peers):
        to_gx, to_row = partner(step)
        pl.semaphore_signal(barrier, inc=1, device_id=(to_gx, plane * group + to_row), device_id_type=MESH)

    @pl.when(plane > 0)
    def _():
        pl.semaphore_signal(barrier, inc=1, device_id=(gx, gz - group), device_id_type=MESH)

    @pl.when(plane < planes - 1)
    def _():
        pl.semaphore_signal(barrier, inc=1, device_id=(gx, gz + group), device_id_type=MESH)

    def go_copy(chunk, step):
        to_gx, to_row = partner(step)
        return pltpu.make_async_remote_copy(
            src_ref=send_box.at[chunk, to_gx * group + to_row],
            dst_ref=columns.at[chunk, row, pl.ds(gx * blocks, blocks)],
            send_sem=go_send.at[chunk], recv_sem=go_recv.at[chunk],
            device_id=(to_gx, plane * group + to_row), device_id_type=MESH)

    def back_copy(index, step):
        begin, count = back_groups[index]
        to_gx, to_row = partner(step)
        return pltpu.make_async_remote_copy(
            src_ref=solved.at[begin:begin + count, to_row, pl.ds(to_gx * blocks, blocks)],
            dst_ref=returned.at[begin:begin + count, me],
            send_sem=back_send.at[index], recv_sem=back_recv.at[index],
            device_id=(to_gx, plane * group + to_row), device_id_type=MESH)

    def own_copy(chunk):
        return pltpu.make_async_copy(
            solved.at[chunk, row, pl.ds(gx * blocks, blocks)], returned.at[chunk, me], own_sem.at[chunk])

    def all_blocks(box, begin, count, sem):
        blocks_here = box.at[pl.ds(begin, count), pl.ds(0, peers - 1)]
        pltpu.make_async_copy(blocks_here, blocks_here, sem).wait()

    part_slots = min(max(1, 32 // rows), slots)
    parts = slots // part_slots

    def up_copy(chunk, part):
        take = pl.ds(part * part_slots, part_slots)
        return pltpu.make_async_remote_copy(
            src_ref=reduced.at[chunk, levels - 1, take], dst_ref=from_below.at[chunk, take],
            send_sem=up_send.at[chunk, part], recv_sem=up_recv.at[chunk, part],
            device_id=(gx, (gz + group) % (planes * group)), device_id_type=MESH)

    def down_copy(chunk, part):
        take = pl.ds(part * part_slots, part_slots)
        return pltpu.make_async_remote_copy(
            src_ref=edge_down.at[chunk, take], dst_ref=from_above.at[chunk, take],
            send_sem=down_send.at[chunk, part], recv_sem=down_recv.at[chunk, part],
            device_id=(gx, (gz + planes * group - group) % (planes * group)), device_id_type=MESH)

    def below(level):
        return coupling[level]

    def above(level):
        return jnp.where(level + 1 < level_count, coupling[jnp.minimum(level + 1, level_count - 1)], 0.0)

    field_high[...], field_low[...] = split_value(field[0])

    def span_step(turn, carry):
        height = batch * peers * rows
        take = pl.ds(pl.multiple_of(turn * height, height), height)
        left = (span_high[take, :], span_low[take, :])
        width = min(2, blocks)
        for block in range(0, blocks, width):
            cols = slice(block * LANES, (block + width) * LANES)
            modes = dot3(left, (field_high[:, cols], field_low[:, cols]))
            for part in range(width):
                piece = modes[:, part * LANES:(part + 1) * LANES]
                piece = piece.reshape(batch, peers, rows, LANES)
                send_box[pl.ds(turn * batch, batch), :, block + part] = piece

        @pl.when(turn == 0)
        def _():
            expected = peers - 1 + jnp.where(plane > 0, 1, 0) + jnp.where(plane < planes - 1, 1, 0)
            pl.semaphore_wait(barrier, expected)

        for index in range(batch):
            chunk = turn * batch + index
            for step in reversed(range(1, peers)):
                go_copy(chunk, step).start()
            columns[chunk, row, pl.ds(gx * blocks, blocks)] = send_box[chunk, me]
        return carry

    lax.fori_loop(0, chunks // batch, span_step, 0)

    def coefficients(chunk):
        def store(target, begin, value):
            count = value.shape[0]
            low, high = (1 if begin == 0 else 0), (count - 1 if begin + count == slots + 1 else count)
            if low:
                target[0, :, :LANES] = value[0]
            if high < count:
                target[0, :, LANES:] = value[high]
            target[begin + low:begin + high, :, :LANES] = value[low:high]
            target[begin + low:begin + high, :, LANES:] = value[low:high]

        middle_unit = slots // 2 + 1
        for begin, end in ((0, middle_unit), (middle_unit, slots + 1)):
            lam = eig_span[chunk * peers + me][None] + eig_stream[begin:end]

            def diagonal(level):
                return lam * spacing[level] + (below(level) + above(level))

            def from_ground(level, pair):
                now, before = pair
                return diagonal(level) * now - (below(level) * below(level)) * before, now

            def from_top(count, pair):
                level = level_count - 1 - count
                now, before = pair
                return diagonal(level) * now - (above(level) * above(level)) * before, now

            nought = lam * 0.0
            start = (nought + 1.0, nought)
            low = lax.fori_loop(0, first, from_ground, start)
            for own in range(levels):
                after = from_ground(first + own, low)
                store(pivots_low.at[chunk, own], begin, low[0] * inverse_of(after[0]))
                low = after
            top = lax.fori_loop(0, level_count - first - levels, from_top, start)
            edge = above(first + levels - 1)
            both = low[0] * top[0]
            store(middle.at[chunk], begin, both * inverse_of(both - (edge * edge) * (low[1] * top[1])))
            for own in reversed(range(levels)):
                after = from_top(level_count - 1 - first - own, top)
                store(pivots_high.at[chunk, own], begin, top[0] * inverse_of(after[0]))
                top = after

    tiles = rows // 8

    def stream_forward(chunk):
        def tile_step(index, carry):
            own, tile = index // tiles, index % tiles
            inner = pl.ds(pl.multiple_of(tile * 8, 8), 8)
            place = pl.ds(pl.multiple_of(own * rows + tile * 8, 8), 8)
            pairs = real_transform([columns[chunk, own, n, inner, :] for n in range(outer)])
            staging[0, place, :LANES] = pairs[0][0]
            staging[0, place, LANES:] = pairs[slots][0]
            for k in range(1, slots):
                real, imag = pairs[k]
                cosine, sine = turn_cos[k:k + 1, :], turn_sin[k:k + 1, :]
                staging[k, place, :LANES] = real * cosine + imag * sine
                staging[k, place, LANES:] = imag * cosine - real * sine
            return carry

        lax.fori_loop(0, levels * tiles, tile_step, 0)
        special = dot3(split_value(staging[0]), (fwd_high[0], fwd_low[0]))
        spectrum[chunk, 0] = special.reshape(levels, rows, 2 * LANES)
        rest = staging[1:].reshape((slots - 1) * levels * rows, 2 * LANES)
        regular = dot3(split_value(rest), (fwd_high[1], fwd_low[1]))
        spectrum[chunk, 1:] = regular.reshape(slots - 1, levels, rows, 2 * LANES)

    def sweep_up(chunk):
        @pl.when(plane == 0)
        def _():
            from_below[chunk] = jnp.zeros(from_below.shape[1:], jnp.float32)

        for part in range(parts):
            @pl.when(plane > 0)
            def _():
                up_copy(chunk, part).wait_recv()

            take = pl.ds(part * part_slots, part_slots)
            value = from_below[chunk, take]
            for own in range(levels):
                level = first + own
                value = (spacing[level] * spectrum[chunk, take, own] + below(level) * value) * pivots_low[chunk, own, take]
                reduced[chunk, own, take] = value

            @pl.when(plane < planes - 1)
            def _():
                up_copy(chunk, part).start()

    def sweep_down(chunk):
        @pl.when(plane == planes - 1)
        def _():
            from_above[chunk] = jnp.zeros(from_above.shape[1:], jnp.float32)

        for part in range(parts):
            @pl.when(plane < planes - 1)
            def _():
                down_copy(chunk, part).wait_recv()

            @pl.when(plane > 0)
            def _():
                take = pl.ds(part * part_slots, part_slots)
                value = from_above[chunk, take]
                for own in reversed(range(levels)):
                    level = first + own
                    value = (spacing[level] * spectrum[chunk, take, own] + above(level) * value) * pivots_high[chunk, own, take]
                edge_down[chunk, take] = value
                down_copy(chunk, part).start()

    def finish(chunk):
        def part_step(part, carry):
            take = pl.ds(part * part_slots, part_slots)
            value = from_above[chunk, take]
            for own in reversed(range(levels)):
                value = reduced[chunk, own, take] + above(first + own) * pivots_low[chunk, own, take] * value
                if own == levels - 1:
                    value = value * middle[chunk, take]
                staging[take, own * rows:(own + 1) * rows, :] = value
            return carry

        lax.fori_loop(0, parts, part_step, 0)
        special = dot3(split_value(staging[0]), (inv_high[0], inv_low[0]))
        rest = staging[1:].reshape((slots - 1) * levels * rows, 2 * LANES)
        regular = dot3(split_value(rest), (inv_high[1], inv_low[1]))
        staging[0] = special
        staging[1:] = regular.reshape(slots - 1, levels * rows, 2 * LANES)

        def tile_step(index, carry):
            own, tile = index // tiles, index % tiles
            inner = pl.ds(pl.multiple_of(tile * 8, 8), 8)
            place = pl.ds(pl.multiple_of(own * rows + tile * 8, 8), 8)
            pairs = [(staging[0, place, :LANES], None)]
            for k in range(1, slots):
                real, imag = staging[k, place, :LANES], staging[k, place, LANES:]
                cosine, sine = turn_cos[k:k + 1, :], turn_sin[k:k + 1, :]
                pairs.append((real * cosine - imag * sine, real * sine + imag * cosine))
            pairs.append((staging[0, place, LANES:], None))
            for n, value in enumerate(real_inverse(pairs)):
                solved[chunk, own, n, inner, :] = value
            return carry

        lax.fori_loop(0, levels * tiles, tile_step, 0)
        own_copy(chunk).start()
        for index, (begin, count) in enumerate(back_groups):
            @pl.when(chunk == begin + count - 1)
            def _():
                for step in reversed(range(1, peers)):
                    back_copy(index, step).start()

    lag_down = planes - 1 - plane
    lag = jnp.maximum(plane, lag_down)

    def step(now, carry):
        @pl.when(now < chunks)
        def _():
            coefficients(now)
            all_blocks(send_box, now, 1, go_recv.at[now])
            stream_forward(now)

        @pl.when(jnp.logical_and(now >= plane, now < plane + chunks))
        def _():
            sweep_up(now - plane)

        @pl.when(jnp.logical_and(now >= lag_down, now < lag_down + chunks))
        def _():
            sweep_down(now - lag_down)

        @pl.when(jnp.logical_and(now >= lag, now < lag + chunks))
        def _():
            finish(now - lag)

        return carry

    lax.fori_loop(0, chunks + planes - 1, step, 0)

    for index, (begin, count) in enumerate(back_groups):
        all_blocks(send_box, begin, count, back_recv.at[index])

    def drain(chunk, carry):
        own_copy(chunk).wait()

        for part in range(parts):
            @pl.when(plane < planes - 1)
            def _():
                up_copy(chunk, part).wait_send()

            @pl.when(plane > 0)
            def _():
                down_copy(chunk, part).wait_send()

        return carry

    lax.fori_loop(0, chunks, drain, 0)
    for chunk in range(chunks):
        all_blocks(send_box, chunk, 1, go_send.at[chunk])
    for index, (begin, count) in enumerate(back_groups):
        all_blocks(send_box, begin, count, back_send.at[index])


def last_product(returned, span_high, span_low, out):
    span, width = out.shape[1], out.shape[2] // LANES
    pieces = [returned[:, :, part].reshape(span, LANES) for part in range(width)]
    right = split_value(jnp.concatenate(pieces, axis=1) if width > 1 else pieces[0])
    out[0] = dot3((span_high[...], span_low[...]), right)


def local(mesh_shape, source_field, coupling, spacing):
    gx_count, gz_count = mesh_shape["gx"], mesh_shape["gz"]
    own, span, part = source_field.shape
    assert own == 1
    group = gz_count // 4 if gz_count % 4 == 0 else 1
    planes = gz_count // group
    levels = group
    peers = gx_count * group
    stream = part * gx_count
    share = span // peers
    chunks = 8
    while share % (8 * chunks):
        chunks //= 2
    rows = share // chunks
    batch = 2 if chunks % 2 == 0 and peers * rows < 128 else 1
    back_groups = [(begin, 1) for begin in range(chunks)]
    blocks = part // LANES
    outer = stream // LANES
    slots = outer // 2
    tables = make_tables(span, stream, rows)
    f32 = jnp.float32
    wide = (slots, rows, 2 * LANES)
    parts = slots // min(max(1, 32 // rows), slots)
    dma = pltpu.SemaphoreType.DMA
    vmem = pl.BlockSpec(memory_space=pltpu.VMEM)
    smem = pl.BlockSpec(memory_space=pltpu.SMEM)
    cfg = (gx_count, group, planes, chunks, rows, levels, batch, back_groups)
    box = (chunks, peers, blocks, rows, LANES)
    tables = [jnp.asarray(table) for table in tables]
    returned = pl.pallas_call(
        functools.partial(kernel, cfg),
        out_shape=jax.ShapeDtypeStruct(box, f32),
        in_specs=[smem, smem] + [vmem] * 11,
        out_specs=pl.BlockSpec(memory_space=pl.ANY),
        scratch_shapes=[
            pltpu.VMEM((span, part), jnp.bfloat16),
            pltpu.VMEM((span, part), jnp.bfloat16),
            pltpu.VMEM((chunks, peers, blocks, rows, LANES), f32),
            pltpu.VMEM((chunks, levels, outer, rows, LANES), f32),
            pltpu.VMEM((slots, levels * rows, 2 * LANES), f32),
            pltpu.VMEM((chunks, slots, levels, rows, 2 * LANES), f32),
            pltpu.VMEM((chunks, levels) + wide, f32),
            pltpu.VMEM((chunks, levels) + wide, f32),
            pltpu.VMEM((chunks,) + wide, f32),
            pltpu.VMEM((chunks, levels) + wide, f32),
            pltpu.VMEM((chunks,) + wide, f32),
            pltpu.VMEM((chunks,) + wide, f32),
            pltpu.VMEM((chunks,) + wide, f32),
            pltpu.VMEM((chunks, levels, outer, rows, LANES), f32),
            dma((chunks,)), dma((chunks,)),
            *[dma((chunks, parts)) for _ in range(4)],
            dma((len(back_groups),)), dma((len(back_groups),)), dma((chunks,)),
        ],
        compiler_params=pltpu.CompilerParams(
            collective_id=0, has_side_effects=True, vmem_limit_bytes=56 * 1024 * 1024),
        cost_estimate=pl.CostEstimate(flops=8 * 10**9, bytes_accessed=8 * 2**20, transcendentals=0),
    )(coupling, spacing, source_field, *tables)
    width = min(2, blocks)
    return pl.pallas_call(
        last_product,
        grid=(blocks // width,),
        out_shape=jax.ShapeDtypeStruct(source_field.shape, f32),
        in_specs=[
            pl.BlockSpec((chunks, peers, width, rows, LANES), lambda index: (0, 0, index, 0, 0)),
            pl.BlockSpec((span, span), lambda index: (0, 0)),
            pl.BlockSpec((span, span), lambda index: (0, 0)),
        ],
        out_specs=pl.BlockSpec((1, span, width * LANES), lambda index: (0, 0, index)),
        compiler_params=pltpu.CompilerParams(vmem_limit_bytes=56 * 1024 * 1024),
        cost_estimate=pl.CostEstimate(flops=2 * 10**9, bytes_accessed=5 * 2**20, transcendentals=0),
    )(returned, tables[0], tables[1])


def solution(mesh):
    in_specs = (P("gz", None, "gx"), P(), P())
    out_specs = P("gz", None, "gx")
    return jax.shard_map(
        functools.partial(local, dict(mesh.shape)), mesh=mesh,
        in_specs=in_specs, out_specs=out_specs, check_vma=False)
```

```python
import functools
import math

import jax
import jax.numpy as jnp
import ml_dtypes
import numpy as np
from jax import lax
from jax.experimental import pallas as pl
from jax.experimental.pallas import tpu as pltpu
from jax.sharding import PartitionSpec as P

LANES = 128
MESH = pl.DeviceIdType.MESH


def cos_sin(product, period):
    angles = (product % period).astype(np.float64) * (2.0 * math.pi / period)
    return np.cos(angles), np.sin(angles)


def split_table(table):
    high = table.astype(np.float32).astype(ml_dtypes.bfloat16)
    low = (table - high.astype(np.float64)).astype(np.float32).astype(ml_dtypes.bfloat16)
    return high, low


def make_tables(span, stream, rows):
    outer = stream // LANES
    slots = outer // 2
    ks = np.arange(span)
    cosine, sine = cos_sin(ks[:, None] * ks[None, :], span)
    span_high, span_low = split_table(cosine + sine)
    lane = np.arange(LANES)
    cosine, sine = cos_sin(lane[:, None] * lane[None, :], LANES)
    regular = np.block([[cosine, -sine], [sine, cosine]])
    half_cos, half_sin = cos_sin(lane[:, None] * (slots + outer * lane[None, :]), stream)
    zeros = np.zeros((LANES, LANES))
    special = np.block([[cosine + sine, zeros], [zeros, half_cos + half_sin]])
    forward = np.stack([special, regular])
    inverse = np.stack([special.T, regular.T]) / (span * stream)
    forward_high, forward_low = split_table(forward)
    inverse_high, inverse_low = split_table(inverse)
    turn_cos, turn_sin = cos_sin(np.arange(slots)[:, None] * lane[None, :], stream)
    wave = np.arange(slots + 1)[:, None] + outer * lane[None, :]
    eigen_stream = 2.0 - 2.0 * cos_sin(wave, stream)[0]
    eigen_stream = np.ascontiguousarray(np.broadcast_to(eigen_stream[:, None, :], (slots + 1, rows, LANES)))
    eigen_span = 2.0 - 2.0 * cos_sin(ks, span)[0]
    eigen_span = np.broadcast_to(eigen_span[:, None], (span, LANES)).reshape(span // rows, rows, LANES)
    return (
        span_high, span_low, forward_high, forward_low, inverse_high, inverse_low,
        turn_cos.astype(np.float32), turn_sin.astype(np.float32),
        eigen_stream.astype(np.float32), np.ascontiguousarray(eigen_span).astype(np.float32),
    )


def real_transform(values):
    count = len(values)
    if count == 2:
        return [(values[0] + values[1], None), (values[0] - values[1], None)]
    even = real_transform(values[0::2])
    odd = real_transform(values[1::2])
    result = [None] * (count // 2 + 1)
    quarter = count // 4
    result[0] = (even[0][0] + odd[0][0], None)
    result[count // 2] = (even[0][0] - odd[0][0], None)
    result[quarter] = (even[quarter][0], -odd[quarter][0])
    for k in range(1, quarter):
        angle = 2.0 * math.pi * k / count
        cosine, sine = math.cos(angle), math.sin(angle)
        odd_real, odd_imag = odd[k]
        turned_real = odd_real * cosine + odd_imag * sine
        turned_imag = odd_imag * cosine - odd_real * sine
        even_real, even_imag = even[k]
        result[k] = (even_real + turned_real, even_imag + turned_imag)
        result[count // 2 - k] = (even_real - turned_real, turned_imag - even_imag)
    return result


def real_inverse(pairs):
    count = 2 * (len(pairs) - 1)
    if count == 2:
        return [pairs[0][0] + pairs[1][0], pairs[0][0] - pairs[1][0]]
    quarter = count // 4
    even, odd = [None] * (quarter + 1), [None] * (quarter + 1)
    even[0] = (pairs[0][0] + pairs[count // 2][0], None)
    odd[0] = (pairs[0][0] - pairs[count // 2][0], None)
    even[quarter] = (2.0 * pairs[quarter][0], None)
    odd[quarter] = (-2.0 * pairs[quarter][1], None)
    for k in range(1, quarter):
        angle = 2.0 * math.pi * k / count
        cosine, sine = math.cos(angle), math.sin(angle)
        low_real, low_imag = pairs[k]
        high_real, high_imag = pairs[count // 2 - k]
        even[k] = (low_real + high_real, low_imag - high_imag)
        diff_real, diff_imag = low_real - high_real, low_imag + high_imag
        odd[k] = (diff_real * cosine - diff_imag * sine, diff_imag * cosine + diff_real * sine)
    even_values, odd_values = real_inverse(even), real_inverse(odd)
    return [(even_values if n % 2 == 0 else odd_values)[n // 2] for n in range(count)]


def split_value(value):
    high = value.astype(jnp.bfloat16)
    return high, (value - high.astype(jnp.float32)).astype(jnp.bfloat16)


def dot3(left, right):
    wide = jnp.concatenate([left[0], left[1], left[0]], axis=1)
    tall = jnp.concatenate([right[0], right[0], right[1]], axis=0)
    return jnp.dot(wide, tall, preferred_element_type=jnp.float32)


def inverse_of(value):
    guess = pl.reciprocal(value, approx=True)
    guess = guess * (2.0 - value * guess)
    return guess * (2.0 - value * guess)


def kernel(
    cfg, coupling, spacing, field, span_high, span_low, fwd_high, fwd_low, inv_high, inv_low,
    turn_cos, turn_sin, eig_stream, eig_span, returned,
    field_high, field_low, send_box, columns, staging, spectrum, pivots_low, pivots_high, middle,
    reduced, edge_down, from_below, from_above, solved,
    go_send, go_recv, up_send, up_recv, down_send, down_recv, back_send, back_recv, own_sem,
):
    gx_count, group, planes, chunks, rows, levels, batch, back_groups = cfg
    peers = gx_count * group
    blocks = field.shape[2] // LANES
    outer = blocks * gx_count
    slots = outer // 2
    level_count = levels * planes
    gx = lax.axis_index("gx")
    gz = lax.axis_index("gz")
    plane = gz // group
    row = gz % group
    me = gx * group + row
    first = plane * levels

    def partner(step):
        return (gx + step // group) % gx_count, (row + step % group) % group

    barrier = pltpu.get_barrier_semaphore()
    for step in range(1, peers):
        to_gx, to_row = partner(step)
        pl.semaphore_signal(barrier, inc=1, device_id=(to_gx, plane * group + to_row), device_id_type=MESH)

    @pl.when(plane > 0)
    def _():
        pl.semaphore_signal(barrier, inc=1, device_id=(gx, gz - group), device_id_type=MESH)

    @pl.when(plane < planes - 1)
    def _():
        pl.semaphore_signal(barrier, inc=1, device_id=(gx, gz + group), device_id_type=MESH)

    def go_copy(chunk, step):
        to_gx, to_row = partner(step)
        return pltpu.make_async_remote_copy(
            src_ref=send_box.at[chunk, to_gx * group + to_row],
            dst_ref=columns.at[chunk, row, pl.ds(gx * blocks, blocks)],
            send_sem=go_send.at[chunk], recv_sem=go_recv.at[chunk],
            device_id=(to_gx, plane * group + to_row), device_id_type=MESH)

    def back_copy(index, step):
        begin, count = back_groups[index]
        to_gx, to_row = partner(step)
        return pltpu.make_async_remote_copy(
            src_ref=solved.at[begin:begin + count, to_row, pl.ds(to_gx * blocks, blocks)],
            dst_ref=returned.at[begin:begin + count, me],
            send_sem=back_send.at[index], recv_sem=back_recv.at[index],
            device_id=(to_gx, plane * group + to_row), device_id_type=MESH)

    def own_copy(chunk):
        return pltpu.make_async_copy(
            solved.at[chunk, row, pl.ds(gx * blocks, blocks)], returned.at[chunk, me], own_sem.at[chunk])

    def all_blocks(box, begin, count, sem):
        blocks_here = box.at[pl.ds(begin, count), pl.ds(0, peers - 1)]
        pltpu.make_async_copy(blocks_here, blocks_here, sem).wait()

    part_slots = min(max(1, 32 // rows), slots)
    parts = slots // part_slots

    def up_copy(chunk, part):
        take = pl.ds(part * part_slots, part_slots)
        return pltpu.make_async_remote_copy(
            src_ref=reduced.at[chunk, levels - 1, take], dst_ref=from_below.at[chunk, take],
            send_sem=up_send.at[chunk, part], recv_sem=up_recv.at[chunk, part],
            device_id=(gx, (gz + group) % (planes * group)), device_id_type=MESH)

    def down_copy(chunk, part):
        take = pl.ds(part * part_slots, part_slots)
        return pltpu.make_async_remote_copy(
            src_ref=edge_down.at[chunk, take], dst_ref=from_above.at[chunk, take],
            send_sem=down_send.at[chunk, part], recv_sem=down_recv.at[chunk, part],
            device_id=(gx, (gz + planes * group - group) % (planes * group)), device_id_type=MESH)

    def below(level):
        return coupling[level]

    def above(level):
        return jnp.where(level + 1 < level_count, coupling[jnp.minimum(level + 1, level_count - 1)], 0.0)

    field_high[...], field_low[...] = split_value(field[0])

    def span_step(turn, carry):
        height = batch * peers * rows
        take = pl.ds(pl.multiple_of(turn * height, height), height)
        left = (span_high[take, :], span_low[take, :])
        width = min(2, blocks)
        for block in range(0, blocks, width):
            cols = slice(block * LANES, (block + width) * LANES)
            modes = dot3(left, (field_high[:, cols], field_low[:, cols]))
            for part in range(width):
                piece = modes[:, part * LANES:(part + 1) * LANES]
                piece = piece.reshape(batch, peers, rows, LANES)
                send_box[pl.ds(turn * batch, batch), :, block + part] = piece

        @pl.when(turn == 0)
        def _():
            expected = peers - 1 + jnp.where(plane > 0, 1, 0) + jnp.where(plane < planes - 1, 1, 0)
            pl.semaphore_wait(barrier, expected)

        for index in range(batch):
            chunk = turn * batch + index
            for step in range(1, peers):
                go_copy(chunk, step).start()
            columns[chunk, row, pl.ds(gx * blocks, blocks)] = send_box[chunk, me]
        return carry

    lax.fori_loop(0, chunks // batch, span_step, 0)

    def coefficients(chunk):
        def store(target, begin, value):
            count = value.shape[0]
            low, high = (1 if begin == 0 else 0), (count - 1 if begin + count == slots + 1 else count)
            if low:
                target[0, :, :LANES] = value[0]
            if high < count:
                target[0, :, LANES:] = value[high]
            target[begin + low:begin + high, :, :LANES] = value[low:high]
            target[begin + low:begin + high, :, LANES:] = value[low:high]

        middle_unit = slots // 2 + 1
        for begin, end in ((0, middle_unit), (middle_unit, slots + 1)):
            lam = eig_span[chunk * peers + me][None] + eig_stream[begin:end]

            def diagonal(level):
                return lam * spacing[level] + (below(level) + above(level))

            def from_ground(level, pair):
                now, before = pair
                return diagonal(level) * now - (below(level) * below(level)) * before, now

            def from_top(count, pair):
                level = level_count - 1 - count
                now, before = pair
                return diagonal(level) * now - (above(level) * above(level)) * before, now

            nought = lam * 0.0
            start = (nought + 1.0, nought)
            low = lax.fori_loop(0, first, from_ground, start)
            for own in range(levels):
                after = from_ground(first + own, low)
                store(pivots_low.at[chunk, own], begin, low[0] * inverse_of(after[0]))
                low = after
            top = lax.fori_loop(0, level_count - first - levels, from_top, start)
            edge = above(first + levels - 1)
            both = low[0] * top[0]
            store(middle.at[chunk], begin, both * inverse_of(both - (edge * edge) * (low[1] * top[1])))
            for own in reversed(range(levels)):
                after = from_top(level_count - 1 - first - own, top)
                store(pivots_high.at[chunk, own], begin, top[0] * inverse_of(after[0]))
                top = after

    tiles = rows // 8

    def stream_forward(chunk):
        def tile_step(index, carry):
            own, tile = index // tiles, index % tiles
            inner = pl.ds(pl.multiple_of(tile * 8, 8), 8)
            place = pl.ds(pl.multiple_of(own * rows + tile * 8, 8), 8)
            pairs = real_transform([columns[chunk, own, n, inner, :] for n in range(outer)])
            staging[0, place, :LANES] = pairs[0][0]
            staging[0, place, LANES:] = pairs[slots][0]
            for k in range(1, slots):
                real, imag = pairs[k]
                cosine, sine = turn_cos[k:k + 1, :], turn_sin[k:k + 1, :]
                staging[k, place, :LANES] = real * cosine + imag * sine
                staging[k, place, LANES:] = imag * cosine - real * sine
            return carry

        lax.fori_loop(0, levels * tiles, tile_step, 0)
        special = dot3(split_value(staging[0]), (fwd_high[0], fwd_low[0]))
        spectrum[chunk, 0] = special.reshape(levels, rows, 2 * LANES)
        rest = staging[1:].reshape((slots - 1) * levels * rows, 2 * LANES)
        regular = dot3(split_value(rest), (fwd_high[1], fwd_low[1]))
        spectrum[chunk, 1:] = regular.reshape(slots - 1, levels, rows, 2 * LANES)

    def sweep_up(chunk):
        @pl.when(plane == 0)
        def _():
            from_below[chunk] = jnp.zeros(from_below.shape[1:], jnp.float32)

        for part in range(parts):
            @pl.when(plane > 0)
            def _():
                up_copy(chunk, part).wait_recv()

            take = pl.ds(part * part_slots, part_slots)
            value = from_below[chunk, take]
            for own in range(levels):
                level = first + own
                value = (spacing[level] * spectrum[chunk, take, own] + below(level) * value) * pivots_low[chunk, own, take]
                reduced[chunk, own, take] = value

            @pl.when(plane < planes - 1)
            def _():
                up_copy(chunk, part).start()

    def sweep_down(chunk):
        @pl.when(plane == planes - 1)
        def _():
            from_above[chunk] = jnp.zeros(from_above.shape[1:], jnp.float32)

        for part in range(parts):
            @pl.when(plane < planes - 1)
            def _():
                down_copy(chunk, part).wait_recv()

            @pl.when(plane > 0)
            def _():
                take = pl.ds(part * part_slots, part_slots)
                value = from_above[chunk, take]
                for own in reversed(range(levels)):
                    level = first + own
                    value = (spacing[level] * spectrum[chunk, take, own] + above(level) * value) * pivots_high[chunk, own, take]
                edge_down[chunk, take] = value
                down_copy(chunk, part).start()

    def finish(chunk):
        def part_step(part, carry):
            take = pl.ds(part * part_slots, part_slots)
            value = from_above[chunk, take]
            for own in reversed(range(levels)):
                value = reduced[chunk, own, take] + above(first + own) * pivots_low[chunk, own, take] * value
                if own == levels - 1:
                    value = value * middle[chunk, take]
                staging[take, own * rows:(own + 1) * rows, :] = value
            return carry

        lax.fori_loop(0, parts, part_step, 0)
        special = dot3(split_value(staging[0]), (inv_high[0], inv_low[0]))
        rest = staging[1:].reshape((slots - 1) * levels * rows, 2 * LANES)
        regular = dot3(split_value(rest), (inv_high[1], inv_low[1]))
        staging[0] = special
        staging[1:] = regular.reshape(slots - 1, levels * rows, 2 * LANES)

        def tile_step(index, carry):
            own, tile = index // tiles, index % tiles
            inner = pl.ds(pl.multiple_of(tile * 8, 8), 8)
            place = pl.ds(pl.multiple_of(own * rows + tile * 8, 8), 8)
            pairs = [(staging[0, place, :LANES], None)]
            for k in range(1, slots):
                real, imag = staging[k, place, :LANES], staging[k, place, LANES:]
                cosine, sine = turn_cos[k:k + 1, :], turn_sin[k:k + 1, :]
                pairs.append((real * cosine - imag * sine, real * sine + imag * cosine))
            pairs.append((staging[0, place, LANES:], None))
            for n, value in enumerate(real_inverse(pairs)):
                solved[chunk, own, n, inner, :] = value
            return carry

        lax.fori_loop(0, levels * tiles, tile_step, 0)
        own_copy(chunk).start()
        for index, (begin, count) in enumerate(back_groups):
            @pl.when(chunk == begin + count - 1)
            def _():
                for step in range(1, peers):
                    back_copy(index, step).start()

    lag_down = planes - 1 - plane
    lag = jnp.maximum(plane, lag_down)

    def step(now, carry):
        @pl.when(now < chunks)
        def _():
            coefficients(now)
            all_blocks(send_box, now, 1, go_recv.at[now])
            stream_forward(now)

        @pl.when(jnp.logical_and(now >= plane, now < plane + chunks))
        def _():
            sweep_up(now - plane)

        @pl.when(jnp.logical_and(now >= lag_down, now < lag_down + chunks))
        def _():
            sweep_down(now - lag_down)

        @pl.when(jnp.logical_and(now >= lag, now < lag + chunks))
        def _():
            finish(now - lag)

        return carry

    lax.fori_loop(0, chunks + planes - 1, step, 0)

    for index, (begin, count) in enumerate(back_groups):
        all_blocks(send_box, begin, count, back_recv.at[index])

    def drain(chunk, carry):
        own_copy(chunk).wait()

        for part in range(parts):
            @pl.when(plane < planes - 1)
            def _():
                up_copy(chunk, part).wait_send()

            @pl.when(plane > 0)
            def _():
                down_copy(chunk, part).wait_send()

        return carry

    lax.fori_loop(0, chunks, drain, 0)
    for chunk in range(chunks):
        all_blocks(send_box, chunk, 1, go_send.at[chunk])
    for index, (begin, count) in enumerate(back_groups):
        all_blocks(send_box, begin, count, back_send.at[index])


def last_product(returned, span_high, span_low, out):
    span, width = out.shape[1], out.shape[2] // LANES
    pieces = [returned[:, :, part].reshape(span, LANES) for part in range(width)]
    right = split_value(jnp.concatenate(pieces, axis=1) if width > 1 else pieces[0])
    out[0] = dot3((span_high[...], span_low[...]), right)


def local(mesh_shape, source_field, coupling, spacing):
    gx_count, gz_count = mesh_shape["gx"], mesh_shape["gz"]
    own, span, part = source_field.shape
    assert own == 1
    group = gz_count // 4 if gz_count % 4 == 0 else 1
    planes = gz_count // group
    levels = group
    peers = gx_count * group
    stream = part * gx_count
    share = span // peers
    chunks = 8
    while share % (8 * chunks):
        chunks //= 2
    rows = share // chunks
    batch = 1
    back_groups = [(begin, 1) for begin in range(chunks)]
    blocks = part // LANES
    outer = stream // LANES
    slots = outer // 2
    tables = make_tables(span, stream, rows)
    f32 = jnp.float32
    wide = (slots, rows, 2 * LANES)
    parts = slots // min(max(1, 32 // rows), slots)
    dma = pltpu.SemaphoreType.DMA
    vmem = pl.BlockSpec(memory_space=pltpu.VMEM)
    smem = pl.BlockSpec(memory_space=pltpu.SMEM)
    cfg = (gx_count, group, planes, chunks, rows, levels, batch, back_groups)
    box = (chunks, peers, blocks, rows, LANES)
    tables = [jnp.asarray(table) for table in tables]
    returned = pl.pallas_call(
        functools.partial(kernel, cfg),
        out_shape=jax.ShapeDtypeStruct(box, f32),
        in_specs=[smem, smem] + [vmem] * 11,
        out_specs=pl.BlockSpec(memory_space=pl.ANY),
        scratch_shapes=[
            pltpu.VMEM((span, part), jnp.bfloat16),
            pltpu.VMEM((span, part), jnp.bfloat16),
            pltpu.VMEM((chunks, peers, blocks, rows, LANES), f32),
            pltpu.VMEM((chunks, levels, outer, rows, LANES), f32),
            pltpu.VMEM((slots, levels * rows, 2 * LANES), f32),
            pltpu.VMEM((chunks, slots, levels, rows, 2 * LANES), f32),
            pltpu.VMEM((chunks, levels) + wide, f32),
            pltpu.VMEM((chunks, levels) + wide, f32),
            pltpu.VMEM((chunks,) + wide, f32),
            pltpu.VMEM((chunks, levels) + wide, f32),
            pltpu.VMEM((chunks,) + wide, f32),
            pltpu.VMEM((chunks,) + wide, f32),
            pltpu.VMEM((chunks,) + wide, f32),
            pltpu.VMEM((chunks, levels, outer, rows, LANES), f32),
            dma((chunks,)), dma((chunks,)),
            *[dma((chunks, parts)) for _ in range(4)],
            dma((len(back_groups),)), dma((len(back_groups),)), dma((chunks,)),
        ],
        compiler_params=pltpu.CompilerParams(
            collective_id=0, has_side_effects=True, vmem_limit_bytes=56 * 1024 * 1024),
        cost_estimate=pl.CostEstimate(flops=8 * 10**9, bytes_accessed=8 * 2**20, transcendentals=0),
    )(coupling, spacing, source_field, *tables)
    width = min(2, blocks)
    return pl.pallas_call(
        last_product,
        grid=(blocks // width,),
        out_shape=jax.ShapeDtypeStruct(source_field.shape, f32),
        in_specs=[
            pl.BlockSpec((chunks, peers, width, rows, LANES), lambda index: (0, 0, index, 0, 0)),
            pl.BlockSpec((span, span), lambda index: (0, 0)),
            pl.BlockSpec((span, span), lambda index: (0, 0)),
        ],
        out_specs=pl.BlockSpec((1, span, width * LANES), lambda index: (0, 0, index)),
        compiler_params=pltpu.CompilerParams(vmem_limit_bytes=56 * 1024 * 1024),
        cost_estimate=pl.CostEstimate(flops=2 * 10**9, bytes_accessed=5 * 2**20, transcendentals=0),
    )(returned, tables[0], tables[1])


def solution(mesh):
    in_specs = (P("gz", None, "gx"), P(), P())
    out_specs = P("gz", None, "gx")
    return jax.shard_map(
        functools.partial(local, dict(mesh.shape)), mesh=mesh,
        in_specs=in_specs, out_specs=out_specs, check_vma=False)
```
